32 devices in a mesh: mp: 8 (over y, x, core), tokens: 4 (over z).
Axes of the slice: x: 2, y: 2, z: 4, core: 2. Of those that a mesh axis runs over, the one named last changes fastest.
Arguments:
- tokens_in: bfloat16 [128, 5120], P(('tokens', 'mp')), may hold values from -6 to 6
- grad_out: bfloat16 [128, 5120], P(('tokens', 'mp')), may hold values from -6 to 6
- pre_act: bfloat16 [128, 13824], P('tokens', 'mp'), may hold values from -6 to 6
- w_in: bfloat16 [5120, 13824], P(None, 'mp'), may hold values from -0.078125 to 0.078125
- w_out: bfloat16 [13824, 5120], P('mp'), may hold values from -0.0546875 to 0.0546875
Outputs:
- grad_in: bfloat16 [128, 5120], P(('tokens', 'mp'))
- grad_w_in: bfloat16 [5120, 13824], P('tokens', 'mp')
- grad_w_out: bfloat16 [13824, 5120], P('mp', 'tokens')
The draws below stay inside these ranges and needn't reach their ends.
All inputs are finite; a program needn't handle non-finite values.
Results may differ from the reference program's by a relative error of at most 0.023.
Values may be sent and summed in bfloat16 or wider, within the bound.
No kernel may reach another device: no remote copies, remote signals or barrier semaphores. Data moves between devices by JAX's collectives and lax.ppermute only.
A program may use at most 128 MiB of HBM per device.

```python
import math
import jax
import jax.numpy as jnp
from jax import lax

D = 5120
FF = 13824
TOKENS = 128
N_TOKENS = 4


def block_levels(rng, shape, pieces, low, largest):
    factor_of = 1.0
    for position, parts in pieces:
        draws = jax.random.uniform(jax.random.fold_in(jax.random.fold_in(rng, 6), position), (parts,), jnp.float32, low / len(pieces), largest / len(pieces))
        factor_of = factor_of * jnp.repeat(jnp.exp(draws), shape[position] // parts).reshape((-1,) + (1,) * (len(shape) - 1 - position))
    return factor_of


def gaussian(own_key, shape, scale, most, shards=(), kind=jnp.bfloat16):
    gain = block_levels(own_key, shape, shards, -0.22, 0.18) if shards else 1.0
    values = jax.random.normal(own_key, shape, jnp.float32) * scale * gain
    return jnp.minimum(jnp.maximum(values, -most), most).astype(kind)


def setup_inputs(seed: int = 0) -> dict:
    arg_keys = jax.random.split(jax.random.key(seed), 6)
    return {
        "tokens_in": gaussian(arg_keys[0], (TOKENS, D), 1.0, 6.0, ((0, 32),)),
        "grad_out": gaussian(arg_keys[1], (TOKENS, D), 1.0, 6.0, ((0, 32),)),
        "pre_act": gaussian(arg_keys[2], (TOKENS, FF), 1.0, 6.0, ((0, 4), (1, 8))),
        "w_in": gaussian(arg_keys[3], (D, FF), D ** -0.5, 0.078125, ((1, 8),)),
        "w_out": gaussian(arg_keys[4], (FF, D), FF ** -0.5, 0.0546875, ((0, 8),)),
    }


root_two_pi = math.sqrt(2.0 / math.pi)
cubic = 0.044715

def gelu_value(pre):
    inner = root_two_pi * (pre + cubic * pre * pre * pre)
    return 0.5 * pre * (1.0 + jnp.tanh(inner))

def gelu_slope(pre):
    tanh_val = jnp.tanh(root_two_pi * (pre + cubic * pre * pre * pre))
    return 0.5 * (1.0 + tanh_val) + 0.5 * pre * (1.0 - tanh_val * tanh_val) * root_two_pi * (1.0 + 3.0 * cubic * pre * pre)

def reference(tokens_in, grad_out, pre_act, w_in, w_out):
    pre = pre_act.astype(jnp.float32)
    activated = gelu_value(pre).astype(jnp.bfloat16)
    slope = gelu_slope(pre)
    grad_act = jnp.dot(grad_out, w_out.T, preferred_element_type=jnp.float32)
    grad_pre = (grad_act * slope).astype(jnp.bfloat16)
    grad_in = jnp.dot(grad_pre, w_in.T, preferred_element_type=jnp.float32).astype(jnp.bfloat16)
    scale_back = 1.0 / math.sqrt(TOKENS)
    groups = N_TOKENS
    rows_per = TOKENS // groups
    x_groups = tokens_in.reshape(groups, rows_per, tokens_in.shape[1])
    g_groups = grad_out.reshape(groups, rows_per, grad_out.shape[1])
    p_groups = grad_pre.reshape(groups, rows_per, grad_pre.shape[1])
    a_groups = activated.reshape(groups, rows_per, activated.shape[1])

    def add_group(carry, items):
        x_rows, g_rows, p_rows, a_rows = items
        part_in = (jnp.dot(x_rows.T, p_rows, preferred_element_type=jnp.float32) * scale_back).astype(jnp.bfloat16)
        part_out = (jnp.dot(a_rows.T, g_rows, preferred_element_type=jnp.float32) * scale_back).astype(jnp.bfloat16)
        return ((carry[0] + part_in.astype(jnp.float32), carry[1] + part_out.astype(jnp.float32)), None)
    start = (jnp.zeros(w_in.shape, jnp.float32), jnp.zeros(w_out.shape, jnp.float32))
    sums, unused = lax.scan(add_group, start, (x_groups, g_groups, p_groups, a_groups))
    return (grad_in, sums[0].astype(jnp.bfloat16), sums[1].astype(jnp.bfloat16))
```

```python
import math

import jax
import jax.numpy as jnp
from jax import lax
from jax.sharding import PartitionSpec as P

root_two_pi = math.sqrt(2.0 / math.pi)
cubic = 0.044715


def gelu_value(pre):
    inner = root_two_pi * (pre + cubic * pre * pre * pre)
    return 0.5 * pre * (1.0 + jnp.tanh(inner))


def gelu_slope(pre):
    tanh_val = jnp.tanh(root_two_pi * (pre + cubic * pre * pre * pre))
    return 0.5 * (1.0 + tanh_val) + 0.5 * pre * (1.0 - tanh_val * tanh_val) * root_two_pi * (
        1.0 + 3.0 * cubic * pre * pre
    )


def swap(x, axis):
    return lax.all_to_all(x, axis, 0, 0)


def gather(x, axis):
    return swap(jnp.broadcast_to(x, (lax.axis_size(axis),) + x.shape), axis)


def shards(tokens_in, grad_out, pre_act, w_in, w_out):
    n_mp, n_tok = lax.axis_size("mp"), lax.axis_size("tokens")
    rows, width = tokens_in.shape
    group, hidden = pre_act.shape
    part = width // n_tok
    total = group * n_tok
    scale_back = 1.0 / math.sqrt(total)

    rows_grad = gather(grad_out, "mp").reshape(group, width)
    pre_all = gather(pre_act, "tokens").reshape(total, hidden)

    both = jnp.stack([tokens_in, grad_out]).reshape(2, rows, n_tok, part)
    cols = swap(both.transpose(2, 0, 1, 3), "tokens")
    cols = gather(cols, "mp")
    cols_in, cols_grad = cols.transpose(2, 1, 0, 3, 4).reshape(2, total, part)

    pre = pre_act.astype(jnp.float32)
    grad_act = lax.dot_general(
        rows_grad, w_out, (((1,), (1,)), ((), ())), preferred_element_type=jnp.float32
    )
    grad_pre = (grad_act * gelu_slope(pre)).astype(jnp.bfloat16)
    grad_pre_all = gather(grad_pre, "tokens").reshape(total, hidden)

    part_grad_in = lax.dot_general(
        grad_pre, w_in, (((1,), (1,)), ((), ())), preferred_element_type=jnp.float32
    )
    blocks = swap(part_grad_in.astype(jnp.bfloat16).reshape(n_mp, rows, width), "mp")
    grad_in = jnp.sum(blocks.astype(jnp.float32), axis=0).astype(jnp.bfloat16)

    activated = gelu_value(pre_all.astype(jnp.float32)).astype(jnp.bfloat16)
    grad_w_out = (
        lax.dot_general(
            activated, cols_grad, (((0,), (0,)), ((), ())), preferred_element_type=jnp.float32
        )
        * scale_back
    ).astype(jnp.bfloat16)
    grad_w_in = (
        lax.dot_general(
            cols_in, grad_pre_all, (((0,), (0,)), ((), ())), preferred_element_type=jnp.float32
        )
        * scale_back
    ).astype(jnp.bfloat16)
    return (grad_in, grad_w_in, grad_w_out)


def solution(mesh):
    placed = (
        P(("tokens", "mp"), None),
        P(("tokens", "mp"), None),
        P("tokens", "mp"),
        P(None, "mp"),
        P("mp", None),
    )
    return jax.shard_map(
        shards,
        mesh=mesh,
        in_specs=placed,
        out_specs=(P(("tokens", "mp"), None), P("tokens", "mp"), P("mp", "tokens")),
        check_vma=False,
    )
```

```python
import functools
import math

import jax
import jax.numpy as jnp
from jax import lax
from jax.experimental import pallas as pl
from jax.experimental.pallas import tpu as pltpu
from jax.sharding import PartitionSpec as P

root_two_pi = math.sqrt(2.0 / math.pi)
cubic = 0.044715


def gelu_value(pre):
    inner = root_two_pi * (pre + cubic * pre * pre * pre)
    return 0.5 * pre * (1.0 + jnp.tanh(inner))


def gelu_slope(pre):
    tanh_val = jnp.tanh(root_two_pi * (pre + cubic * pre * pre * pre))
    return 0.5 * (1.0 + tanh_val) + 0.5 * pre * (1.0 - tanh_val * tanh_val) * root_two_pi * (
        1.0 + 3.0 * cubic * pre * pre
    )


def partner(i, k, n):
    return i ^ k if n & (n - 1) == 0 else (i + k) % n


def fetch(x, axis, k):
    n = lax.axis_size(axis)
    return lax.ppermute(x, axis, [(partner(i, k, n), i) for i in range(n)])


def swap(x, axis):
    return lax.all_to_all(x, axis, 0, 0)


def block_of(width, most):
    return max([b for b in range(128, most + 1, 128) if width % b == 0], default=width)


def grad_pre_body(steps, rows_ref, pre_ref, w_ref, out_ref, total_ref):
    step = pl.program_id(0)
    term = lax.dot_general(
        rows_ref[...], w_ref[...], (((1,), (1,)), ((), ())), preferred_element_type=jnp.float32
    )

    @pl.when(step == 0)
    def _():
        total_ref[...] = term

    @pl.when(step > 0)
    def _():
        total_ref[...] += term

    @pl.when(step == steps - 1)
    def _():
        slope = gelu_slope(pre_ref[...].astype(jnp.float32))
        out_ref[...] = (total_ref[...] * slope).astype(jnp.bfloat16)


def grad_pre_of(rows_grad, pre_act, w_out):
    group, width = rows_grad.shape
    hidden = w_out.shape[0]
    block = block_of(width, 1024)
    return pl.pallas_call(
        functools.partial(grad_pre_body, width // block),
        grid=(width // block,),
        in_specs=[
            pl.BlockSpec((group, block), lambda i: (0, i)),
            pl.BlockSpec((group, hidden), lambda i: (0, 0)),
            pl.BlockSpec((hidden, block), lambda i: (0, i)),
        ],
        out_specs=pl.BlockSpec((group, hidden), lambda i: (0, 0)),
        out_shape=jax.ShapeDtypeStruct((group, hidden), jnp.bfloat16),
        scratch_shapes=[pltpu.VMEM((group, hidden), jnp.float32)],
        compiler_params=pltpu.CompilerParams(vmem_limit_bytes=32 << 20),
        cost_estimate=pl.CostEstimate(
            flops=2 * group * width * hidden, bytes_accessed=2 * hidden * width, transcendentals=0
        ),
        name="grad_pre",
    )(rows_grad, pre_act, w_out)


def grad_in_body(grad_pre_ref, w_ref, out_ref):
    out_ref[...] = jnp.dot(
        grad_pre_ref[...], w_ref[...], preferred_element_type=jnp.float32
    ).astype(jnp.bfloat16)


def grad_in_part(grad_pre, w_in_t):
    group, hidden = grad_pre.shape
    width = w_in_t.shape[1]
    block = block_of(width, 1024)
    return pl.pallas_call(
        grad_in_body,
        grid=(width // block,),
        in_specs=[
            pl.BlockSpec((group, hidden), lambda i: (0, 0)),
            pl.BlockSpec((hidden, block), lambda i: (0, i)),
        ],
        out_specs=pl.BlockSpec((group, block), lambda i: (0, i)),
        out_shape=jax.ShapeDtypeStruct((group, width), jnp.bfloat16),
        compiler_params=pltpu.CompilerParams(vmem_limit_bytes=32 << 20),
        cost_estimate=pl.CostEstimate(
            flops=2 * group * width * hidden, bytes_accessed=2 * hidden * width, transcendentals=0
        ),
        name="grad_in_part",
    )(grad_pre, w_in_t)


def shards(tokens_in, grad_out, pre_act, w_in, w_out):
    n_mp, n_tok = lax.axis_size("mp"), lax.axis_size("tokens")
    t = lax.axis_index("tokens")
    rows, width = tokens_in.shape
    group, hidden = pre_act.shape
    part = width // n_tok
    total = group * n_tok
    scale_back = 1.0 / math.sqrt(total)

    both = jnp.concatenate([tokens_in, grad_out], axis=0)
    wide = max(hidden, part)
    own_pre = jnp.pad(pre_act, ((0, 0), (0, wide - hidden)))
    pre, cols = [], []
    for k in range(n_tok):
        taker = t ^ k if n_tok & (n_tok - 1) == 0 else (t - k) % n_tok
        piece = lax.dynamic_slice_in_dim(both, taker * part, part, axis=1)
        if k == 0:
            pre.append(pre_act)
            cols.append(piece)
        else:
            piece = jnp.pad(piece, ((0, 0), (0, wide - part)))
            packed = fetch(jnp.concatenate([own_pre, piece], axis=0), "tokens", k)
            pre.append(packed[:group, :hidden])
            cols.append(packed[group:, :part])
    pre_all = jnp.concatenate(pre, axis=0)
    cols = jnp.stack(cols).reshape(n_tok, 2, rows, part).transpose(1, 0, 2, 3)
    cols = swap(jnp.broadcast_to(cols, (n_mp,) + cols.shape), "mp")
    cols = cols.transpose(1, 2, 0, 3, 4)
    cols_in, cols_grad = cols.reshape(2, total, part)

    rows_grad = lax.all_gather(grad_out, "mp", axis=0, tiled=True)
    grad_pre = grad_pre_of(rows_grad, pre_act, w_out)
    grad_pre_all = jnp.concatenate(
        [grad_pre] + [fetch(grad_pre, "tokens", k) for k in range(1, n_tok)], axis=0
    )

    blocks = swap(grad_in_part(grad_pre, w_in.T).reshape(n_mp, rows, width), "mp")
    grad_in = jnp.sum(blocks.astype(jnp.float32), axis=0).astype(jnp.bfloat16)

    activated = gelu_value(pre_all.astype(jnp.float32)).astype(jnp.bfloat16)
    grad_w_out = (
        lax.dot_general(
            activated, cols_grad, (((0,), (0,)), ((), ())), preferred_element_type=jnp.float32
        )
        * scale_back
    ).astype(jnp.bfloat16)
    grad_w_in = (
        lax.dot_general(
            cols_in, grad_pre_all, (((0,), (0,)), ((), ())), preferred_element_type=jnp.float32
        )
        * scale_back
    ).astype(jnp.bfloat16)
    return (grad_in, grad_w_in, grad_w_out)


def solution(mesh):
    placed = (
        P(("tokens", "mp"), None),
        P(("tokens", "mp"), None),
        P("tokens", "mp"),
        P(None, "mp"),
        P("mp", None),
    )
    return jax.shard_map(
        shards,
        mesh=mesh,
        in_specs=placed,
        out_specs=(P(("tokens", "mp"), None), P("tokens", "mp"), P("mp", "tokens")),
        check_vma=False,
    )
```

```python
import functools
import math

import jax
import jax.numpy as jnp
from jax import lax
from jax.experimental import pallas as pl
from jax.experimental.pallas import tpu as pltpu
from jax.sharding import PartitionSpec as P

root_two_pi = math.sqrt(2.0 / math.pi)
cubic = 0.044715


def gelu_value(pre):
    inner = root_two_pi * (pre + cubic * pre * pre * pre)
    return 0.5 * pre * (1.0 + jnp.tanh(inner))


def gelu_slope(pre):
    tanh_val = jnp.tanh(root_two_pi * (pre + cubic * pre * pre * pre))
    return 0.5 * (1.0 + tanh_val) + 0.5 * pre * (1.0 - tanh_val * tanh_val) * root_two_pi * (
        1.0 + 3.0 * cubic * pre * pre
    )


def partner(i, k, n):
    return i ^ k if n & (n - 1) == 0 else (i + k) % n


def fetch(x, axis, k):
    n = lax.axis_size(axis)
    return lax.ppermute(x, axis, [(partner(i, k, n), i) for i in range(n)])


def swap(x, axis):
    return lax.all_to_all(x, axis, 0, 0)


def block_of(size, most, unit):
    return max([b for b in range(unit, most + 1, unit) if size % b == 0], default=size)


def grad_pre_body(steps, rows_ref, pre_ref, w_ref, out_ref, total_ref):
    step = pl.program_id(0)
    block = w_ref.shape[0]
    here = pl.ds(pl.multiple_of(step * block, block), block)
    total_ref[here, :] = lax.dot_general(
        w_ref[...], rows_ref[...], (((1,), (1,)), ((), ())), preferred_element_type=jnp.float32
    )

    @pl.when(step == steps - 1)
    def _():
        slope = gelu_slope(pre_ref[...].astype(jnp.float32))
        out_ref[...] = (total_ref[...].T * slope).astype(jnp.bfloat16)


def grad_pre_of(rows_grad, pre_act, w_out):
    group, width = rows_grad.shape
    hidden = w_out.shape[0]
    block = block_of(hidden, 192, 16)
    return pl.pallas_call(
        functools.partial(grad_pre_body, hidden // block),
        grid=(hidden // block,),
        in_specs=[
            pl.BlockSpec((group, width), lambda i: (0, 0)),
            pl.BlockSpec((group, hidden), lambda i: (0, 0)),
            pl.BlockSpec((block, width), lambda i: (i, 0)),
        ],
        out_specs=pl.BlockSpec((group, hidden), lambda i: (0, 0)),
        out_shape=jax.ShapeDtypeStruct((group, hidden), jnp.bfloat16),
        scratch_shapes=[pltpu.VMEM((hidden, group), jnp.float32)],
        compiler_params=pltpu.CompilerParams(vmem_limit_bytes=56 << 20),
        cost_estimate=pl.CostEstimate(
            flops=2 * group * width * hidden, bytes_accessed=2 * hidden * width, transcendentals=0
        ),
        name="grad_pre",
    )(rows_grad, pre_act, w_out)


def grad_in_body(grad_pre_ref, w_ref, out_ref):
    out_ref[...] = jnp.dot(
        grad_pre_ref[...], w_ref[...], preferred_element_type=jnp.float32
    ).astype(jnp.bfloat16)


def grad_in_part(grad_pre, w_in_t):
    group, hidden = grad_pre.shape
    width = w_in_t.shape[1]
    block = block_of(width, 512, 128)
    return pl.pallas_call(
        grad_in_body,
        grid=(width // block,),
        in_specs=[
            pl.BlockSpec((group, hidden), lambda i: (0, 0)),
            pl.BlockSpec((hidden, block), lambda i: (0, i)),
        ],
        out_specs=pl.BlockSpec((group, block), lambda i: (0, i)),
        out_shape=jax.ShapeDtypeStruct((group, width), jnp.bfloat16),
        compiler_params=pltpu.CompilerParams(vmem_limit_bytes=56 << 20),
        cost_estimate=pl.CostEstimate(
            flops=2 * group * width * hidden, bytes_accessed=2 * hidden * width, transcendentals=0
        ),
        name="grad_in_part",
    )(grad_pre, w_in_t)


def grad_w_body(places, scale_back, *refs):
    pre_refs, grad_pre_refs = refs[:places], refs[places : 2 * places]
    cols_ref, in_ref, out_ref, act_t, grad_pre_t = refs[2 * places :]
    group, hidden = grad_pre_refs[0].shape

    @pl.when(pl.program_id(0) == 0)
    def _():
        for k in range(places):
            here = slice(k * group, (k + 1) * group)
            pre = pre_refs[k][:group, :hidden].astype(jnp.float32)
            act_t[:, here] = gelu_value(pre).T.astype(jnp.bfloat16)
            grad_pre_t[:, here] = grad_pre_refs[k][...].astype(jnp.float32).T.astype(jnp.bfloat16)

    for left, right, to_ref in ((grad_pre_t, 0, in_ref), (act_t, 1, out_ref)):
        term = jnp.dot(left[...], cols_ref[right], preferred_element_type=jnp.float32)
        to_ref[...] = (term * scale_back).astype(jnp.bfloat16)


def grad_w_of(pre, grad_pre, cols, scale_back):
    places = len(pre)
    group, hidden = grad_pre[0].shape
    total, part = cols.shape[1:]
    block = block_of(part, 256, 128)
    whole = [pl.BlockSpec(x.shape, lambda i: (0, 0)) for x in (*pre, *grad_pre)]
    shape = jax.ShapeDtypeStruct((hidden, part), jnp.bfloat16)
    return pl.pallas_call(
        functools.partial(grad_w_body, places, scale_back),
        grid=(part // block,),
        in_specs=[*whole, pl.BlockSpec((2, total, block), lambda i: (0, 0, i))],
        out_specs=[pl.BlockSpec((hidden, block), lambda i: (0, i))] * 2,
        out_shape=[shape, shape],
        scratch_shapes=[pltpu.VMEM((hidden, total), jnp.bfloat16)] * 2,
        compiler_params=pltpu.CompilerParams(vmem_limit_bytes=56 << 20),
        cost_estimate=pl.CostEstimate(
            flops=4 * total * part * hidden,
            bytes_accessed=4 * hidden * part,
            transcendentals=total * hidden,
        ),
        name="grad_w",
    )(*pre, *grad_pre, cols)


def shards(tokens_in, grad_out, pre_act, w_in, w_out):
    n_mp, n_tok = lax.axis_size("mp"), lax.axis_size("tokens")
    t = lax.axis_index("tokens")
    rows, width = tokens_in.shape
    group, hidden = pre_act.shape
    part = width // n_tok
    total = group * n_tok
    scale_back = 1.0 / math.sqrt(total)

    both = jnp.concatenate([tokens_in, grad_out], axis=0)
    wide = max(hidden, part)
    own_pre = jnp.pad(pre_act, ((0, 0), (0, wide - hidden)))
    pre, cols = [], []
    for k in range(n_tok):
        taker = t ^ k if n_tok & (n_tok - 1) == 0 else (t - k) % n_tok
        piece = lax.dynamic_slice_in_dim(both, taker * part, part, axis=1)
        if k == 0:
            pre.append(pre_act)
            cols.append(piece)
        else:
            piece = jnp.pad(piece, ((0, 0), (0, wide - part)))
            packed = fetch(jnp.concatenate([own_pre, piece], axis=0), "tokens", k)
            pre.append(packed)
            cols.append(packed[group:, :part])
    cols = jnp.stack(cols).reshape(n_tok, 2, rows, part).transpose(1, 0, 2, 3)
    cols = swap(jnp.broadcast_to(cols, (n_mp,) + cols.shape), "mp")
    cols = cols.transpose(1, 2, 0, 3, 4).reshape(2, total, part)

    rows_grad = lax.all_gather(grad_out, "mp", axis=0, tiled=True)
    grad_pre = grad_pre_of(rows_grad, pre_act, w_out)
    grad_pre_all = [grad_pre] + [fetch(grad_pre, "tokens", k) for k in range(1, n_tok)]

    blocks = swap(grad_in_part(grad_pre, w_in.T).reshape(n_mp, rows, width), "mp")
    grad_in = jnp.sum(blocks.astype(jnp.float32), axis=0).astype(jnp.bfloat16)

    grad_w_in_t, grad_w_out = grad_w_of(pre, grad_pre_all, cols, scale_back)
    return (grad_in, grad_w_in_t.T, grad_w_out)


def solution(mesh):
    placed = (
        P(("tokens", "mp"), None),
        P(("tokens", "mp"), None),
        P("tokens", "mp"),
        P(None, "mp"),
        P("mp", None),
    )
    return jax.shard_map(
        shards,
        mesh=mesh,
        in_specs=placed,
        out_specs=(P(("tokens", "mp"), None), P("tokens", "mp"), P("mp", "tokens")),
        check_vma=False,
    )
```

```python
import functools
import math

import jax
import jax.numpy as jnp
from jax import lax
from jax.experimental import pallas as pl
from jax.experimental.pallas import tpu as pltpu
from jax.sharding import PartitionSpec as P

root_two_pi = math.sqrt(2.0 / math.pi)
cubic = 0.044715


def gelu_value(pre):
    inner = root_two_pi * (pre + cubic * pre * pre * pre)
    return 0.5 * pre * (1.0 + jnp.tanh(inner))


def gelu_slope(pre):
    tanh_val = jnp.tanh(root_two_pi * (pre + cubic * pre * pre * pre))
    return 0.5 * (1.0 + tanh_val) + 0.5 * pre * (1.0 - tanh_val * tanh_val) * root_two_pi * (
        1.0 + 3.0 * cubic * pre * pre
    )


def partner(i, k, n):
    return i ^ k if n & (n - 1) == 0 else (i + k) % n


def fetch(x, axis, k):
    n = lax.axis_size(axis)
    return lax.ppermute(x, axis, [(partner(i, k, n), i) for i in range(n)])


def swap(x, axis):
    return lax.all_to_all(x, axis, 0, 0)


def block_of(size, most, unit):
    return max([b for b in range(unit, most + 1, unit) if size % b == 0], default=size)


def stream(source, held, sems, block, depth, work):
    steps = source.shape[1] // block

    def copy(i):
        here = pl.ds(pl.multiple_of(i * block, block), block)
        return pltpu.make_async_copy(source.at[:, here], held.at[:, here], sems.at[i])

    depth = min(depth, steps)
    for i in range(depth):
        copy(i).start()

    def step(i, carry):
        copy(i).wait()

        @pl.when(i + depth < steps)
        def _():
            copy(i + depth).start()

        work(pl.ds(pl.multiple_of(i * block, block), block))
        return carry

    lax.fori_loop(0, steps, step, 0)


def grad_pre_body(block, depth, rows_ref, pre_ref, w_ref, out_ref, held, rows, total, sems):
    places, each, _ = rows_ref.shape
    for k in range(places):
        rows[k * each : (k + 1) * each, :] = rows_ref[k].astype(jnp.float32)
    total[...] = jnp.zeros_like(total)

    def work(here):
        total[...] += lax.dot_general(
            held[:, here],
            rows[:, here].astype(jnp.bfloat16),
            (((1,), (1,)), ((), ())),
            preferred_element_type=jnp.float32,
        )

    stream(w_ref, held, sems, block, depth, work)
    slope = gelu_slope(pre_ref[...].astype(jnp.float32))
    out_ref[...] = (total[...].T * slope).astype(jnp.bfloat16)


def grad_pre_of(rows_grad, pre_act, w_out):
    group, hidden = pre_act.shape
    width = w_out.shape[1]
    block = block_of(width, 512, 128)
    return pl.pallas_call(
        functools.partial(grad_pre_body, block, 4),
        in_specs=[
            pl.BlockSpec(memory_space=pltpu.VMEM),
            pl.BlockSpec(memory_space=pltpu.VMEM),
            pl.BlockSpec(memory_space=pltpu.HBM),
        ],
        out_specs=pl.BlockSpec(memory_space=pltpu.VMEM),
        out_shape=jax.ShapeDtypeStruct((group, hidden), jnp.bfloat16),
        scratch_shapes=[
            pltpu.VMEM((hidden, width), jnp.bfloat16),
            pltpu.VMEM((group, width), jnp.float32),
            pltpu.VMEM((hidden, group), jnp.float32),
            pltpu.SemaphoreType.DMA((width // block,)),
        ],
        compiler_params=pltpu.CompilerParams(vmem_limit_bytes=28 << 20),
        cost_estimate=pl.CostEstimate(
            flops=2 * group * width * hidden, bytes_accessed=2 * hidden * width, transcendentals=0
        ),
        name="grad_pre",
    )(rows_grad, pre_act, w_out)


def grad_in_body(block, depth, grad_pre_ref, w_ref, out_ref, held, sems):
    places, each, _ = out_ref.shape

    def work(here):
        term = jnp.dot(grad_pre_ref[...], held[:, here], preferred_element_type=jnp.float32)
        for k in range(places):
            out_ref[k, :, here] = term[k * each : (k + 1) * each].astype(jnp.bfloat16)

    stream(w_ref, held, sems, block, depth, work)


def grad_in_part(grad_pre, w_in_t, places):
    group, hidden = grad_pre.shape
    width = w_in_t.shape[1]
    block = block_of(width, 512, 128)
    return pl.pallas_call(
        functools.partial(grad_in_body, block, 4),
        in_specs=[
            pl.BlockSpec(memory_space=pltpu.VMEM),
            pl.BlockSpec(memory_space=pltpu.HBM),
        ],
        out_specs=pl.BlockSpec(memory_space=pltpu.VMEM),
        out_shape=jax.ShapeDtypeStruct((places, group // places, width), jnp.bfloat16),
        scratch_shapes=[
            pltpu.VMEM((hidden, width), jnp.bfloat16),
            pltpu.SemaphoreType.DMA((width // block,)),
        ],
        compiler_params=pltpu.CompilerParams(vmem_limit_bytes=28 << 20),
        cost_estimate=pl.CostEstimate(
            flops=2 * group * width * hidden, bytes_accessed=2 * hidden * width, transcendentals=0
        ),
        name="grad_in_part",
    )(grad_pre, w_in_t)


def turn(x_ref, to_ref, unit):
    hidden = x_ref.shape[1]
    for low in range(0, hidden, unit):
        size = min(unit, hidden - low)
        eye = lax.broadcasted_iota(jnp.int32, (size, size), 0) == lax.broadcasted_iota(
            jnp.int32, (size, size), 1
        )
        to_ref[low : low + size, :] = lax.dot_general(
            eye.astype(jnp.float32).astype(jnp.bfloat16),
            x_ref[:, low : low + size],
            (((1,), (1,)), ((), ())),
            preferred_element_type=jnp.float32,
        ).astype(jnp.bfloat16)


def grad_w_body(places, scale_back, block, *refs):
    pre_refs, grad_pre_refs = refs[:places], refs[places : 2 * places]
    cols_ref, in_ref, out_ref, flat, act_t, grad_pre_t, held_in, held_out, sems = refs[2 * places :]
    group, hidden = grad_pre_refs[0].shape
    part = cols_ref.shape[2]
    copies = []

    def product(left, right, held, to_ref):
        for low in range(0, part, block):
            here = slice(low, low + block)
            term = jnp.dot(left[...], cols_ref[right, :, here], preferred_element_type=jnp.float32)
            held[:, here] = (term * scale_back).astype(jnp.bfloat16)
            copies.append(
                pltpu.make_async_copy(held.at[:, here], to_ref.at[:, here], sems.at[len(copies)])
            )
            copies[-1].start()

    for k in range(places):
        pre = pre_refs[k][:group, :hidden].astype(jnp.float32)
        flat[k * group : (k + 1) * group, :] = gelu_value(pre).astype(jnp.bfloat16)
    turn(flat, act_t, 256)
    product(act_t, 1, held_out, out_ref)
    for k in range(places):
        flat[k * group : (k + 1) * group, :] = grad_pre_refs[k][...]
    turn(flat, grad_pre_t, 256)
    product(grad_pre_t, 0, held_in, in_ref)
    for copy in copies:
        copy.wait()


def grad_w_of(pre, grad_pre, cols, scale_back):
    places = len(pre)
    group, hidden = grad_pre[0].shape
    total, part = cols.shape[1:]
    block = block_of(part, 256, 128)
    shape = jax.ShapeDtypeStruct((hidden, part), jnp.bfloat16)
    return pl.pallas_call(
        functools.partial(grad_w_body, places, scale_back, block),
        in_specs=[pl.BlockSpec(memory_space=pltpu.VMEM)] * (2 * places + 1),
        out_specs=[pl.BlockSpec(memory_space=pltpu.HBM)] * 2,
        out_shape=[shape, shape],
        scratch_shapes=[
            pltpu.VMEM((total, hidden), jnp.bfloat16),
            pltpu.VMEM((hidden, total), jnp.bfloat16),
            pltpu.VMEM((hidden, total), jnp.bfloat16),
            pltpu.VMEM((hidden, part), jnp.bfloat16),
            pltpu.VMEM((hidden, part), jnp.bfloat16),
            pltpu.SemaphoreType.DMA((2 * (part // block),)),
        ],
        compiler_params=pltpu.CompilerParams(vmem_limit_bytes=28 << 20),
        cost_estimate=pl.CostEstimate(
            flops=4 * total * part * hidden,
            bytes_accessed=4 * hidden * part,
            transcendentals=total * hidden,
        ),
        name="grad_w",
    )(*pre, *grad_pre, cols)


def shards(tokens_in, grad_out, pre_act, w_in, w_out):
    n_mp, n_tok = lax.axis_size("mp"), lax.axis_size("tokens")
    t = lax.axis_index("tokens")
    rows, width = tokens_in.shape
    group, hidden = pre_act.shape
    part = width // n_tok
    total = group * n_tok
    scale_back = 1.0 / math.sqrt(total)

    both = jnp.concatenate([tokens_in, grad_out], axis=0)
    wide = max(hidden, part)
    own_pre = jnp.pad(pre_act, ((0, 0), (0, wide - hidden)))
    pre, cols = [], []
    for k in range(n_tok):
        taker = t ^ k if n_tok & (n_tok - 1) == 0 else (t - k) % n_tok
        piece = lax.dynamic_slice_in_dim(both, taker * part, part, axis=1)
        if k == 0:
            pre.append(pre_act)
            cols.append(piece)
        else:
            piece = jnp.pad(piece, ((0, 0), (0, wide - part)))
            packed = fetch(jnp.concatenate([own_pre, piece], axis=0), "tokens", k)
            pre.append(packed)
            cols.append(packed[group:, :part])
    rows_grad = swap(jnp.broadcast_to(grad_out, (n_mp,) + grad_out.shape), "mp")
    grad_pre = grad_pre_of(rows_grad, pre_act, w_out)
    grad_pre_all = [grad_pre] + [fetch(grad_pre, "tokens", k) for k in range(1, n_tok)]

    cols = jnp.stack(cols).reshape(n_tok, 2, rows, part).transpose(1, 0, 2, 3)
    cols, grad_pre = lax.optimization_barrier((cols, grad_pre))
    cols = swap(jnp.broadcast_to(cols, (n_mp,) + cols.shape), "mp")

    blocks = grad_in_part(grad_pre, w_in.T, n_mp)
    cols, blocks = lax.optimization_barrier((cols, blocks))
    blocks = swap(blocks, "mp")
    cols = cols.transpose(1, 2, 0, 3, 4).reshape(2, total, part)
    grad_w_in_t, grad_w_out = grad_w_of(pre, grad_pre_all, cols, scale_back)
    grad_in = jnp.sum(blocks.astype(jnp.float32), axis=0).astype(jnp.bfloat16)
    return (grad_in, grad_w_in_t.T, grad_w_out)


def solution(mesh):
    placed = (
        P(("tokens", "mp"), None),
        P(("tokens", "mp"), None),
        P("tokens", "mp"),
        P(None, "mp"),
        P("mp", None),
    )
    return jax.shard_map(
        shards,
        mesh=mesh,
        in_specs=placed,
        out_specs=(P(("tokens", "mp"), None), P("tokens", "mp"), P("mp", "tokens")),
        check_vma=False,
    )
```

```python
import functools
import math

import jax
import jax.numpy as jnp
from jax import lax
from jax.experimental import pallas as pl
from jax.experimental.pallas import tpu as pltpu
from jax.sharding import PartitionSpec as P

root_two_pi = math.sqrt(2.0 / math.pi)
cubic = 0.044715


def gelu_value(pre):
    inner = root_two_pi * (pre + cubic * pre * pre * pre)
    return 0.5 * pre * (1.0 + jnp.tanh(inner))


def gelu_slope(pre):
    tanh_val = jnp.tanh(root_two_pi * (pre + cubic * pre * pre * pre))
    return 0.5 * (1.0 + tanh_val) + 0.5 * pre * (1.0 - tanh_val * tanh_val) * root_two_pi * (
        1.0 + 3.0 * cubic * pre * pre
    )


def partner(i, k, n):
    return i ^ k if n & (n - 1) == 0 else (i + k) % n


def fetch(x, axis, k):
    n = lax.axis_size(axis)
    return lax.ppermute(x, axis, [(partner(i, k, n), i) for i in range(n)])


def swap(x, axis):
    return lax.all_to_all(x, axis, 0, 0)


def block_of(size, most, unit):
    return max([b for b in range(unit, most + 1, unit) if size % b == 0], default=size)


def stream(source, held, sems, block, depth, work):
    steps = source.shape[1] // block

    def copy(i):
        here = pl.ds(pl.multiple_of(i * block, block), block)
        return pltpu.make_async_copy(source.at[:, here], held.at[:, here], sems.at[i])

    depth = min(depth, steps)
    for i in range(depth):
        copy(i).start()

    def step(i, carry):
        copy(i).wait()

        @pl.when(i + depth < steps)
        def _():
            copy(i + depth).start()

        work(pl.ds(pl.multiple_of(i * block, block), block))
        return carry

    lax.fori_loop(0, steps, step, 0)


def grad_pre_body(block, depth, rows_ref, pre_ref, w_ref, out_ref, held, pre, rows, total, sems, sem):
    pre_copy = pltpu.make_async_copy(pre_ref, pre, sem)
    pre_copy.start()
    places, each, _ = rows_ref.shape
    for k in range(places):
        rows[k * each : (k + 1) * each, :] = rows_ref[k].astype(jnp.float32)
    total[...] = jnp.zeros_like(total)

    def work(here):
        total[...] += lax.dot_general(
            held[:, here],
            rows[:, here].astype(jnp.bfloat16),
            (((1,), (1,)), ((), ())),
            preferred_element_type=jnp.float32,
        )

    stream(w_ref, held, sems, block, depth, work)
    pre_copy.wait()
    slope = gelu_slope(pre[...].astype(jnp.float32))
    out_ref[...] = (total[...].T * slope).astype(jnp.bfloat16)


def grad_pre_of(rows_grad, pre_act, w_out):
    group, hidden = pre_act.shape
    width = w_out.shape[1]
    block = block_of(width, 512, 128)
    return pl.pallas_call(
        functools.partial(grad_pre_body, block, 4),
        in_specs=[
            pl.BlockSpec(memory_space=pltpu.VMEM),
            pl.BlockSpec(memory_space=pltpu.HBM),
            pl.BlockSpec(memory_space=pltpu.HBM),
        ],
        out_specs=pl.BlockSpec(memory_space=pltpu.VMEM),
        out_shape=jax.ShapeDtypeStruct((group, hidden), jnp.bfloat16),
        scratch_shapes=[
            pltpu.VMEM((hidden, width), jnp.bfloat16),
            pltpu.VMEM((group, hidden), jnp.bfloat16),
            pltpu.VMEM((group, width), jnp.float32),
            pltpu.VMEM((hidden, group), jnp.float32),
            pltpu.SemaphoreType.DMA((width // block,)),
            pltpu.SemaphoreType.DMA,
        ],
        compiler_params=pltpu.CompilerParams(vmem_limit_bytes=56 << 20),
        cost_estimate=pl.CostEstimate(
            flops=2 * group * width * hidden, bytes_accessed=2 * hidden * width, transcendentals=0
        ),
        name="grad_pre",
    )(rows_grad, pre_act, w_out)


def grad_in_body(block, depth, grad_pre_ref, w_ref, out_ref, held, sems):
    places, each, _ = out_ref.shape

    def work(here):
        term = jnp.dot(grad_pre_ref[...], held[:, here], preferred_element_type=jnp.float32)
        for k in range(places):
            out_ref[k, :, here] = term[k * each : (k + 1) * each].astype(jnp.bfloat16)

    stream(w_ref, held, sems, block, depth, work)


def grad_in_part(grad_pre, w_in_t, places):
    group, hidden = grad_pre.shape
    width = w_in_t.shape[1]
    block = block_of(width, 512, 128)
    return pl.pallas_call(
        functools.partial(grad_in_body, block, 4),
        in_specs=[
            pl.BlockSpec(memory_space=pltpu.VMEM),
            pl.BlockSpec(memory_space=pltpu.HBM),
        ],
        out_specs=pl.BlockSpec(memory_space=pltpu.VMEM),
        out_shape=jax.ShapeDtypeStruct((places, group // places, width), jnp.bfloat16),
        scratch_shapes=[
            pltpu.VMEM((hidden, width), jnp.bfloat16),
            pltpu.SemaphoreType.DMA((width // block,)),
        ],
        compiler_params=pltpu.CompilerParams(vmem_limit_bytes=56 << 20),
        cost_estimate=pl.CostEstimate(
            flops=2 * group * width * hidden, bytes_accessed=2 * hidden * width, transcendentals=0
        ),
        name="grad_in_part",
    )(grad_pre, w_in_t)


def turn(x_ref, to_ref, unit):
    hidden = x_ref.shape[1]
    for low in range(0, hidden, unit):
        size = min(unit, hidden - low)
        eye = lax.broadcasted_iota(jnp.int32, (size, size), 0) == lax.broadcasted_iota(
            jnp.int32, (size, size), 1
        )
        to_ref[low : low + size, :] = lax.dot_general(
            eye.astype(jnp.float32).astype(jnp.bfloat16),
            x_ref[:, low : low + size],
            (((1,), (1,)), ((), ())),
            preferred_element_type=jnp.float32,
        ).astype(jnp.bfloat16)


def grad_w_body(places, scale_back, block, *refs):
    pre_refs, grad_pre_refs = refs[:places], refs[places : 2 * places]
    cols_ref, in_ref, out_ref, flat, act_t, grad_pre_t, held_in, held_out, sems = refs[2 * places :]
    group, hidden = grad_pre_refs[0].shape
    part = cols_ref.shape[2]
    copies = []

    def product(left, right, held, to_ref):
        for low in range(0, part, block):
            here = slice(low, low + block)
            term = jnp.dot(left[...], cols_ref[right, :, here], preferred_element_type=jnp.float32)
            held[:, here] = (term * scale_back).astype(jnp.bfloat16)
            copies.append(
                pltpu.make_async_copy(held.at[:, here], to_ref.at[:, here], sems.at[len(copies)])
            )
            copies[-1].start()

    for k in range(places):
        pre = pre_refs[k][:group, :hidden].astype(jnp.float32)
        flat[k * group : (k + 1) * group, :] = gelu_value(pre).astype(jnp.bfloat16)
    turn(flat, act_t, 256)
    product(act_t, 1, held_out, out_ref)
    for k in range(places):
        flat[k * group : (k + 1) * group, :] = grad_pre_refs[k][...]
    turn(flat, grad_pre_t, 256)
    product(grad_pre_t, 0, held_in, in_ref)
    for copy in copies:
        copy.wait()


def grad_w_of(pre, grad_pre, cols, scale_back):
    places = len(pre)
    group, hidden = grad_pre[0].shape
    total, part = cols.shape[1:]
    block = block_of(part, 256, 128)
    shape = jax.ShapeDtypeStruct((hidden, part), jnp.bfloat16)
    return pl.pallas_call(
        functools.partial(grad_w_body, places, scale_back, block),
        in_specs=[pl.BlockSpec(memory_space=pltpu.VMEM)] * (2 * places + 1),
        out_specs=[pl.BlockSpec(memory_space=pltpu.HBM)] * 2,
        out_shape=[shape, shape],
        scratch_shapes=[
            pltpu.VMEM((total, hidden), jnp.bfloat16),
            pltpu.VMEM((hidden, total), jnp.bfloat16),
            pltpu.VMEM((hidden, total), jnp.bfloat16),
            pltpu.VMEM((hidden, part), jnp.bfloat16),
            pltpu.VMEM((hidden, part), jnp.bfloat16),
            pltpu.SemaphoreType.DMA((2 * (part // block),)),
        ],
        compiler_params=pltpu.CompilerParams(vmem_limit_bytes=20 << 20),
        cost_estimate=pl.CostEstimate(
            flops=80 * total * part * hidden,
            bytes_accessed=40 * hidden * part,
            transcendentals=total * hidden,
        ),
        name="grad_w",
    )(*pre, *grad_pre, cols)


def shards(tokens_in, grad_out, pre_act, w_in, w_out):
    n_mp, n_tok = lax.axis_size("mp"), lax.axis_size("tokens")
    t = lax.axis_index("tokens")
    rows, width = tokens_in.shape
    group, hidden = pre_act.shape
    part = width // n_tok
    total = group * n_tok
    scale_back = 1.0 / math.sqrt(total)

    rows_grad = jnp.broadcast_to(grad_out, (n_mp,) + grad_out.shape)
    rows_grad, tokens_in, grad_out = lax.optimization_barrier((rows_grad, tokens_in, grad_out))
    rows_grad = swap(rows_grad, "mp")

    both = jnp.concatenate([tokens_in, grad_out], axis=0)
    wide = max(hidden, part)
    own_pre = jnp.pad(pre_act, ((0, 0), (0, wide - hidden)))
    packed = []
    for k in range(n_tok):
        taker = t ^ k if n_tok & (n_tok - 1) == 0 else (t - k) % n_tok
        piece = lax.dynamic_slice_in_dim(both, taker * part, part, axis=1)
        if k == 0:
            own_piece = piece
        else:
            piece = jnp.pad(piece, ((0, 0), (0, wide - part)))
            packed.append(fetch(jnp.concatenate([own_pre, piece], axis=0), "tokens", k))

    grad_pre = grad_pre_of(rows_grad, pre_act, w_out)
    grad_pre_all = [grad_pre] + [fetch(grad_pre, "tokens", k) for k in range(1, n_tok)]

    packed, grad_pre = lax.optimization_barrier((packed, grad_pre))
    pre = [pre_act] + packed
    cols = jnp.stack([own_piece] + [x[group:, :part] for x in packed])
    cols = cols.reshape(n_tok, 2, rows, part).transpose(1, 0, 2, 3)
    cols = swap(jnp.broadcast_to(cols, (n_mp,) + cols.shape), "mp")

    blocks = grad_in_part(grad_pre, w_in.T, n_mp)
    cols, blocks = lax.optimization_barrier((cols, blocks))
    blocks = swap(blocks, "mp")
    cols = cols.transpose(1, 2, 0, 3, 4).reshape(2, total, part)
    grad_w_in_t, grad_w_out = grad_w_of(pre, grad_pre_all, cols, scale_back)
    grad_in = jnp.sum(blocks.astype(jnp.float32), axis=0).astype(jnp.bfloat16)
    return (grad_in, grad_w_in_t.T, grad_w_out)


def solution(mesh):
    placed = (
        P(("tokens", "mp"), None),
        P(("tokens", "mp"), None),
        P("tokens", "mp"),
        P(None, "mp"),
        P("mp", None),
    )
    return jax.shard_map(
        shards,
        mesh=mesh,
        in_specs=placed,
        out_specs=(P(("tokens", "mp"), None), P("tokens", "mp"), P("mp", "tokens")),
        check_vma=False,
    )
```

```python
import functools
import math

import jax
import jax.numpy as jnp
from jax import lax
from jax.experimental import pallas as pl
from jax.experimental.pallas import tpu as pltpu
from jax.sharding import PartitionSpec as P

root_two_pi = math.sqrt(2.0 / math.pi)
cubic = 0.044715


def gelu_value(pre):
    inner = root_two_pi * (pre + cubic * pre * pre * pre)
    return 0.5 * pre * (1.0 + jnp.tanh(inner))


def gelu_slope(pre):
    tanh_val = jnp.tanh(root_two_pi * (pre + cubic * pre * pre * pre))
    return 0.5 * (1.0 + tanh_val) + 0.5 * pre * (1.0 - tanh_val * tanh_val) * root_two_pi * (
        1.0 + 3.0 * cubic * pre * pre
    )


def partner(i, k, n):
    return i ^ k if n & (n - 1) == 0 else (i + k) % n


def fetch(x, axis, k):
    n = lax.axis_size(axis)
    return lax.ppermute(x, axis, [(partner(i, k, n), i) for i in range(n)])


def swap(x, axis):
    return lax.all_to_all(x, axis, 0, 0)


def block_of(size, most, unit):
    return max([b for b in range(unit, most + 1, unit) if size % b == 0], default=size)


def stream(source, held, sems, axis, block, depth, work):
    steps = source.shape[axis] // block

    def place(i):
        here = pl.ds(pl.multiple_of(i * block, block), block)
        return (here, slice(None)) if axis == 0 else (slice(None), here)

    def copy(i):
        return pltpu.make_async_copy(source.at[place(i)], held.at[place(i)], sems.at[i])

    depth = min(depth, steps)
    for i in range(depth):
        copy(i).start()

    def step(i, carry):
        copy(i).wait()

        @pl.when(i + depth < steps)
        def _():
            copy(i + depth).start()

        work(pl.ds(pl.multiple_of(i * block, block), block))
        return carry

    lax.fori_loop(0, steps, step, 0)


def grad_pre_body(block, depth, rows_ref, pre_ref, w_ref, out_ref, held, pre, rows, total, sems, sem):
    pre_copy = pltpu.make_async_copy(pre_ref, pre, sem)
    pre_copy.start()
    places = rows_ref.shape[0]
    rows[...] = jnp.concatenate(
        [rows_ref[k].astype(jnp.float32) for k in range(places)], axis=0
    ).astype(jnp.bfloat16)

    def work(here):
        total[here, :] = lax.dot_general(
            held[here, :], rows[...], (((1,), (1,)), ((), ())), preferred_element_type=jnp.float32
        )

    stream(w_ref, held, sems, 0, block, depth, work)
    pre_copy.wait()
    slope = gelu_slope(pre[...].astype(jnp.float32))
    out_ref[...] = (total[...].T * slope).astype(jnp.bfloat16)


def grad_pre_of(rows_grad, pre_act, w_out):
    group, hidden = pre_act.shape
    width = w_out.shape[1]
    block = block_of(hidden, 96, 16)
    return pl.pallas_call(
        functools.partial(grad_pre_body, block, 4),
        in_specs=[
            pl.BlockSpec(memory_space=pltpu.VMEM),
            pl.BlockSpec(memory_space=pltpu.HBM),
            pl.BlockSpec(memory_space=pltpu.HBM),
        ],
        out_specs=pl.BlockSpec(memory_space=pltpu.VMEM),
        out_shape=jax.ShapeDtypeStruct((group, hidden), jnp.bfloat16),
        scratch_shapes=[
            pltpu.VMEM((hidden, width), jnp.bfloat16),
            pltpu.VMEM((group, hidden), jnp.bfloat16),
            pltpu.VMEM((group, width), jnp.bfloat16),
            pltpu.VMEM((hidden, group), jnp.float32),
            pltpu.SemaphoreType.DMA((hidden // block,)),
            pltpu.SemaphoreType.DMA,
        ],
        compiler_params=pltpu.CompilerParams(vmem_limit_bytes=48 << 20),
        cost_estimate=pl.CostEstimate(
            flops=2 * group * width * hidden, bytes_accessed=2 * hidden * width, transcendentals=0
        ),
        name="grad_pre",
    )(rows_grad, pre_act, w_out)


def grad_in_body(block, depth, grad_pre_ref, w_ref, out_ref, held, sems):
    places, each, _ = out_ref.shape

    def work(here):
        term = jnp.dot(grad_pre_ref[...], held[:, here], preferred_element_type=jnp.float32)
        for k in range(places):
            out_ref[k, :, here] = term[k * each : (k + 1) * each].astype(jnp.bfloat16)

    stream(w_ref, held, sems, 1, block, depth, work)


def grad_in_part(grad_pre, w_in_t, places):
    group, hidden = grad_pre.shape
    width = w_in_t.shape[1]
    block = block_of(width, 256, 128)
    return pl.pallas_call(
        functools.partial(grad_in_body, block, 4),
        in_specs=[
            pl.BlockSpec(memory_space=pltpu.VMEM),
            pl.BlockSpec(memory_space=pltpu.HBM),
        ],
        out_specs=pl.BlockSpec(memory_space=pltpu.VMEM),
        out_shape=jax.ShapeDtypeStruct((places, group // places, width), jnp.bfloat16),
        scratch_shapes=[
            pltpu.VMEM((hidden, width), jnp.bfloat16),
            pltpu.SemaphoreType.DMA((width // block,)),
        ],
        compiler_params=pltpu.CompilerParams(vmem_limit_bytes=48 << 20),
        cost_estimate=pl.CostEstimate(
            flops=2 * group * width * hidden, bytes_accessed=2 * hidden * width, transcendentals=0
        ),
        name="grad_in_part",
    )(grad_pre, w_in_t)


def turn(x_ref, to_ref, unit):
    hidden = x_ref.shape[1]
    for low in range(0, hidden, unit):
        size = min(unit, hidden - low)
        eye = lax.broadcasted_iota(jnp.int32, (size, size), 0) == lax.broadcasted_iota(
            jnp.int32, (size, size), 1
        )
        to_ref[low : low + size, :] = lax.dot_general(
            eye.astype(jnp.float32).astype(jnp.bfloat16),
            x_ref[:, low : low + size],
            (((1,), (1,)), ((), ())),
            preferred_element_type=jnp.float32,
        ).astype(jnp.bfloat16)


def grad_w_body(places, scale_back, block, *refs):
    pre_refs, grad_pre_refs = refs[:places], refs[places : 2 * places]
    cols_ref, in_ref, out_ref, flat, act_t, grad_pre_t, held_in, held_out, sems = refs[2 * places :]
    group, hidden = grad_pre_refs[0].shape
    part = cols_ref.shape[2]
    copies = []

    def product(left, right, held, to_ref):
        for low in range(0, part, block):
            here = slice(low, low + block)
            term = jnp.dot(left[...], cols_ref[right, :, here], preferred_element_type=jnp.float32)
            held[:, here] = (term * scale_back).astype(jnp.bfloat16)
            copies.append(
                pltpu.make_async_copy(held.at[:, here], to_ref.at[:, here], sems.at[len(copies)])
            )
            copies[-1].start()

    for k in range(places):
        pre = pre_refs[k][:group, :hidden].astype(jnp.float32)
        flat[k * group : (k + 1) * group, :] = gelu_value(pre).astype(jnp.bfloat16)
    turn(flat, act_t, 256)
    product(act_t, 1, held_out, out_ref)
    for k in range(places):
        flat[k * group : (k + 1) * group, :] = grad_pre_refs[k][...]
    turn(flat, grad_pre_t, 256)
    product(grad_pre_t, 0, held_in, in_ref)
    for copy in copies:
        copy.wait()


def grad_w_of(pre, grad_pre, cols, scale_back):
    places = len(pre)
    group, hidden = grad_pre[0].shape
    total, part = cols.shape[1:]
    block = block_of(part, 256, 128)
    shape = jax.ShapeDtypeStruct((hidden, part), jnp.bfloat16)
    return pl.pallas_call(
        functools.partial(grad_w_body, places, scale_back, block),
        in_specs=[pl.BlockSpec(memory_space=pltpu.VMEM)] * (2 * places + 1),
        out_specs=[pl.BlockSpec(memory_space=pltpu.HBM)] * 2,
        out_shape=[shape, shape],
        scratch_shapes=[
            pltpu.VMEM((total, hidden), jnp.bfloat16),
            pltpu.VMEM((hidden, total), jnp.bfloat16),
            pltpu.VMEM((hidden, total), jnp.bfloat16),
            pltpu.VMEM((hidden, part), jnp.bfloat16),
            pltpu.VMEM((hidden, part), jnp.bfloat16),
            pltpu.SemaphoreType.DMA((2 * (part // block),)),
        ],
        compiler_params=pltpu.CompilerParams(vmem_limit_bytes=20 << 20),
        cost_estimate=pl.CostEstimate(
            flops=80 * total * part * hidden,
            bytes_accessed=40 * hidden * part,
            transcendentals=total * hidden,
        ),
        name="grad_w",
    )(*pre, *grad_pre, cols)


def shards(tokens_in, grad_out, pre_act, w_in, w_out):
    n_mp, n_tok = lax.axis_size("mp"), lax.axis_size("tokens")
    t = lax.axis_index("tokens")
    rows, width = tokens_in.shape
    group, hidden = pre_act.shape
    part = width // n_tok
    total = group * n_tok
    scale_back = 1.0 / math.sqrt(total)

    rows_grad = jnp.broadcast_to(grad_out, (n_mp,) + grad_out.shape)
    rows_grad, tokens_in, grad_out = lax.optimization_barrier((rows_grad, tokens_in, grad_out))
    rows_grad = swap(rows_grad, "mp")

    both = jnp.concatenate([tokens_in, grad_out], axis=0)
    wide = max(hidden, part)
    own_pre = jnp.pad(pre_act, ((0, 0), (0, wide - hidden)))
    packed = []
    for k in range(n_tok):
        taker = t ^ k if n_tok & (n_tok - 1) == 0 else (t - k) % n_tok
        piece = lax.dynamic_slice_in_dim(both, taker * part, part, axis=1)
        if k == 0:
            own_piece = piece
        else:
            piece = jnp.pad(piece, ((0, 0), (0, wide - part)))
            packed.append(fetch(jnp.concatenate([own_pre, piece], axis=0), "tokens", k))

    grad_pre = grad_pre_of(rows_grad, pre_act, w_out)
    grad_pre_all = [grad_pre] + [fetch(grad_pre, "tokens", k) for k in range(1, n_tok)]

    packed, grad_pre = lax.optimization_barrier((packed, grad_pre))
    pre = [pre_act] + packed
    cols = jnp.stack([own_piece] + [x[group:, :part] for x in packed])
    cols = cols.reshape(n_tok, 2, rows, part).transpose(1, 0, 2, 3)
    cols = swap(jnp.broadcast_to(cols, (n_mp,) + cols.shape), "mp")

    blocks = grad_in_part(grad_pre, w_in.T, n_mp)
    cols, blocks = lax.optimization_barrier((cols, blocks))
    blocks = swap(blocks, "mp")
    cols = cols.transpose(1, 2, 0, 3, 4).reshape(2, total, part)
    grad_w_in_t, grad_w_out = grad_w_of(pre, grad_pre_all, cols, scale_back)
    grad_in = jnp.sum(blocks.astype(jnp.float32), axis=0).astype(jnp.bfloat16)
    return (grad_in, grad_w_in_t.T, grad_w_out)


def solution(mesh):
    placed = (
        P(("tokens", "mp"), None),
        P(("tokens", "mp"), None),
        P("tokens", "mp"),
        P(None, "mp"),
        P("mp", None),
    )
    return jax.shard_map(
        shards,
        mesh=mesh,
        in_specs=placed,
        out_specs=(P(("tokens", "mp"), None), P("tokens", "mp"), P("mp", "tokens")),
        check_vma=False,
    )
```

```python
import functools
import math

import jax
import jax.numpy as jnp
from jax import lax
from jax.experimental import pallas as pl
from jax.experimental.pallas import tpu as pltpu
from jax.sharding import PartitionSpec as P

root_two_pi = math.sqrt(2.0 / math.pi)
cubic = 0.044715


def gelu_value(pre):
    inner = root_two_pi * (pre + cubic * pre * pre * pre)
    return 0.5 * pre * (1.0 + jnp.tanh(inner))


def gelu_slope(pre):
    tanh_val = jnp.tanh(root_two_pi * (pre + cubic * pre * pre * pre))
    return 0.5 * (1.0 + tanh_val) + 0.5 * pre * (1.0 - tanh_val * tanh_val) * root_two_pi * (
        1.0 + 3.0 * cubic * pre * pre
    )


def partner(i, k, n):
    return i ^ k if n & (n - 1) == 0 else (i + k) % n


def fetch(x, axis, k):
    n = lax.axis_size(axis)
    return lax.ppermute(x, axis, [(partner(i, k, n), i) for i in range(n)])


def swap(x, axis):
    return lax.all_to_all(x, axis, 0, 0)


def block_of(size, most, unit):
    return max([b for b in range(unit, most + 1, unit) if size % b == 0], default=size)


def pack_body(takers, tokens_ref, grad_ref, pre_ref, *refs):
    *packed, own, pre_copy, slabs = refs
    places, rows, part = slabs.shape
    hidden = pre_ref.shape[1]
    both = jnp.concatenate(
        [tokens_ref[...].astype(jnp.float32), grad_ref[...].astype(jnp.float32)], axis=0
    )
    for p in range(places):
        slabs[p] = both[:, p * part : (p + 1) * part]
    t = lax.axis_index("tokens")
    own[...] = slabs[t].astype(jnp.bfloat16)
    pre_copy[...] = pre_ref[...]
    pre = pre_ref[...].astype(jnp.float32)
    for k, ref in enumerate(packed):
        piece = slabs[takers(t, k + 1)]
        wide = ref.shape[1]
        ref[...] = jnp.concatenate(
            [
                jnp.pad(pre, ((0, 0), (0, wide - hidden))),
                jnp.pad(piece, ((0, 0), (0, wide - part))),
            ],
            axis=0,
        ).astype(jnp.bfloat16)


def pack(tokens_in, grad_out, pre_act, n_tok):
    def takers(t, k):
        return t ^ k if n_tok & (n_tok - 1) == 0 else lax.rem(t - k + n_tok, n_tok)

    rows, width = tokens_in.shape
    group, hidden = pre_act.shape
    part = width // n_tok
    shapes = [(group + 2 * rows, max(hidden, part))] * (n_tok - 1) + [(2 * rows, part), pre_act.shape]
    return pl.pallas_call(
        functools.partial(pack_body, takers),
        in_specs=[pl.BlockSpec(memory_space=pltpu.VMEM)] * 3,
        out_specs=[pl.BlockSpec(memory_space=pltpu.VMEM)] * (n_tok + 1),
        out_shape=[jax.ShapeDtypeStruct(shape, jnp.bfloat16) for shape in shapes],
        scratch_shapes=[pltpu.VMEM((n_tok, 2 * rows, part), jnp.float32)],
        compiler_params=pltpu.CompilerParams(vmem_limit_bytes=8 << 20),
        cost_estimate=pl.CostEstimate(flops=10**10, bytes_accessed=36 * 10**6, transcendentals=0),
        name="pack",
    )(tokens_in, grad_out, pre_act)


def grad_pre_body(block, rows_ref, pre_ref, w_ref, out_ref, rows, total):
    places = rows_ref.shape[0]
    hidden = w_ref.shape[0]
    rows[...] = jnp.concatenate(
        [rows_ref[k].astype(jnp.float32) for k in range(places)], axis=0
    ).astype(jnp.bfloat16)
    for low in range(0, hidden, block):
        here = slice(low, low + block)
        total[here, :] = lax.dot_general(
            w_ref[here, :], rows[...], (((1,), (1,)), ((), ())), preferred_element_type=jnp.float32
        )
    slope = gelu_slope(pre_ref[...].astype(jnp.float32))
    out_ref[...] = (total[...].T * slope).astype(jnp.bfloat16)


def grad_pre_of(rows_grad, pre_act, w_out):
    group, hidden = pre_act.shape
    width = w_out.shape[1]
    block = block_of(hidden, 432, 16)
    return pl.pallas_call(
        functools.partial(grad_pre_body, block),
        in_specs=[pl.BlockSpec(memory_space=pltpu.VMEM)] * 3,
        out_specs=pl.BlockSpec(memory_space=pltpu.VMEM),
        out_shape=jax.ShapeDtypeStruct((group, hidden), jnp.bfloat16),
        scratch_shapes=[
            pltpu.VMEM((group, width), jnp.bfloat16),
            pltpu.VMEM((hidden, group), jnp.float32),
        ],
        compiler_params=pltpu.CompilerParams(vmem_limit_bytes=8 << 20),
        cost_estimate=pl.CostEstimate(
            flops=2 * group * width * hidden, bytes_accessed=2 * hidden * width, transcendentals=0
        ),
        name="grad_pre",
    )(rows_grad, pre_act, w_out)


def grad_in_body(block, grad_pre_ref, w_ref, out_ref):
    places, each, width = out_ref.shape
    for low in range(0, width, block):
        here = slice(low, low + block)
        term = jnp.dot(grad_pre_ref[...], w_ref[:, here], preferred_element_type=jnp.float32)
        for k in range(places):
            out_ref[k, :, here] = term[k * each : (k + 1) * each].astype(jnp.bfloat16)


def grad_in_part(grad_pre, w_in_t, places):
    group, hidden = grad_pre.shape
    width = w_in_t.shape[1]
    block = block_of(width, 1024, 128)
    return pl.pallas_call(
        functools.partial(grad_in_body, block),
        in_specs=[pl.BlockSpec(memory_space=pltpu.VMEM)] * 2,
        out_specs=pl.BlockSpec(memory_space=pltpu.VMEM),
        out_shape=jax.ShapeDtypeStruct((places, group // places, width), jnp.bfloat16),
        compiler_params=pltpu.CompilerParams(vmem_limit_bytes=8 << 20),
        cost_estimate=pl.CostEstimate(
            flops=2 * group * width * hidden, bytes_accessed=2 * hidden * width, transcendentals=0
        ),
        name="grad_in_part",
    )(grad_pre, w_in_t)


def turn(x_ref, to_ref, unit):
    hidden = x_ref.shape[1]
    for low in range(0, hidden, unit):
        size = min(unit, hidden - low)
        eye = lax.broadcasted_iota(jnp.int32, (size, size), 0) == lax.broadcasted_iota(
            jnp.int32, (size, size), 1
        )
        to_ref[low : low + size, :] = lax.dot_general(
            eye.astype(jnp.float32).astype(jnp.bfloat16),
            x_ref[:, low : low + size],
            (((1,), (1,)), ((), ())),
            preferred_element_type=jnp.float32,
        ).astype(jnp.bfloat16)


def grad_w_body(places, scale_back, block, *refs):
    pre_refs, grad_pre_refs = refs[:places], refs[places : 2 * places]
    cols_ref, in_ref, out_ref, flat, act_t, grad_pre_t, held_in, held_out, sems = refs[2 * places :]
    group, hidden = grad_pre_refs[0].shape
    part = cols_ref.shape[2]
    copies = []

    def product(left, right, held, to_ref):
        for low in range(0, part, block):
            here = slice(low, low + block)
            term = jnp.dot(left[...], cols_ref[right, :, here], preferred_element_type=jnp.float32)
            held[:, here] = (term * scale_back).astype(jnp.bfloat16)
            copies.append(
                pltpu.make_async_copy(held.at[:, here], to_ref.at[:, here], sems.at[len(copies)])
            )
            copies[-1].start()

    for k in range(places):
        pre = pre_refs[k][:group, :hidden].astype(jnp.float32)
        flat[k * group : (k + 1) * group, :] = gelu_value(pre).astype(jnp.bfloat16)
    turn(flat, act_t, 256)
    product(act_t, 1, held_out, out_ref)
    for k in range(places):
        flat[k * group : (k + 1) * group, :] = grad_pre_refs[k][...]
    turn(flat, grad_pre_t, 256)
    product(grad_pre_t, 0, held_in, in_ref)
    for copy in copies:
        copy.wait()


def grad_w_of(pre, grad_pre, cols, scale_back):
    places = len(pre)
    group, hidden = grad_pre[0].shape
    total, part = cols.shape[1:]
    block = block_of(part, 256, 128)
    shape = jax.ShapeDtypeStruct((hidden, part), jnp.bfloat16)
    return pl.pallas_call(
        functools.partial(grad_w_body, places, scale_back, block),
        in_specs=[pl.BlockSpec(memory_space=pltpu.VMEM)] * (2 * places + 1),
        out_specs=[pl.BlockSpec(memory_space=pltpu.HBM)] * 2,
        out_shape=[shape, shape],
        scratch_shapes=[
            pltpu.VMEM((total, hidden), jnp.bfloat16),
            pltpu.VMEM((hidden, total), jnp.bfloat16),
            pltpu.VMEM((hidden, total), jnp.bfloat16),
            pltpu.VMEM((hidden, part), jnp.bfloat16),
            pltpu.VMEM((hidden, part), jnp.bfloat16),
            pltpu.SemaphoreType.DMA((2 * (part // block),)),
        ],
        compiler_params=pltpu.CompilerParams(vmem_limit_bytes=20 << 20),
        cost_estimate=pl.CostEstimate(
            flops=80 * total * part * hidden,
            bytes_accessed=40 * hidden * part,
            transcendentals=total * hidden,
        ),
        name="grad_w",
    )(*pre, *grad_pre, cols)


def shards(tokens_in, grad_out, pre_act, w_in, w_out):
    n_mp, n_tok = lax.axis_size("mp"), lax.axis_size("tokens")
    rows, width = tokens_in.shape
    group, hidden = pre_act.shape
    part = width // n_tok
    total = group * n_tok
    scale_back = 1.0 / math.sqrt(total)

    rows_grad = jnp.broadcast_to(grad_out, (n_mp,) + grad_out.shape)
    rows_grad, tokens_in, grad_out = lax.optimization_barrier((rows_grad, tokens_in, grad_out))
    rows_grad = swap(rows_grad, "mp")

    *packed, own_piece, pre_act = pack(tokens_in, grad_out, pre_act, n_tok)
    packed = [fetch(x, "tokens", k + 1) for k, x in enumerate(packed)]

    grad_pre = grad_pre_of(rows_grad, pre_act, w_out)
    grad_pre_all = [grad_pre] + [fetch(grad_pre, "tokens", k) for k in range(1, n_tok)]

    packed, grad_pre = lax.optimization_barrier((packed, grad_pre))
    pre = [pre_act] + packed
    cols = jnp.stack([own_piece] + [x[group:, :part] for x in packed])
    cols = cols.reshape(n_tok, 2, rows, part).transpose(1, 0, 2, 3)
    cols = swap(jnp.broadcast_to(cols, (n_mp,) + cols.shape), "mp")

    blocks = grad_in_part(grad_pre, w_in.T, n_mp)
    cols, blocks = lax.optimization_barrier((cols, blocks))
    blocks = swap(blocks, "mp")
    cols = cols.transpose(1, 2, 0, 3, 4).reshape(2, total, part)
    grad_w_in_t, grad_w_out = grad_w_of(pre, grad_pre_all, cols, scale_back)
    grad_in = jnp.sum(blocks.astype(jnp.float32), axis=0).astype(jnp.bfloat16)
    return (grad_in, grad_w_in_t.T, grad_w_out)


def solution(mesh):
    placed = (
        P(("tokens", "mp"), None),
        P(("tokens", "mp"), None),
        P("tokens", "mp"),
        P(None, "mp"),
        P("mp", None),
    )
    return jax.shard_map(
        shards,
        mesh=mesh,
        in_specs=placed,
        out_specs=(P(("tokens", "mp"), None), P("tokens", "mp"), P("mp", "tokens")),
        check_vma=False,
    )
```

```python
import functools
import math

import jax
import jax.numpy as jnp
from jax import lax
from jax.experimental import pallas as pl
from jax.experimental.pallas import tpu as pltpu
from jax.sharding import PartitionSpec as P

root_two_pi = math.sqrt(2.0 / math.pi)
cubic = 0.044715


def gelu_value(pre):
    inner = root_two_pi * (pre + cubic * pre * pre * pre)
    return 0.5 * pre * (1.0 + jnp.tanh(inner))


def gelu_slope(pre):
    tanh_val = jnp.tanh(root_two_pi * (pre + cubic * pre * pre * pre))
    return 0.5 * (1.0 + tanh_val) + 0.5 * pre * (1.0 - tanh_val * tanh_val) * root_two_pi * (
        1.0 + 3.0 * cubic * pre * pre
    )


def partner(i, k, n):
    if n & (n - 1) == 0:
        return i ^ k
    return (i + k) % n if isinstance(i, int) else lax.rem(i + k, n)


def fetch(x, axis, k):
    n = lax.axis_size(axis)
    return lax.ppermute(x, axis, [(partner(i, k, n), i) for i in range(n)])


def other_core(x):
    return lax.ppermute(x, "mp", [(i ^ 1, i) for i in range(lax.axis_size("mp"))])


def chip_pairs(k):
    n = lax.axis_size("mp")
    return [(i, partner(i // 2, k, n // 2) * 2 + i % 2) for i in range(n)]


def fetch_chip(x, k):
    return lax.ppermute(x, "mp", [(there, here) for here, there in chip_pairs(k)])


def give_chip(x, k):
    return lax.ppermute(x, "mp", chip_pairs(k))


def block_of(size, most, unit):
    return max([b for b in range(unit, most + 1, unit) if size % b == 0], default=size)


def call(body, shapes, args, name, scratch=(), limit=8, flops=10**6, bytes_accessed=10**5, out_space=pltpu.VMEM):
    return pl.pallas_call(
        body,
        in_specs=[pl.BlockSpec(memory_space=pltpu.VMEM)] * len(args),
        out_specs=[pl.BlockSpec(memory_space=out_space)] * len(shapes),
        out_shape=[jax.ShapeDtypeStruct(*shape) for shape in shapes],
        scratch_shapes=list(scratch),
        compiler_params=pltpu.CompilerParams(vmem_limit_bytes=limit << 20),
        cost_estimate=pl.CostEstimate(
            flops=flops, bytes_accessed=bytes_accessed, transcendentals=0
        ),
        name=name,
    )(*args)


def place_of(block, chips):
    m = lax.axis_index("mp")
    core, k = divmod(block, chips)
    return 2 * partner(lax.shift_right_logical(m, 1), k, chips) + ((m & 1) ^ core)


def pack_body(tokens_ref, grad_ref, pre_ref, *refs):
    *packed, own, pre_copy, grad_copy, slabs = refs
    places, rows, part = slabs.shape
    hidden = pre_ref.shape[1]
    grad_copy[...] = grad_ref[...]
    both = jnp.concatenate(
        [tokens_ref[...].astype(jnp.float32), grad_ref[...].astype(jnp.float32)], axis=0
    )
    for p in range(places):
        slabs[p] = both[:, p * part : (p + 1) * part]
    t = lax.axis_index("tokens")
    own[...] = slabs[t].astype(jnp.bfloat16)
    pre_copy[...] = pre_ref[...]
    pre = pre_ref[...].astype(jnp.float32)
    for k, ref in enumerate(packed, 1):
        taker = t ^ k if places & (places - 1) == 0 else lax.rem(t - k + places, places)
        wide = ref.shape[1]
        ref[...] = jnp.concatenate(
            [
                jnp.pad(pre, ((0, 0), (0, wide - hidden))),
                jnp.pad(slabs[taker], ((0, 0), (0, wide - part))),
            ],
            axis=0,
        ).astype(jnp.bfloat16)


def pack(tokens_in, grad_out, pre_act, n_tok):
    rows, width = tokens_in.shape
    group, hidden = pre_act.shape
    part = width // n_tok
    shapes = [(group + 2 * rows, max(hidden, part))] * (n_tok - 1)
    shapes += [(2 * rows, part), pre_act.shape, grad_out.shape]
    return call(
        pack_body,
        [(shape, jnp.bfloat16) for shape in shapes],
        [tokens_in, grad_out, pre_act],
        "pack",
        [pltpu.VMEM((n_tok, 2 * rows, part), jnp.float32)],
        flops=10**10,
        bytes_accessed=36 * 10**6,
    )


def join_body(*refs):
    *pieces, out = refs
    out[...] = jnp.concatenate([x[...].astype(jnp.float32) for x in pieces], axis=0).astype(
        jnp.bfloat16
    )


def join(pieces):
    shape = (sum(x.shape[0] for x in pieces), pieces[0].shape[1])
    return call(join_body, [(shape, jnp.bfloat16)], pieces, "join")[0]


def sort_body(own, *refs):
    *packed, out = refs
    rows, part = own.shape[0] // 2, own.shape[1]
    pieces = [own[...].astype(jnp.float32)]
    for ref in packed:
        group = ref.shape[0] - 2 * rows
        pieces.append(ref[...].astype(jnp.float32)[group:, :part])
    for a in range(2):
        out[a] = jnp.concatenate([x[a * rows : (a + 1) * rows] for x in pieces], axis=0).astype(
            jnp.bfloat16
        )


def sort(own, packed):
    shape = (2, own.shape[0] // 2 * (len(packed) + 1), own.shape[1])
    return call(sort_body, [(shape, jnp.bfloat16)], [own, *packed], "sort")[0]


def stack_body(*refs):
    *pieces, out = refs
    for k, x in enumerate(pieces):
        out[k] = x[...]


def stack(pieces):
    shape = (len(pieces),) + pieces[0].shape
    return call(stack_body, [(shape, jnp.bfloat16)], pieces, "stack")[0]


def grad_pre_body(block, own_ref, other_ref, pre_ref, w_ref, out_ref, rows, total):
    hidden, group = total.shape
    half = own_ref.shape[0]
    rows[:half, :] = own_ref[...]
    rows[half:, :] = other_ref[...]
    for low in range(0, hidden, block):
        here = slice(low, low + block)
        total[here, :] = lax.dot_general(
            w_ref[here, :], rows[...], (((1,), (1,)), ((), ())), preferred_element_type=jnp.float32
        )
    each = group // lax.axis_size("mp")
    chips = half // each
    row = lax.broadcasted_iota(jnp.int32, (group, 1), 0)
    from_row = row
    for b in range(group // each):
        inside = (row >= b * each) & (row < (b + 1) * each)
        from_row = jnp.where(inside, row + (place_of(b, chips) - b) * each, from_row)
    pick = from_row == lax.broadcasted_iota(jnp.int32, (group, group), 1)
    pre = jnp.dot(
        pick.astype(jnp.float32).astype(jnp.bfloat16), pre_ref[...], preferred_element_type=jnp.float32
    )
    out_ref[...] = (total[...].T * gelu_slope(pre)).astype(jnp.bfloat16)


def grad_pre_of(own, other, pre_act, w_out):
    group, hidden = pre_act.shape
    width = w_out.shape[1]
    return call(
        functools.partial(grad_pre_body, block_of(hidden, 432, 16)),
        [((group, hidden), jnp.bfloat16)],
        [own, other, pre_act, w_out],
        "grad_pre",
        [pltpu.VMEM((group, width), jnp.bfloat16), pltpu.VMEM((hidden, group), jnp.float32)],
        flops=2 * group * width * hidden,
        bytes_accessed=2 * hidden * width,
    )[0]


def grad_in_body(block, grad_pre_ref, w_ref, own_ref, other_ref):
    half, width = own_ref.shape
    for low in range(0, width, block):
        here = slice(low, low + block)
        term = jnp.dot(grad_pre_ref[...], w_ref[:, here], preferred_element_type=jnp.float32)
        own_ref[:, here] = term[:half]
        other_ref[:, here] = term[half:].astype(jnp.bfloat16)


def grad_in_part(grad_pre, w_in_t):
    group, hidden = grad_pre.shape
    width = w_in_t.shape[1]
    half = (group // 2, width)
    return call(
        functools.partial(grad_in_body, block_of(width, 1024, 128)),
        [(half, jnp.float32), (half, jnp.bfloat16)],
        [grad_pre, w_in_t],
        "grad_in_part",
        flops=2 * group * width * hidden,
        bytes_accessed=2 * hidden * width,
    )


def pair_body(own_ref, other_ref, first_ref, *rest):
    rows = first_ref.shape[0]
    total = own_ref[...] + other_ref[...].astype(jnp.float32)
    first_ref[...] = total[:rows]
    for k, ref in enumerate(rest, 1):
        ref[...] = total[k * rows : (k + 1) * rows].astype(jnp.bfloat16)


def pair(own, other, chips):
    shape = (own.shape[0] // chips, own.shape[1])
    shapes = [(shape, jnp.float32)] + [(shape, jnp.bfloat16)] * (chips - 1)
    return call(pair_body, shapes, [own, other], "pair")


def finish_body(first_ref, *refs):
    *rest, out = refs
    total = first_ref[...]
    for ref in rest:
        total = total + ref[...].astype(jnp.float32)
    out[...] = total.astype(jnp.bfloat16)


def finish(first, rest):
    return call(finish_body, [(first.shape, jnp.bfloat16)], [first, *rest], "finish")[0]


def turn(x_ref, to_ref, unit):
    hidden = x_ref.shape[1]
    for low in range(0, hidden, unit):
        size = min(unit, hidden - low)
        eye = lax.broadcasted_iota(jnp.int32, (size, size), 0) == lax.broadcasted_iota(
            jnp.int32, (size, size), 1
        )
        to_ref[low : low + size, :] = lax.dot_general(
            eye.astype(jnp.float32).astype(jnp.bfloat16),
            x_ref[:, low : low + size],
            (((1,), (1,)), ((), ())),
            preferred_element_type=jnp.float32,
        ).astype(jnp.bfloat16)


def grad_w_body(places, scale_back, block, *refs):
    pre_refs, grad_pre_refs = refs[:places], refs[places : 2 * places]
    own_ref, other_ref, in_ref, out_ref, flat, sorted_rows, turned, held_in, held_out, sems = refs[
        2 * places :
    ]
    group, hidden = grad_pre_refs[0].shape
    chips, _, each, part = own_ref.shape
    rows = each // places
    total = places * group
    copies = []

    def arrange(place):
        size = block_of(total, 128, each)
        for low in range(0, total, size):
            row = low + lax.broadcasted_iota(jnp.int32, (size, 1), 0)
            from_row = row
            for b in range(low // each, (low + size) // each):
                for k in range(places):
                    first = b * each + k * rows
                    inside = (row >= first) & (row < first + rows)
                    shift = k * group + place(b) * rows - first
                    from_row = jnp.where(inside, row + shift, from_row)
            pick = from_row == lax.broadcasted_iota(jnp.int32, (size, total), 1)
            sorted_rows[low : low + size, :] = jnp.dot(
                pick.astype(jnp.float32).astype(jnp.bfloat16),
                flat[...],
                preferred_element_type=jnp.float32,
            ).astype(jnp.bfloat16)
        turn(sorted_rows, turned, 256)

    def product(right, held, to_ref):
        for low in range(0, part, block):
            here = slice(low, low + block)
            cols = jnp.concatenate(
                [ref[k, right, :, here] for ref in (own_ref, other_ref) for k in range(chips)], axis=0
            )
            term = jnp.dot(turned[...], cols, preferred_element_type=jnp.float32)
            held[:, here] = (term * scale_back).astype(jnp.bfloat16)
            copies.append(
                pltpu.make_async_copy(held.at[:, here], to_ref.at[:, here], sems.at[len(copies)])
            )
            copies[-1].start()

    for k in range(places):
        pre = pre_refs[k][:group, :hidden].astype(jnp.float32)
        flat[k * group : (k + 1) * group, :] = gelu_value(pre).astype(jnp.bfloat16)
    arrange(lambda b: place_of(b, chips))
    product(1, held_out, out_ref)
    for k in range(places):
        flat[k * group : (k + 1) * group, :] = grad_pre_refs[k][...]
    arrange(lambda b: b)
    product(0, held_in, in_ref)
    for copy in copies:
        copy.wait()


def grad_w_of(pre, grad_pre, own, other, scale_back):
    places = len(pre)
    group, hidden = grad_pre[0].shape
    total, part = places * group, own.shape[3]
    block = block_of(part, 256, 128)
    return call(
        functools.partial(grad_w_body, places, scale_back, block),
        [((hidden, part), jnp.bfloat16)] * 2,
        [*pre, *grad_pre, own, other],
        "grad_w",
        [
            pltpu.VMEM((total, hidden), jnp.bfloat16),
            pltpu.VMEM((total, hidden), jnp.bfloat16),
            pltpu.VMEM((hidden, total), jnp.bfloat16),
            pltpu.VMEM((hidden, part), jnp.bfloat16),
            pltpu.VMEM((hidden, part), jnp.bfloat16),
            pltpu.SemaphoreType.DMA((2 * (part // block),)),
        ],
        limit=20,
        flops=80 * total * part * hidden,
        bytes_accessed=40 * hidden * part,
        out_space=pltpu.HBM,
    )


def shards(tokens_in, grad_out, pre_act, w_in, w_out):
    n_mp, n_tok = lax.axis_size("mp"), lax.axis_size("tokens")
    chips = n_mp // 2
    scale_back = 1.0 / math.sqrt(pre_act.shape[0] * n_tok)

    rows_grad = [fetch_chip(grad_out, k) for k in range(1, chips)]
    *packed, own_piece, pre_act, grad_out = pack(tokens_in, grad_out, pre_act, n_tok)
    own_rows = join([grad_out, *rows_grad])
    other_rows = other_core(own_rows)
    packed = [fetch(x, "tokens", k) for k, x in enumerate(packed, 1)]

    grad_pre = grad_pre_of(own_rows, other_rows, pre_act, w_out)
    grad_pre_all = [grad_pre] + [fetch(grad_pre, "tokens", k) for k in range(1, n_tok)]

    packed, own_piece, grad_pre = lax.optimization_barrier((packed, own_piece, grad_pre))
    cols = sort(own_piece, packed)
    cols_chips = [fetch_chip(cols, k) for k in range(1, chips)]

    own, other = grad_in_part(grad_pre, w_in.T)
    first, *rest = pair(own, other_core(other), chips)
    rest = [give_chip(x, k) for k, x in enumerate(rest, 1)]

    own_cols = stack([cols, *cols_chips])
    other_cols = other_core(own_cols)
    grad_w_in_t, grad_w_out = grad_w_of(
        [pre_act] + packed, grad_pre_all, own_cols, other_cols, scale_back
    )
    return (finish(first, rest), grad_w_in_t.T, grad_w_out)


def solution(mesh):
    placed = (
        P(("tokens", "mp"), None),
        P(("tokens", "mp"), None),
        P("tokens", "mp"),
        P(None, "mp"),
        P("mp", None),
    )
    return jax.shard_map(
        shards,
        mesh=mesh,
        in_specs=placed,
        out_specs=(P(("tokens", "mp"), None), P("tokens", "mp"), P("mp", "tokens")),
        check_vma=False,
    )
```

```python
import functools
import math

import jax
import jax.numpy as jnp
from jax import lax
from jax.experimental import pallas as pl
from jax.experimental.pallas import tpu as pltpu
from jax.sharding import PartitionSpec as P

root_two_pi = math.sqrt(2.0 / math.pi)
cubic = 0.044715


def gelu_value(pre):
    inner = root_two_pi * (pre + cubic * pre * pre * pre)
    return 0.5 * pre * (1.0 + jnp.tanh(inner))


def gelu_slope(pre):
    tanh_val = jnp.tanh(root_two_pi * (pre + cubic * pre * pre * pre))
    return 0.5 * (1.0 + tanh_val) + 0.5 * pre * (1.0 - tanh_val * tanh_val) * root_two_pi * (
        1.0 + 3.0 * cubic * pre * pre
    )


def partner(i, k, n):
    if n & (n - 1) == 0:
        return i ^ k
    return (i + k) % n if isinstance(i, int) else lax.rem(i + k, n)


def fetch(x, axis, k):
    n = lax.axis_size(axis)
    return lax.ppermute(x, axis, [(partner(i, k, n), i) for i in range(n)])


def other_core(x):
    return lax.ppermute(x, "mp", [(i ^ 1, i) for i in range(lax.axis_size("mp"))])


def chip_pairs(k):
    n = lax.axis_size("mp")
    return [(i, partner(i // 2, k, n // 2) * 2 + i % 2) for i in range(n)]


def fetch_chip(x, k):
    return lax.ppermute(x, "mp", [(there, here) for here, there in chip_pairs(k)])


def give_chip(x, k):
    return lax.ppermute(x, "mp", chip_pairs(k))


def block_of(size, most, unit):
    return max([b for b in range(unit, most + 1, unit) if size % b == 0], default=size)


def call(body, shapes, args, name, scratch=(), limit=8, flops=10**6, bytes_accessed=10**5,
         in_space=pltpu.VMEM, out_space=pltpu.VMEM):
    return pl.pallas_call(
        body,
        in_specs=[pl.BlockSpec(memory_space=in_space)] * len(args),
        out_specs=[pl.BlockSpec(memory_space=out_space)] * len(shapes),
        out_shape=[jax.ShapeDtypeStruct(*shape) for shape in shapes],
        scratch_shapes=list(scratch),
        compiler_params=pltpu.CompilerParams(vmem_limit_bytes=limit << 20),
        cost_estimate=pl.CostEstimate(
            flops=flops, bytes_accessed=bytes_accessed, transcendentals=0
        ),
        name=name,
    )(*args)


def place_of(block, chips):
    m = lax.axis_index("mp")
    core, k = divmod(block, chips)
    return 2 * partner(lax.shift_right_logical(m, 1), k, chips) + ((m & 1) ^ core)


def lead_body(out):
    out[...] = jnp.zeros_like(out)


def lead():
    return call(
        lead_body, [((8, 128), jnp.float32)], [], "lead", flops=10**10, bytes_accessed=36 * 10**6
    )[0]


def pack_body(tokens_in, grad_in, pre_in, after, *refs):
    *packed, own, pre_ref, grad_ref, slabs, tokens_ref, sems = refs
    copies = [
        pltpu.make_async_copy(source, target, sems.at[i])
        for i, (source, target) in enumerate(
            ((tokens_in, tokens_ref), (grad_in, grad_ref), (pre_in, pre_ref))
        )
    ]
    for copy in copies:
        copy.start()
    for copy in copies:
        copy.wait()
    places, rows, part = slabs.shape
    hidden = pre_ref.shape[1]
    both = jnp.concatenate(
        [tokens_ref[...].astype(jnp.float32), grad_ref[...].astype(jnp.float32)], axis=0
    )
    for p in range(places):
        slabs[p] = both[:, p * part : (p + 1) * part]
    t = lax.axis_index("tokens")
    own[...] = slabs[t].astype(jnp.bfloat16)
    pre = pre_ref[...].astype(jnp.float32)
    for k, ref in enumerate(packed, 1):
        taker = t ^ k if places & (places - 1) == 0 else lax.rem(t - k + places, places)
        wide = ref.shape[1]
        ref[...] = jnp.concatenate(
            [
                jnp.pad(pre, ((0, 0), (0, wide - hidden))),
                jnp.pad(slabs[taker], ((0, 0), (0, wide - part))),
            ],
            axis=0,
        ).astype(jnp.bfloat16)


def pack(tokens_in, grad_out, pre_act, n_tok, after):
    rows, width = tokens_in.shape
    group, hidden = pre_act.shape
    part = width // n_tok
    shapes = [(group + 2 * rows, max(hidden, part))] * (n_tok - 1)
    shapes += [(2 * rows, part), pre_act.shape, grad_out.shape]
    return call(
        pack_body,
        [(shape, jnp.bfloat16) for shape in shapes],
        [tokens_in, grad_out, pre_act, after],
        "pack",
        [
            pltpu.VMEM((n_tok, 2 * rows, part), jnp.float32),
            pltpu.VMEM(tokens_in.shape, jnp.bfloat16),
            pltpu.SemaphoreType.DMA((3,)),
        ],
        flops=10**10,
        bytes_accessed=36 * 10**6,
        in_space=pltpu.HBM,
    )


def join_body(after, *refs):
    *pieces, out = refs
    out[...] = jnp.concatenate([x[...].astype(jnp.float32) for x in pieces], axis=0).astype(
        jnp.bfloat16
    )


def join(pieces, after):
    shape = (sum(x.shape[0] for x in pieces), pieces[0].shape[1])
    return call(join_body, [(shape, jnp.bfloat16)], [after, *pieces], "join")[0]


def sort_body(own, *refs):
    *packed, out = refs
    rows, part = own.shape[0] // 2, own.shape[1]
    pieces = [own[...].astype(jnp.float32)]
    for ref in packed:
        group = ref.shape[0] - 2 * rows
        pieces.append(ref[...].astype(jnp.float32)[group:, :part])
    for a in range(2):
        out[a] = jnp.concatenate([x[a * rows : (a + 1) * rows] for x in pieces], axis=0).astype(
            jnp.bfloat16
        )


def sort(own, packed):
    shape = (2, own.shape[0] // 2 * (len(packed) + 1), own.shape[1])
    return call(sort_body, [(shape, jnp.bfloat16)], [own, *packed], "sort")[0]


def stack_body(*refs):
    *pieces, out = refs
    for k, x in enumerate(pieces):
        out[k] = x[...]


def stack(pieces):
    shape = (len(pieces),) + pieces[0].shape
    return call(stack_body, [(shape, jnp.bfloat16)], pieces, "stack")[0]


def grad_pre_body(block, own_ref, other_ref, pre_ref, w_ref, out_ref, rows, total):
    hidden, group = total.shape
    half = own_ref.shape[0]
    rows[:half, :] = own_ref[...]
    rows[half:, :] = other_ref[...]
    for low in range(0, hidden, block):
        here = slice(low, low + block)
        total[here, :] = lax.dot_general(
            w_ref[here, :], rows[...], (((1,), (1,)), ((), ())), preferred_element_type=jnp.float32
        )
    each = group // lax.axis_size("mp")
    chips = half // each
    row = lax.broadcasted_iota(jnp.int32, (group, 1), 0)
    from_row = row
    for b in range(group // each):
        inside = (row >= b * each) & (row < (b + 1) * each)
        from_row = jnp.where(inside, row + (place_of(b, chips) - b) * each, from_row)
    pick = from_row == lax.broadcasted_iota(jnp.int32, (group, group), 1)
    pre = jnp.dot(
        pick.astype(jnp.float32).astype(jnp.bfloat16), pre_ref[...], preferred_element_type=jnp.float32
    )
    out_ref[...] = (total[...].T * gelu_slope(pre)).astype(jnp.bfloat16)


def grad_pre_of(own, other, pre_act, w_out):
    group, hidden = pre_act.shape
    width = w_out.shape[1]
    return call(
        functools.partial(grad_pre_body, block_of(hidden, 432, 16)),
        [((group, hidden), jnp.bfloat16)],
        [own, other, pre_act, w_out],
        "grad_pre",
        [pltpu.VMEM((group, width), jnp.bfloat16), pltpu.VMEM((hidden, group), jnp.float32)],
    )[0]


def grad_in_body(block, grad_pre_ref, w_ref, after, out_ref):
    places, rows, width = out_ref.shape
    for low in range(0, width, block):
        here = slice(low, low + block)
        term = jnp.dot(grad_pre_ref[...], w_ref[:, here], preferred_element_type=jnp.float32)
        for b in range(places):
            out_ref[place_of(b, places // 2), :, here] = term[b * rows : (b + 1) * rows].astype(
                jnp.bfloat16
            )


def grad_in_part(grad_pre, w_in_t, places, after):
    group, hidden = grad_pre.shape
    width = w_in_t.shape[1]
    return call(
        functools.partial(grad_in_body, block_of(width, 1024, 128)),
        [((places, group // places, width), jnp.bfloat16)],
        [grad_pre, w_in_t, after],
        "grad_in_part",
        flops=2 * group * width * hidden,
        bytes_accessed=2 * hidden * width,
    )[0]


def finish_body(terms_ref, out):
    total = terms_ref[0].astype(jnp.float32)
    for k in range(1, terms_ref.shape[0]):
        total = total + terms_ref[k].astype(jnp.float32)
    out[...] = total.astype(jnp.bfloat16)


def finish(terms):
    return call(finish_body, [(terms.shape[1:], jnp.bfloat16)], [terms], "finish")[0]


def turn(x_ref, to_ref, unit):
    hidden = x_ref.shape[1]
    for low in range(0, hidden, unit):
        size = min(unit, hidden - low)
        eye = lax.broadcasted_iota(jnp.int32, (size, size), 0) == lax.broadcasted_iota(
            jnp.int32, (size, size), 1
        )
        to_ref[low : low + size, :] = lax.dot_general(
            eye.astype(jnp.float32).astype(jnp.bfloat16),
            x_ref[:, low : low + size],
            (((1,), (1,)), ((), ())),
            preferred_element_type=jnp.float32,
        ).astype(jnp.bfloat16)


def grad_w_body(places, scale_back, block, *refs):
    pre_refs, grad_pre_refs = refs[:places], refs[places : 2 * places]
    own_ref, other_ref, in_ref, out_ref, flat, sorted_rows, turned, held_in, held_out, sems = refs[
        2 * places :
    ]
    group, hidden = grad_pre_refs[0].shape
    chips, _, each, part = own_ref.shape
    rows = each // places
    total = places * group
    copies = []

    def arrange(place):
        size = block_of(total, 128, each)
        for low in range(0, total, size):
            row = low + lax.broadcasted_iota(jnp.int32, (size, 1), 0)
            from_row = row
            for b in range(low // each, (low + size) // each):
                for k in range(places):
                    first = b * each + k * rows
                    inside = (row >= first) & (row < first + rows)
                    shift = k * group + place(b) * rows - first
                    from_row = jnp.where(inside, row + shift, from_row)
            pick = from_row == lax.broadcasted_iota(jnp.int32, (size, total), 1)
            sorted_rows[low : low + size, :] = jnp.dot(
                pick.astype(jnp.float32).astype(jnp.bfloat16),
                flat[...],
                preferred_element_type=jnp.float32,
            ).astype(jnp.bfloat16)
        turn(sorted_rows, turned, 256)

    def product(right, held, to_ref):
        for low in range(0, part, block):
            here = slice(low, low + block)
            cols = jnp.concatenate(
                [ref[k, right, :, here] for ref in (own_ref, other_ref) for k in range(chips)], axis=0
            )
            term = jnp.dot(turned[...], cols, preferred_element_type=jnp.float32)
            held[:, here] = (term * scale_back).astype(jnp.bfloat16)
            copies.append(
                pltpu.make_async_copy(held.at[:, here], to_ref.at[:, here], sems.at[len(copies)])
            )
            copies[-1].start()

    for k in range(places):
        pre = pre_refs[k][:group, :hidden].astype(jnp.float32)
        flat[k * group : (k + 1) * group, :] = gelu_value(pre).astype(jnp.bfloat16)
    arrange(lambda b: place_of(b, chips))
    product(1, held_out, out_ref)
    for k in range(places):
        flat[k * group : (k + 1) * group, :] = grad_pre_refs[k][...]
    arrange(lambda b: b)
    product(0, held_in, in_ref)
    for copy in copies:
        copy.wait()


def grad_w_of(pre, grad_pre, own, other, scale_back):
    places = len(pre)
    group, hidden = grad_pre[0].shape
    total, part = places * group, own.shape[3]
    block = block_of(part, 256, 128)
    return call(
        functools.partial(grad_w_body, places, scale_back, block),
        [((hidden, part), jnp.bfloat16)] * 2,
        [*pre, *grad_pre, own, other],
        "grad_w",
        [
            pltpu.VMEM((total, hidden), jnp.bfloat16),
            pltpu.VMEM((total, hidden), jnp.bfloat16),
            pltpu.VMEM((hidden, total), jnp.bfloat16),
            pltpu.VMEM((hidden, part), jnp.bfloat16),
            pltpu.VMEM((hidden, part), jnp.bfloat16),
            pltpu.SemaphoreType.DMA((2 * (part // block),)),
        ],
        limit=20,
        flops=80 * total * part * hidden,
        bytes_accessed=40 * hidden * part,
        out_space=pltpu.HBM,
    )


def shards(tokens_in, grad_out, pre_act, w_in, w_out):
    n_mp, n_tok = lax.axis_size("mp"), lax.axis_size("tokens")
    chips = n_mp // 2
    scale_back = 1.0 / math.sqrt(pre_act.shape[0] * n_tok)

    rows_grad = [fetch_chip(grad_out, k) for k in range(1, chips)]
    *packed, own_piece, pre_act, grad_out = pack(tokens_in, grad_out, pre_act, n_tok, lead())
    packed = [fetch(x, "tokens", k) for k, x in enumerate(packed, 1)]
    own_rows = join([grad_out, *rows_grad], packed[0])
    other_rows = other_core(own_rows)

    grad_pre = grad_pre_of(own_rows, other_rows, pre_act, w_out)
    grad_pre_all = [grad_pre] + [fetch(grad_pre, "tokens", k) for k in range(1, n_tok)]

    packed, own_piece, grad_pre = lax.optimization_barrier((packed, own_piece, grad_pre))
    cols = sort(own_piece, packed)
    cols_chips = [fetch_chip(cols, k) for k in range(1, chips)]

    terms = lax.all_to_all(grad_in_part(grad_pre, w_in.T, n_mp, grad_pre_all[1]), "mp", 0, 0)

    own_cols = stack([cols, *cols_chips])
    other_cols = other_core(own_cols)
    grad_w_in_t, grad_w_out = grad_w_of(
        [pre_act] + packed, grad_pre_all, own_cols, other_cols, scale_back
    )
    return (finish(terms), grad_w_in_t.T, grad_w_out)


def solution(mesh):
    placed = (
        P(("tokens", "mp"), None),
        P(("tokens", "mp"), None),
        P("tokens", "mp"),
        P(None, "mp"),
        P("mp", None),
    )
    return jax.shard_map(
        shards,
        mesh=mesh,
        in_specs=placed,
        out_specs=(P(("tokens", "mp"), None), P("tokens", "mp"), P("mp", "tokens")),
        check_vma=False,
    )
```

```python
import functools
import math

import jax
import jax.numpy as jnp
from jax import lax
from jax.experimental import pallas as pl
from jax.experimental.pallas import tpu as pltpu
from jax.sharding import PartitionSpec as P

root_two_pi = math.sqrt(2.0 / math.pi)
cubic = 0.044715


def gelu_value(pre):
    inner = root_two_pi * (pre + cubic * pre * pre * pre)
    return 0.5 * pre * (1.0 + jnp.tanh(inner))


def gelu_slope(pre):
    tanh_val = jnp.tanh(root_two_pi * (pre + cubic * pre * pre * pre))
    return 0.5 * (1.0 + tanh_val) + 0.5 * pre * (1.0 - tanh_val * tanh_val) * root_two_pi * (
        1.0 + 3.0 * cubic * pre * pre
    )


def partner(i, k, n):
    if n & (n - 1) == 0:
        return i ^ k
    return (i + k) % n if isinstance(i, int) else lax.rem(i + k, n)


def fetch(x, axis, k):
    n = lax.axis_size(axis)
    return lax.ppermute(x, axis, [(partner(i, k, n), i) for i in range(n)])


def other_core(x):
    return lax.ppermute(x, "mp", [(i ^ 1, i) for i in range(lax.axis_size("mp"))])


def chip_pairs(k):
    n = lax.axis_size("mp")
    return [(i, partner(i // 2, k, n // 2) * 2 + i % 2) for i in range(n)]


def fetch_chip(x, k):
    return lax.ppermute(x, "mp", [(there, here) for here, there in chip_pairs(k)])


def give_chip(x, k):
    return lax.ppermute(x, "mp", chip_pairs(k))


def block_of(size, most, unit):
    return max([b for b in range(unit, most + 1, unit) if size % b == 0], default=size)


def call(body, shapes, args, name, scratch=(), limit=8, flops=10**6, bytes_accessed=10**5,
         in_space=pltpu.VMEM, out_spaces=None):
    return pl.pallas_call(
        body,
        in_specs=[pl.BlockSpec(memory_space=in_space)] * len(args),
        out_specs=[
            pl.BlockSpec(memory_space=space) for space in out_spaces or [pltpu.VMEM] * len(shapes)
        ],
        out_shape=[jax.ShapeDtypeStruct(*shape) for shape in shapes],
        scratch_shapes=list(scratch),
        compiler_params=pltpu.CompilerParams(vmem_limit_bytes=limit << 20),
        cost_estimate=pl.CostEstimate(
            flops=flops, bytes_accessed=bytes_accessed, transcendentals=0
        ),
        name=name,
    )(*args)


def place_of(block, chips):
    m = lax.axis_index("mp")
    core, k = divmod(block, chips)
    return 2 * partner(lax.shift_right_logical(m, 1), k, chips) + ((m & 1) ^ core)


def lead_body(out):
    out[...] = jnp.zeros_like(out)


def lead():
    return call(
        lead_body, [((8, 128), jnp.float32)], [], "lead", flops=10**10, bytes_accessed=36 * 10**6
    )[0]


def pack_body(tokens_in, grad_in, pre_in, after, *refs):
    *pieces, own, pre_ref, grad_ref, slabs, tokens_ref, sems = refs
    copies = [
        pltpu.make_async_copy(source, target, sems.at[i])
        for i, (source, target) in enumerate(
            ((tokens_in, tokens_ref), (grad_in, grad_ref), (pre_in, pre_ref))
        )
    ]
    for copy in copies:
        copy.start()
    for copy in copies:
        copy.wait()
    places, rows, part = slabs.shape
    both = jnp.concatenate(
        [tokens_ref[...].astype(jnp.float32), grad_ref[...].astype(jnp.float32)], axis=0
    )
    for p in range(places):
        slabs[p] = both[:, p * part : (p + 1) * part]
    t = lax.axis_index("tokens")
    own[...] = slabs[t].astype(jnp.bfloat16)
    for k, ref in enumerate(pieces, 1):
        taker = t ^ k if places & (places - 1) == 0 else lax.rem(t - k + places, places)
        ref[...] = slabs[taker].astype(jnp.bfloat16)


def pack(tokens_in, grad_out, pre_act, n_tok, after):
    rows, width = tokens_in.shape
    part = width // n_tok
    shapes = [(2 * rows, part)] * n_tok + [pre_act.shape, grad_out.shape]
    return call(
        pack_body,
        [(shape, jnp.bfloat16) for shape in shapes],
        [tokens_in, grad_out, pre_act, after],
        "pack",
        [
            pltpu.VMEM((n_tok, 2 * rows, part), jnp.float32),
            pltpu.VMEM(tokens_in.shape, jnp.bfloat16),
            pltpu.SemaphoreType.DMA((3,)),
        ],
        flops=10**10,
        bytes_accessed=36 * 10**6,
        in_space=pltpu.HBM,
    )


def join_body(after, *refs):
    *pieces, out = refs
    out[...] = jnp.concatenate([x[...].astype(jnp.float32) for x in pieces], axis=0).astype(
        jnp.bfloat16
    )


def join(pieces, after):
    shape = (sum(x.shape[0] for x in pieces), pieces[0].shape[1])
    return call(join_body, [(shape, jnp.bfloat16)], [after, *pieces], "join")[0]


def sort_body(*refs):
    *pieces, out = refs
    rows = pieces[0].shape[0] // 2
    pieces = [x[...].astype(jnp.float32) for x in pieces]
    for a in range(2):
        out[a] = jnp.concatenate([x[a * rows : (a + 1) * rows] for x in pieces], axis=0).astype(
            jnp.bfloat16
        )


def sort(pieces):
    rows, part = pieces[0].shape
    shape = (2, rows // 2 * len(pieces), part)
    return call(sort_body, [(shape, jnp.bfloat16)], pieces, "sort")[0]


def stack_body(*refs):
    *pieces, out = refs
    for k, x in enumerate(pieces):
        out[k] = x[...]


def stack(pieces):
    shape = (len(pieces),) + pieces[0].shape
    return call(stack_body, [(shape, jnp.bfloat16)], pieces, "stack")[0]


def grad_pre_body(block, own_ref, other_ref, pre_ref, w_ref, after, out_ref, rows, total):
    hidden, group = total.shape
    half = own_ref.shape[0]
    rows[:half, :] = own_ref[...]
    rows[half:, :] = other_ref[...]
    for low in range(0, hidden, block):
        here = slice(low, low + block)
        total[here, :] = lax.dot_general(
            w_ref[here, :], rows[...], (((1,), (1,)), ((), ())), preferred_element_type=jnp.float32
        )
    each = group // lax.axis_size("mp")
    chips = half // each
    row = lax.broadcasted_iota(jnp.int32, (group, 1), 0)
    from_row = row
    for b in range(group // each):
        inside = (row >= b * each) & (row < (b + 1) * each)
        from_row = jnp.where(inside, row + (place_of(b, chips) - b) * each, from_row)
    pick = from_row == lax.broadcasted_iota(jnp.int32, (group, group), 1)
    pre = jnp.dot(
        pick.astype(jnp.float32).astype(jnp.bfloat16), pre_ref[...], preferred_element_type=jnp.float32
    )
    out_ref[...] = (total[...].T * gelu_slope(pre)).astype(jnp.bfloat16)


def grad_pre_of(own, other, pre_act, w_out, after):
    group, hidden = pre_act.shape
    width = w_out.shape[1]
    return call(
        functools.partial(grad_pre_body, block_of(hidden, 432, 16)),
        [((group, hidden), jnp.bfloat16)],
        [own, other, pre_act, w_out, after],
        "grad_pre",
        [pltpu.VMEM((group, width), jnp.bfloat16), pltpu.VMEM((hidden, group), jnp.float32)],
        flops=2 * group * width * hidden,
        bytes_accessed=2 * hidden * width,
    )[0]


def grad_in_body(block, grad_pre_ref, w_ref, *refs):
    out_ref = refs[-1]
    places, rows, width = out_ref.shape
    for low in range(0, width, block):
        here = slice(low, low + block)
        term = jnp.dot(grad_pre_ref[...], w_ref[:, here], preferred_element_type=jnp.float32)
        for b in range(places):
            out_ref[place_of(b, places // 2), :, here] = term[b * rows : (b + 1) * rows].astype(
                jnp.bfloat16
            )


def grad_in_part(grad_pre, w_in_t, places, after):
    group, hidden = grad_pre.shape
    width = w_in_t.shape[1]
    return call(
        functools.partial(grad_in_body, block_of(width, 1024, 128)),
        [((places, group // places, width), jnp.bfloat16)],
        [grad_pre, w_in_t, *after],
        "grad_in_part",
        flops=2 * group * width * hidden,
        bytes_accessed=2 * hidden * width,
    )[0]


def finish_body(terms_ref, after, out):
    total = terms_ref[0].astype(jnp.float32)
    for k in range(1, terms_ref.shape[0]):
        total = total + terms_ref[k].astype(jnp.float32)
    out[...] = total.astype(jnp.bfloat16)


def finish(terms, after):
    return call(finish_body, [(terms.shape[1:], jnp.bfloat16)], [terms, after], "finish")[0]


def turn(x_ref, to_ref, unit):
    hidden = x_ref.shape[1]
    for low in range(0, hidden, unit):
        size = min(unit, hidden - low)
        eye = lax.broadcasted_iota(jnp.int32, (size, size), 0) == lax.broadcasted_iota(
            jnp.int32, (size, size), 1
        )
        to_ref[low : low + size, :] = lax.dot_general(
            eye.astype(jnp.float32).astype(jnp.bfloat16),
            x_ref[:, low : low + size],
            (((1,), (1,)), ((), ())),
            preferred_element_type=jnp.float32,
        ).astype(jnp.bfloat16)


def grad_w_body(places, scale_back, block, *refs):
    pre_refs, grad_pre_refs = refs[:places], refs[places : 2 * places]
    own_ref, other_ref, in_ref, out_ref, end_ref = refs[2 * places : 2 * places + 5]
    flat, sorted_rows, turned, held_in, held_out, sems = refs[2 * places + 5 :]
    end_ref[...] = jnp.zeros_like(end_ref)
    group, hidden = grad_pre_refs[0].shape
    chips, _, each, part = own_ref.shape
    rows = each // places
    total = places * group
    copies = []

    def arrange(place):
        size = block_of(total, 128, each)
        for low in range(0, total, size):
            row = low + lax.broadcasted_iota(jnp.int32, (size, 1), 0)
            from_row = row
            for b in range(low // each, (low + size) // each):
                for k in range(places):
                    first = b * each + k * rows
                    inside = (row >= first) & (row < first + rows)
                    shift = k * group + place(b) * rows - first
                    from_row = jnp.where(inside, row + shift, from_row)
            pick = from_row == lax.broadcasted_iota(jnp.int32, (size, total), 1)
            sorted_rows[low : low + size, :] = jnp.dot(
                pick.astype(jnp.float32).astype(jnp.bfloat16),
                flat[...],
                preferred_element_type=jnp.float32,
            ).astype(jnp.bfloat16)
        turn(sorted_rows, turned, 256)

    def product(right, held, to_ref):
        for low in range(0, part, block):
            here = slice(low, low + block)
            cols = jnp.concatenate(
                [ref[k, right, :, here] for ref in (own_ref, other_ref) for k in range(chips)], axis=0
            )
            term = jnp.dot(turned[...], cols, preferred_element_type=jnp.float32)
            held[:, here] = (term * scale_back).astype(jnp.bfloat16)
            copies.append(
                pltpu.make_async_copy(held.at[:, here], to_ref.at[:, here], sems.at[len(copies)])
            )
            copies[-1].start()

    for k in range(places):
        pre = pre_refs[k][...].astype(jnp.float32)
        flat[k * group : (k + 1) * group, :] = gelu_value(pre).astype(jnp.bfloat16)
    arrange(lambda b: place_of(b, chips))
    product(1, held_out, out_ref)
    for k in range(places):
        flat[k * group : (k + 1) * group, :] = grad_pre_refs[k][...]
    arrange(lambda b: b)
    product(0, held_in, in_ref)
    for copy in copies:
        copy.wait()


def grad_w_of(pre, grad_pre, own, other, scale_back):
    places = len(pre)
    group, hidden = grad_pre[0].shape
    total, part = places * group, own.shape[3]
    block = block_of(part, 256, 128)
    return call(
        functools.partial(grad_w_body, places, scale_back, block),
        [((hidden, part), jnp.bfloat16)] * 2 + [((8, 128), jnp.float32)],
        [*pre, *grad_pre, own, other],
        "grad_w",
        [
            pltpu.VMEM((total, hidden), jnp.bfloat16),
            pltpu.VMEM((total, hidden), jnp.bfloat16),
            pltpu.VMEM((hidden, total), jnp.bfloat16),
            pltpu.VMEM((hidden, part), jnp.bfloat16),
            pltpu.VMEM((hidden, part), jnp.bfloat16),
            pltpu.SemaphoreType.DMA((2 * (part // block),)),
        ],
        limit=20,
        flops=80 * total * part * hidden,
        bytes_accessed=40 * hidden * part,
        out_spaces=[pltpu.HBM, pltpu.HBM, pltpu.VMEM],
    )


def shards(tokens_in, grad_out, pre_act, w_in, w_out):
    n_mp, n_tok = lax.axis_size("mp"), lax.axis_size("tokens")
    chips = n_mp // 2
    scale_back = 1.0 / math.sqrt(pre_act.shape[0] * n_tok)

    *pieces, own_piece, pre_act, own_grad = pack(tokens_in, grad_out, pre_act, n_tok, lead())
    rows_grad = [fetch_chip(grad_out, k) for k in range(1, chips)]
    cols = sort([own_piece] + [fetch(x, "tokens", k) for k, x in enumerate(pieces, 1)])
    cols_chips = [fetch_chip(cols, k) for k in range(1, chips)]

    own_rows = join([own_grad, *rows_grad], cols)
    other_rows = other_core(own_rows)
    own_cols = stack([cols, *cols_chips])
    other_cols = other_core(own_cols)
    pre = [fetch(pre_act, "tokens", k) for k in range(1, n_tok)]

    grad_pre = grad_pre_of(own_rows, other_rows, pre_act, w_out, own_cols)
    grad_pre_all = [grad_pre] + [fetch(grad_pre, "tokens", k) for k in range(1, n_tok)]
    terms = lax.all_to_all(grad_in_part(grad_pre, w_in.T, n_mp, pre), "mp", 0, 0)
    grad_w_in_t, grad_w_out, end = grad_w_of(
        [pre_act] + pre, grad_pre_all, own_cols, other_cols, scale_back
    )
    return (finish(terms, end), grad_w_in_t.T, grad_w_out)


def solution(mesh):
    placed = (
        P(("tokens", "mp"), None),
        P(("tokens", "mp"), None),
        P("tokens", "mp"),
        P(None, "mp"),
        P("mp", None),
    )
    return jax.shard_map(
        shards,
        mesh=mesh,
        in_specs=placed,
        out_specs=(P(("tokens", "mp"), None), P("tokens", "mp"), P("mp", "tokens")),
        check_vma=False,
    )
```

```python
import functools
import math

import jax
import jax.numpy as jnp
from jax import lax
from jax.experimental import pallas as pl
from jax.experimental.pallas import tpu as pltpu
from jax.sharding import PartitionSpec as P

root_two_pi = math.sqrt(2.0 / math.pi)
cubic = 0.044715


def gelu_value(pre):
    inner = root_two_pi * (pre + cubic * pre * pre * pre)
    return 0.5 * pre * (1.0 + jnp.tanh(inner))


def gelu_slope(pre):
    tanh_val = jnp.tanh(root_two_pi * (pre + cubic * pre * pre * pre))
    return 0.5 * (1.0 + tanh_val) + 0.5 * pre * (1.0 - tanh_val * tanh_val) * root_two_pi * (
        1.0 + 3.0 * cubic * pre * pre
    )


def partner(i, k, n):
    if n & (n - 1) == 0:
        return i ^ k
    return (i + k) % n if isinstance(i, int) else lax.rem(i + k, n)


def fetch(x, axis, k):
    n = lax.axis_size(axis)
    return lax.ppermute(x, axis, [(partner(i, k, n), i) for i in range(n)])


def other_core(x):
    return lax.ppermute(x, "mp", [(i ^ 1, i) for i in range(lax.axis_size("mp"))])


def chip_pairs(k):
    n = lax.axis_size("mp")
    return [(i, partner(i // 2, k, n // 2) * 2 + i % 2) for i in range(n)]


def fetch_chip(x, k):
    return lax.ppermute(x, "mp", [(there, here) for here, there in chip_pairs(k)])


def give_chip(x, k):
    return lax.ppermute(x, "mp", chip_pairs(k))


def block_of(size, most, unit):
    return max([b for b in range(unit, most + 1, unit) if size % b == 0], default=size)


def call(body, shapes, args, name, scratch=(), limit=8, flops=10**6, bytes_accessed=10**5,
         in_space=pltpu.VMEM, out_spaces=None):
    return pl.pallas_call(
        body,
        in_specs=[pl.BlockSpec(memory_space=in_space)] * len(args),
        out_specs=[
            pl.BlockSpec(memory_space=space) for space in out_spaces or [pltpu.VMEM] * len(shapes)
        ],
        out_shape=[jax.ShapeDtypeStruct(*shape) for shape in shapes],
        scratch_shapes=list(scratch),
        compiler_params=pltpu.CompilerParams(vmem_limit_bytes=limit << 20),
        cost_estimate=pl.CostEstimate(
            flops=flops, bytes_accessed=bytes_accessed, transcendentals=0
        ),
        name=name,
    )(*args)


def place_of(block, chips):
    m = lax.axis_index("mp")
    core, k = divmod(block, chips)
    return 2 * partner(lax.shift_right_logical(m, 1), k, chips) + ((m & 1) ^ core)


def lead_body(out):
    out[...] = jnp.zeros_like(out)


def lead():
    return call(
        lead_body, [((8, 128), jnp.float32)], [], "lead", flops=10**10, bytes_accessed=36 * 10**6
    )[0]


def pack_body(tokens_in, grad_in, pre_in, after, *refs):
    *pieces, own, pre_ref, grad_ref, slabs, tokens_ref, sems = refs
    copies = [
        pltpu.make_async_copy(source, target, sems.at[i])
        for i, (source, target) in enumerate(
            ((tokens_in, tokens_ref), (grad_in, grad_ref), (pre_in, pre_ref))
        )
    ]
    for copy in copies:
        copy.start()
    for copy in copies:
        copy.wait()
    places, rows, part = slabs.shape
    both = jnp.concatenate(
        [tokens_ref[...].astype(jnp.float32), grad_ref[...].astype(jnp.float32)], axis=0
    )
    for p in range(places):
        slabs[p] = both[:, p * part : (p + 1) * part]
    t = lax.axis_index("tokens")
    own[...] = slabs[t].astype(jnp.bfloat16)
    for k, ref in enumerate(pieces, 1):
        taker = t ^ k if places & (places - 1) == 0 else lax.rem(t - k + places, places)
        ref[...] = slabs[taker].astype(jnp.bfloat16)


def pack(tokens_in, grad_out, pre_act, n_tok, after):
    rows, width = tokens_in.shape
    part = width // n_tok
    shapes = [(2 * rows, part)] * n_tok + [pre_act.shape, grad_out.shape]
    return call(
        pack_body,
        [(shape, jnp.bfloat16) for shape in shapes],
        [tokens_in, grad_out, pre_act, after],
        "pack",
        [
            pltpu.VMEM((n_tok, 2 * rows, part), jnp.float32),
            pltpu.VMEM(tokens_in.shape, jnp.bfloat16),
            pltpu.SemaphoreType.DMA((3,)),
        ],
        flops=10**10,
        bytes_accessed=36 * 10**6,
        in_space=pltpu.HBM,
    )


def join_body(*refs):
    *pieces, out = refs
    out[...] = jnp.concatenate([x[...].astype(jnp.float32) for x in pieces], axis=0).astype(
        jnp.bfloat16
    )


def join(pieces):
    shape = (sum(x.shape[0] for x in pieces), pieces[0].shape[1])
    return call(join_body, [(shape, jnp.bfloat16)], pieces, "join")[0]


def sort_body(count, *refs):
    pieces, out = refs[:count], refs[-1]
    rows = pieces[0].shape[0] // 2
    pieces = [x[...].astype(jnp.float32) for x in pieces]
    for a in range(2):
        out[a] = jnp.concatenate([x[a * rows : (a + 1) * rows] for x in pieces], axis=0).astype(
            jnp.bfloat16
        )


def sort(pieces, after):
    rows, part = pieces[0].shape
    shape = (2, rows // 2 * len(pieces), part)
    body = functools.partial(sort_body, len(pieces))
    return call(body, [(shape, jnp.bfloat16)], [*pieces, *after], "sort")[0]


def stack_body(count, *refs):
    pieces, out = refs[:count], refs[-1]
    for k, x in enumerate(pieces):
        out[k] = x[...]


def stack(pieces, after=()):
    shape = (len(pieces),) + pieces[0].shape
    body = functools.partial(stack_body, len(pieces))
    return call(body, [(shape, jnp.bfloat16)], [*pieces, *after], "stack")[0]


def pile_body(low, high, out):
    count = low.shape[0]
    out[:count] = low[...]
    out[count:] = high[...]


def spread(x, masks):
    held, got, order = stack([x]), [], [0]
    where = {}
    n = lax.axis_size("tokens")
    for mask in masks:
        if got:
            shape = (2 * held.shape[0],) + held.shape[1:]
            held = call(pile_body, [(shape, jnp.bfloat16)], [held, got[-1]], "pile")[0]
        got.append(lax.ppermute(held, "tokens", [(i ^ mask, i) for i in range(n)]))
        for j, k in enumerate(order):
            where[k ^ mask] = (len(got), j)
        order = order + [k ^ mask for k in order]
    return held, got, where


def grad_pre_body(block, own_ref, other_ref, pre_ref, w_ref, out_ref, rows, total):
    hidden, group = total.shape
    half = own_ref.shape[0]
    rows[:half, :] = own_ref[...]
    rows[half:, :] = other_ref[...]
    for low in range(0, hidden, block):
        here = slice(low, low + block)
        total[here, :] = lax.dot_general(
            w_ref[here, :], rows[...], (((1,), (1,)), ((), ())), preferred_element_type=jnp.float32
        )
    each = group // lax.axis_size("mp")
    chips = half // each
    row = lax.broadcasted_iota(jnp.int32, (group, 1), 0)
    from_row = row
    for b in range(group // each):
        inside = (row >= b * each) & (row < (b + 1) * each)
        from_row = jnp.where(inside, row + (place_of(b, chips) - b) * each, from_row)
    pick = from_row == lax.broadcasted_iota(jnp.int32, (group, group), 1)
    pre = jnp.dot(
        pick.astype(jnp.float32).astype(jnp.bfloat16), pre_ref[...], preferred_element_type=jnp.float32
    )
    out_ref[...] = (total[...].T * gelu_slope(pre)).astype(jnp.bfloat16)


def grad_pre_of(own, other, pre_act, w_out):
    group, hidden = pre_act.shape
    width = w_out.shape[1]
    return call(
        functools.partial(grad_pre_body, block_of(hidden, 432, 16)),
        [((group, hidden), jnp.bfloat16)],
        [own, other, pre_act, w_out],
        "grad_pre",
        [pltpu.VMEM((group, width), jnp.bfloat16), pltpu.VMEM((hidden, group), jnp.float32)],
        flops=2 * group * width * hidden,
        bytes_accessed=2 * hidden * width,
    )[0]


def grad_in_body(block, grad_pre_ref, w_ref, *refs):
    out_ref = refs[-1]
    places, rows, width = out_ref.shape
    for low in range(0, width, block):
        here = slice(low, low + block)
        term = jnp.dot(grad_pre_ref[...], w_ref[:, here], preferred_element_type=jnp.float32)
        for b in range(places):
            out_ref[place_of(b, places // 2), :, here] = term[b * rows : (b + 1) * rows].astype(
                jnp.bfloat16
            )


def grad_in_part(grad_pre, w_in_t, places, after):
    group, hidden = grad_pre.shape
    width = w_in_t.shape[1]
    return call(
        functools.partial(grad_in_body, block_of(width, 1024, 128)),
        [((places, group // places, width), jnp.bfloat16)],
        [grad_pre, w_in_t, *after],
        "grad_in_part",
        flops=2 * group * width * hidden,
        bytes_accessed=2 * hidden * width,
    )[0]


def finish_body(terms_ref, after, out):
    total = terms_ref[0].astype(jnp.float32)
    for k in range(1, terms_ref.shape[0]):
        total = total + terms_ref[k].astype(jnp.float32)
    out[...] = total.astype(jnp.bfloat16)


def finish(terms, after):
    return call(finish_body, [(terms.shape[1:], jnp.bfloat16)], [terms, after], "finish")[0]


def turn(x_ref, to_ref, unit):
    hidden = x_ref.shape[1]
    for low in range(0, hidden, unit):
        size = min(unit, hidden - low)
        eye = lax.broadcasted_iota(jnp.int32, (size, size), 0) == lax.broadcasted_iota(
            jnp.int32, (size, size), 1
        )
        to_ref[low : low + size, :] = lax.dot_general(
            eye.astype(jnp.float32).astype(jnp.bfloat16),
            x_ref[:, low : low + size],
            (((1,), (1,)), ((), ())),
            preferred_element_type=jnp.float32,
        ).astype(jnp.bfloat16)


def grad_w_body(places, arrays, where, scale_back, block, *refs):
    pre_refs, grad_pre_refs = refs[:arrays], refs[arrays : arrays + places]
    own_ref, other_ref, in_ref, out_ref, end_ref = refs[arrays + places : arrays + places + 5]
    flat, sorted_rows, turned, held_in, held_out, sems = refs[arrays + places + 5 :]
    end_ref[...] = jnp.zeros_like(end_ref)
    group, hidden = grad_pre_refs[0].shape
    chips, _, each, part = own_ref.shape
    rows = each // places
    total = places * group
    copies = []

    def arrange(place):
        size = block_of(total, 128, each)
        for low in range(0, total, size):
            row = low + lax.broadcasted_iota(jnp.int32, (size, 1), 0)
            from_row = row
            for b in range(low // each, (low + size) // each):
                for k in range(places):
                    first = b * each + k * rows
                    inside = (row >= first) & (row < first + rows)
                    shift = k * group + place(b) * rows - first
                    from_row = jnp.where(inside, row + shift, from_row)
            pick = from_row == lax.broadcasted_iota(jnp.int32, (size, total), 1)
            sorted_rows[low : low + size, :] = jnp.dot(
                pick.astype(jnp.float32).astype(jnp.bfloat16),
                flat[...],
                preferred_element_type=jnp.float32,
            ).astype(jnp.bfloat16)
        turn(sorted_rows, turned, 256)

    def product(right, held, to_ref):
        for low in range(0, part, block):
            here = slice(low, low + block)
            cols = jnp.concatenate(
                [ref[k, right, :, here] for ref in (own_ref, other_ref) for k in range(chips)], axis=0
            )
            term = jnp.dot(turned[...], cols, preferred_element_type=jnp.float32)
            held[:, here] = (term * scale_back).astype(jnp.bfloat16)
            copies.append(
                pltpu.make_async_copy(held.at[:, here], to_ref.at[:, here], sems.at[len(copies)])
            )
            copies[-1].start()

    for k in range(places):
        array, j = where[k]
        pre = (pre_refs[array][j] if array else pre_refs[0][...]).astype(jnp.float32)
        flat[k * group : (k + 1) * group, :] = gelu_value(pre).astype(jnp.bfloat16)
    arrange(lambda b: place_of(b, chips))
    product(1, held_out, out_ref)
    for k in range(places):
        flat[k * group : (k + 1) * group, :] = grad_pre_refs[k][...]
    arrange(lambda b: b)
    product(0, held_in, in_ref)
    for copy in copies:
        copy.wait()


def grad_w_of(pre, where, grad_pre, own, other, scale_back):
    places = len(grad_pre)
    group, hidden = grad_pre[0].shape
    total, part = places * group, own.shape[3]
    block = block_of(part, 256, 128)
    return call(
        functools.partial(grad_w_body, places, len(pre), where, scale_back, block),
        [((hidden, part), jnp.bfloat16)] * 2 + [((8, 128), jnp.float32)],
        [*pre, *grad_pre, own, other],
        "grad_w",
        [
            pltpu.VMEM((total, hidden), jnp.bfloat16),
            pltpu.VMEM((total, hidden), jnp.bfloat16),
            pltpu.VMEM((hidden, total), jnp.bfloat16),
            pltpu.VMEM((hidden, part), jnp.bfloat16),
            pltpu.VMEM((hidden, part), jnp.bfloat16),
            pltpu.SemaphoreType.DMA((2 * (part // block),)),
        ],
        limit=20,
        flops=80 * total * part * hidden,
        bytes_accessed=40 * hidden * part,
        out_spaces=[pltpu.HBM, pltpu.HBM, pltpu.VMEM],
    )


def shards(tokens_in, grad_out, pre_act, w_in, w_out):
    n_mp, n_tok = lax.axis_size("mp"), lax.axis_size("tokens")
    chips = n_mp // 2
    scale_back = 1.0 / math.sqrt(pre_act.shape[0] * n_tok)

    *pieces, own_piece, pre_act, own_grad = pack(tokens_in, grad_out, pre_act, n_tok, lead())
    own_rows = join([own_grad] + [fetch_chip(grad_out, k) for k in range(1, chips)])
    other_rows = other_core(own_rows)
    masks = (3, 1) if n_tok == 4 else [1 << i for i in range(n_tok.bit_length() - 1)]
    held, pre, where = spread(pre_act, masks)
    where[0] = (0, 0)
    pieces = [fetch(x, "tokens", k) for k, x in enumerate(pieces, 1)]
    grad_pre = grad_pre_of(own_rows, other_rows, pre_act, w_out)
    cols = sort([own_piece, *pieces], [grad_pre])
    own_cols = stack([cols] + [fetch_chip(cols, k) for k in range(1, chips)])
    other_cols = other_core(own_cols)
    grad_pre_all = [grad_pre] + [fetch(grad_pre, "tokens", k) for k in range(1, n_tok)]
    terms = lax.all_to_all(grad_in_part(grad_pre, w_in.T, n_mp, [pre[-1]]), "mp", 0, 0)
    grad_w_in_t, grad_w_out, end = grad_w_of(
        [pre_act, *pre], where, grad_pre_all, own_cols, other_cols, scale_back
    )
    return (finish(terms, end), grad_w_in_t.T, grad_w_out)


def solution(mesh):
    placed = (
        P(("tokens", "mp"), None),
        P(("tokens", "mp"), None),
        P("tokens", "mp"),
        P(None, "mp"),
        P("mp", None),
    )
    return jax.shard_map(
        shards,
        mesh=mesh,
        in_specs=placed,
        out_specs=(P(("tokens", "mp"), None), P("tokens", "mp"), P("mp", "tokens")),
        check_vma=False,
    )
```

```python
import functools
import math

import jax
import jax.numpy as jnp
from jax import lax
from jax.experimental import pallas as pl
from jax.experimental.pallas import tpu as pltpu
from jax.sharding import PartitionSpec as P

root_two_pi = math.sqrt(2.0 / math.pi)
cubic = 0.044715


def gelu_value(pre):
    inner = root_two_pi * (pre + cubic * pre * pre * pre)
    return 0.5 * pre * (1.0 + jnp.tanh(inner))


def gelu_slope(pre):
    tanh_val = jnp.tanh(root_two_pi * (pre + cubic * pre * pre * pre))
    return 0.5 * (1.0 + tanh_val) + 0.5 * pre * (1.0 - tanh_val * tanh_val) * root_two_pi * (
        1.0 + 3.0 * cubic * pre * pre
    )


def partner(i, k, n):
    if n & (n - 1) == 0:
        return i ^ k
    return (i + k) % n if isinstance(i, int) else lax.rem(i + k, n)


def fetch(x, axis, k):
    n = lax.axis_size(axis)
    return lax.ppermute(x, axis, [(partner(i, k, n), i) for i in range(n)])


def other_core(x):
    return lax.ppermute(x, "mp", [(i ^ 1, i) for i in range(lax.axis_size("mp"))])


def chip_pairs(k):
    n = lax.axis_size("mp")
    return [(i, partner(i // 2, k, n // 2) * 2 + i % 2) for i in range(n)]


def fetch_chip(x, k):
    return lax.ppermute(x, "mp", [(there, here) for here, there in chip_pairs(k)])


def give_chip(x, k):
    return lax.ppermute(x, "mp", chip_pairs(k))


def block_of(size, most, unit):
    return max([b for b in range(unit, most + 1, unit) if size % b == 0], default=size)


def call(body, shapes, args, name, scratch=(), limit=8, flops=10**6, bytes_accessed=10**5,
         in_space=pltpu.VMEM, out_spaces=None):
    return pl.pallas_call(
        body,
        in_specs=[pl.BlockSpec(memory_space=in_space)] * len(args),
        out_specs=[
            pl.BlockSpec(memory_space=space) for space in out_spaces or [pltpu.VMEM] * len(shapes)
        ],
        out_shape=[jax.ShapeDtypeStruct(*shape) for shape in shapes],
        scratch_shapes=list(scratch),
        compiler_params=pltpu.CompilerParams(vmem_limit_bytes=limit << 20),
        cost_estimate=pl.CostEstimate(
            flops=flops, bytes_accessed=bytes_accessed, transcendentals=0
        ),
        name=name,
    )(*args)


def place_of(block, chips):
    m = lax.axis_index("mp")
    core, k = divmod(block, chips)
    return 2 * partner(lax.shift_right_logical(m, 1), k, chips) + ((m & 1) ^ core)


def lead_body(out):
    out[...] = jnp.zeros_like(out)


def lead():
    return call(
        lead_body, [((8, 128), jnp.float32)], [], "lead", flops=10**10, bytes_accessed=36 * 10**6
    )[0]


def pack_body(tokens_in, grad_in, pre_in, after, *refs):
    *pieces, own, pre_ref, grad_ref, slabs, tokens_ref, sems = refs
    copies = [
        pltpu.make_async_copy(source, target, sems.at[i])
        for i, (source, target) in enumerate(
            ((tokens_in, tokens_ref), (grad_in, grad_ref), (pre_in, pre_ref))
        )
    ]
    for copy in copies:
        copy.start()
    for copy in copies:
        copy.wait()
    places, rows, part = slabs.shape
    both = jnp.concatenate(
        [tokens_ref[...].astype(jnp.float32), grad_ref[...].astype(jnp.float32)], axis=0
    )
    for p in range(places):
        slabs[p] = both[:, p * part : (p + 1) * part]
    t = lax.axis_index("tokens")
    own[...] = slabs[t].astype(jnp.bfloat16)
    for k, ref in enumerate(pieces, 1):
        taker = t ^ k if places & (places - 1) == 0 else lax.rem(t - k + places, places)
        ref[...] = slabs[taker].astype(jnp.bfloat16)


def pack(tokens_in, grad_out, pre_act, n_tok, after):
    rows, width = tokens_in.shape
    part = width // n_tok
    shapes = [(2 * rows, part)] * n_tok + [pre_act.shape, grad_out.shape]
    return call(
        pack_body,
        [(shape, jnp.bfloat16) for shape in shapes],
        [tokens_in, grad_out, pre_act, after],
        "pack",
        [
            pltpu.VMEM((n_tok, 2 * rows, part), jnp.float32),
            pltpu.VMEM(tokens_in.shape, jnp.bfloat16),
            pltpu.SemaphoreType.DMA((3,)),
        ],
        flops=10**10,
        bytes_accessed=36 * 10**6,
        in_space=pltpu.HBM,
    )


def join_body(after, *refs):
    *pieces, out = refs
    out[...] = jnp.concatenate([x[...].astype(jnp.float32) for x in pieces], axis=0).astype(
        jnp.bfloat16
    )


def join(pieces, after):
    shape = (sum(x.shape[0] for x in pieces), pieces[0].shape[1])
    return call(join_body, [(shape, jnp.bfloat16)], [after, *pieces], "join")[0]


def sort_body(count, *refs):
    pieces, out = refs[:count], refs[-1]
    rows = pieces[0].shape[0] // 2
    pieces = [x[...].astype(jnp.float32) for x in pieces]
    for a in range(2):
        out[a] = jnp.concatenate([x[a * rows : (a + 1) * rows] for x in pieces], axis=0).astype(
            jnp.bfloat16
        )


def sort(pieces, after):
    rows, part = pieces[0].shape
    shape = (2, rows // 2 * len(pieces), part)
    body = functools.partial(sort_body, len(pieces))
    return call(body, [(shape, jnp.bfloat16)], [*pieces, *after], "sort")[0]


def stack_body(count, *refs):
    pieces, out = refs[:count], refs[-1]
    for k, x in enumerate(pieces):
        out[k] = x[...]


def stack(pieces, after=()):
    shape = (len(pieces),) + pieces[0].shape
    body = functools.partial(stack_body, len(pieces))
    return call(body, [(shape, jnp.bfloat16)], [*pieces, *after], "stack")[0]


def pile_body(low, high, out):
    count = out.shape[0] // 2
    if count == 1:
        out[0] = low[...]
        out[1] = high[...]
    else:
        out[:count] = low[...]
        out[count:] = high[...]


def spread(x, masks):
    held, got, order, where = x, [], [0], {0: (0, 0)}
    n = lax.axis_size("tokens")
    for mask in masks:
        if got:
            shape = (len(order),) + x.shape
            held = call(pile_body, [(shape, jnp.bfloat16)], [held, got[-1]], "pile")[0]
        got.append(lax.ppermute(held, "tokens", [(i ^ mask, i) for i in range(n)]))
        for j, k in enumerate(order):
            where[k ^ mask] = (len(got), j)
        order = order + [k ^ mask for k in order]
    return held, got, where


def grad_pre_body(block, own_ref, other_ref, pre_ref, w_ref, out_ref, rows, total):
    hidden, group = total.shape
    half = own_ref.shape[0]
    rows[:half, :] = own_ref[...]
    rows[half:, :] = other_ref[...]
    for low in range(0, hidden, block):
        here = slice(low, low + block)
        total[here, :] = lax.dot_general(
            w_ref[here, :], rows[...], (((1,), (1,)), ((), ())), preferred_element_type=jnp.float32
        )
    each = group // lax.axis_size("mp")
    chips = half // each
    row = lax.broadcasted_iota(jnp.int32, (group, 1), 0)
    from_row = row
    for b in range(group // each):
        inside = (row >= b * each) & (row < (b + 1) * each)
        from_row = jnp.where(inside, row + (place_of(b, chips) - b) * each, from_row)
    pick = from_row == lax.broadcasted_iota(jnp.int32, (group, group), 1)
    pre = jnp.dot(
        pick.astype(jnp.float32).astype(jnp.bfloat16), pre_ref[...], preferred_element_type=jnp.float32
    )
    out_ref[...] = (total[...].T * gelu_slope(pre)).astype(jnp.bfloat16)


def grad_pre_of(own, other, pre_act, w_out):
    group, hidden = pre_act.shape
    width = w_out.shape[1]
    return call(
        functools.partial(grad_pre_body, block_of(hidden, 432, 16)),
        [((group, hidden), jnp.bfloat16)],
        [own, other, pre_act, w_out],
        "grad_pre",
        [pltpu.VMEM((group, width), jnp.bfloat16), pltpu.VMEM((hidden, group), jnp.float32)],
        flops=2 * group * width * hidden,
        bytes_accessed=2 * hidden * width,
    )[0]


def grad_in_body(block, grad_pre_ref, w_ref, *refs):
    out_ref = refs[-1]
    places, rows, width = out_ref.shape
    for low in range(0, width, block):
        here = slice(low, low + block)
        term = jnp.dot(grad_pre_ref[...], w_ref[:, here], preferred_element_type=jnp.float32)
        for b in range(places):
            out_ref[place_of(b, places // 2), :, here] = term[b * rows : (b + 1) * rows].astype(
                jnp.bfloat16
            )


def grad_in_part(grad_pre, w_in_t, places, after):
    group, hidden = grad_pre.shape
    width = w_in_t.shape[1]
    return call(
        functools.partial(grad_in_body, block_of(width, 1024, 128)),
        [((places, group // places, width), jnp.bfloat16)],
        [grad_pre, w_in_t, *after],
        "grad_in_part",
        flops=2 * group * width * hidden,
        bytes_accessed=2 * hidden * width,
    )[0]


def finish_body(terms_ref, after, out):
    total = terms_ref[0].astype(jnp.float32)
    for k in range(1, terms_ref.shape[0]):
        total = total + terms_ref[k].astype(jnp.float32)
    out[...] = total.astype(jnp.bfloat16)


def finish(terms, after):
    return call(finish_body, [(terms.shape[1:], jnp.bfloat16)], [terms, after], "finish")[0]


def turn(x_ref, to_ref, unit):
    hidden = x_ref.shape[1]
    for low in range(0, hidden, unit):
        size = min(unit, hidden - low)
        eye = lax.broadcasted_iota(jnp.int32, (size, size), 0) == lax.broadcasted_iota(
            jnp.int32, (size, size), 1
        )
        to_ref[low : low + size, :] = lax.dot_general(
            eye.astype(jnp.float32).astype(jnp.bfloat16),
            x_ref[:, low : low + size],
            (((1,), (1,)), ((), ())),
            preferred_element_type=jnp.float32,
        ).astype(jnp.bfloat16)


def grad_w_body(places, arrays, where, scale_back, block, *refs):
    pre_refs, grad_pre_refs = refs[:arrays], refs[arrays : arrays + places]
    own_ref, other_ref, in_ref, out_ref, end_ref = refs[arrays + places : arrays + places + 5]
    flat, sorted_rows, turned, held_in, held_out, sems = refs[arrays + places + 5 :]
    end_ref[...] = jnp.zeros_like(end_ref)
    group, hidden = grad_pre_refs[0].shape
    chips, _, each, part = own_ref.shape
    rows = each // places
    total = places * group
    copies = []

    def arrange(place):
        size = block_of(total, 128, each)
        for low in range(0, total, size):
            row = low + lax.broadcasted_iota(jnp.int32, (size, 1), 0)
            from_row = row
            for b in range(low // each, (low + size) // each):
                for k in range(places):
                    first = b * each + k * rows
                    inside = (row >= first) & (row < first + rows)
                    shift = k * group + place(b) * rows - first
                    from_row = jnp.where(inside, row + shift, from_row)
            pick = from_row == lax.broadcasted_iota(jnp.int32, (size, total), 1)
            sorted_rows[low : low + size, :] = jnp.dot(
                pick.astype(jnp.float32).astype(jnp.bfloat16),
                flat[...],
                preferred_element_type=jnp.float32,
            ).astype(jnp.bfloat16)
        turn(sorted_rows, turned, 256)

    def product(right, held, to_ref):
        for low in range(0, part, block):
            here = slice(low, low + block)
            cols = jnp.concatenate(
                [ref[k, right, :, here] for ref in (own_ref, other_ref) for k in range(chips)], axis=0
            )
            term = jnp.dot(turned[...], cols, preferred_element_type=jnp.float32)
            held[:, here] = (term * scale_back).astype(jnp.bfloat16)
            copies.append(
                pltpu.make_async_copy(held.at[:, here], to_ref.at[:, here], sems.at[len(copies)])
            )
            copies[-1].start()

    for k in range(places):
        array, j = where[k]
        ref = pre_refs[array]
        pre = (ref[...] if len(ref.shape) == 2 else ref[j]).astype(jnp.float32)
        flat[k * group : (k + 1) * group, :] = gelu_value(pre).astype(jnp.bfloat16)
    arrange(lambda b: place_of(b, chips))
    product(1, held_out, out_ref)
    for k in range(places):
        flat[k * group : (k + 1) * group, :] = grad_pre_refs[k][...]
    arrange(lambda b: b)
    product(0, held_in, in_ref)
    for copy in copies:
        copy.wait()


def grad_w_of(pre, where, grad_pre, own, other, scale_back):
    places = len(grad_pre)
    group, hidden = grad_pre[0].shape
    total, part = places * group, own.shape[3]
    block = block_of(part, 256, 128)
    return call(
        functools.partial(grad_w_body, places, len(pre), where, scale_back, block),
        [((hidden, part), jnp.bfloat16)] * 2 + [((8, 128), jnp.float32)],
        [*pre, *grad_pre, own, other],
        "grad_w",
        [
            pltpu.VMEM((total, hidden), jnp.bfloat16),
            pltpu.VMEM((total, hidden), jnp.bfloat16),
            pltpu.VMEM((hidden, total), jnp.bfloat16),
            pltpu.VMEM((hidden, part), jnp.bfloat16),
            pltpu.VMEM((hidden, part), jnp.bfloat16),
            pltpu.SemaphoreType.DMA((2 * (part // block),)),
        ],
        limit=20,
        flops=80 * total * part * hidden,
        bytes_accessed=40 * hidden * part,
        out_spaces=[pltpu.HBM, pltpu.HBM, pltpu.VMEM],
    )


def shards(tokens_in, grad_out, pre_act, w_in, w_out):
    n_mp, n_tok = lax.axis_size("mp"), lax.axis_size("tokens")
    chips = n_mp // 2
    scale_back = 1.0 / math.sqrt(pre_act.shape[0] * n_tok)

    masks = (3, 1) if n_tok == 4 else [1 << i for i in range(n_tok.bit_length() - 1)]
    held, pre, where = spread(pre_act, masks)
    *pieces, own_piece, pre_act, own_grad = pack(tokens_in, grad_out, pre_act, n_tok, lead())
    own_rows = join([own_grad] + [fetch_chip(grad_out, k) for k in range(1, chips)], held)
    other_rows = other_core(own_rows)
    pieces = [fetch(x, "tokens", k) for k, x in enumerate(pieces, 1)]
    grad_pre = grad_pre_of(own_rows, other_rows, pre_act, w_out)
    cols = sort([own_piece, *pieces], [grad_pre])
    own_cols = stack([cols] + [fetch_chip(cols, k) for k in range(1, chips)])
    other_cols = other_core(own_cols)
    grad_pre_all = [grad_pre] + [fetch(grad_pre, "tokens", k) for k in range(1, n_tok)]
    terms = lax.all_to_all(grad_in_part(grad_pre, w_in.T, n_mp, []), "mp", 0, 0)
    grad_w_in_t, grad_w_out, end = grad_w_of(
        [pre_act, *pre], where, grad_pre_all, own_cols, other_cols, scale_back
    )
    return (finish(terms, end), grad_w_in_t.T, grad_w_out)


def solution(mesh):
    placed = (
        P(("tokens", "mp"), None),
        P(("tokens", "mp"), None),
        P("tokens", "mp"),
        P(None, "mp"),
        P("mp", None),
    )
    return jax.shard_map(
        shards,
        mesh=mesh,
        in_specs=placed,
        out_specs=(P(("tokens", "mp"), None), P("tokens", "mp"), P("mp", "tokens")),
        check_vma=False,
    )
```

```python
import functools
import math

import jax
import jax.numpy as jnp
from jax import lax
from jax.experimental import pallas as pl
from jax.experimental.pallas import tpu as pltpu
from jax.sharding import PartitionSpec as P

root_two_pi = math.sqrt(2.0 / math.pi)
cubic = 0.044715


def gelu_value(pre):
    inner = root_two_pi * (pre + cubic * pre * pre * pre)
    return 0.5 * pre * (1.0 + jnp.tanh(inner))


def gelu_slope(pre):
    tanh_val = jnp.tanh(root_two_pi * (pre + cubic * pre * pre * pre))
    return 0.5 * (1.0 + tanh_val) + 0.5 * pre * (1.0 - tanh_val * tanh_val) * root_two_pi * (
        1.0 + 3.0 * cubic * pre * pre
    )


def partner(i, k, n):
    if n & (n - 1) == 0:
        return i ^ k
    return (i + k) % n if isinstance(i, int) else lax.rem(i + k, n)


def fetch(x, axis, k):
    n = lax.axis_size(axis)
    return lax.ppermute(x, axis, [(partner(i, k, n), i) for i in range(n)])


def other_core(x):
    return lax.ppermute(x, "mp", [(i ^ 1, i) for i in range(lax.axis_size("mp"))])


def chip_pairs(k):
    n = lax.axis_size("mp")
    return [(i, partner(i // 2, k, n // 2) * 2 + i % 2) for i in range(n)]


def fetch_chip(x, k):
    return lax.ppermute(x, "mp", [(there, here) for here, there in chip_pairs(k)])


def give_chip(x, k):
    return lax.ppermute(x, "mp", chip_pairs(k))


def block_of(size, most, unit):
    return max([b for b in range(unit, most + 1, unit) if size % b == 0], default=size)


def call(body, shapes, args, name, scratch=(), limit=8, flops=10**6, bytes_accessed=10**5,
         in_space=pltpu.VMEM, out_spaces=None):
    return pl.pallas_call(
        body,
        in_specs=[pl.BlockSpec(memory_space=in_space)] * len(args),
        out_specs=[
            pl.BlockSpec(memory_space=space) for space in out_spaces or [pltpu.VMEM] * len(shapes)
        ],
        out_shape=[jax.ShapeDtypeStruct(*shape) for shape in shapes],
        scratch_shapes=list(scratch),
        compiler_params=pltpu.CompilerParams(vmem_limit_bytes=limit << 20),
        cost_estimate=pl.CostEstimate(
            flops=flops, bytes_accessed=bytes_accessed, transcendentals=0
        ),
        name=name,
    )(*args)


def place_of(block, chips):
    m = lax.axis_index("mp")
    core, k = divmod(block, chips)
    return 2 * partner(lax.shift_right_logical(m, 1), k, chips) + ((m & 1) ^ core)


def lead_body(out):
    out[...] = jnp.zeros_like(out)


def lead():
    return call(
        lead_body, [((8, 128), jnp.float32)], [], "lead", flops=10**10, bytes_accessed=36 * 10**6
    )[0]


def pack_body(tokens_in, grad_in, pre_in, after, both, pre_ref, tokens_ref, grad_ref, sems):
    copies = [
        pltpu.make_async_copy(source, target, sems.at[i])
        for i, (source, target) in enumerate(
            ((tokens_in, tokens_ref), (grad_in, grad_ref), (pre_in, pre_ref))
        )
    ]
    for copy in copies:
        copy.start()
    for copy in copies:
        copy.wait()
    both[...] = jnp.concatenate(
        [tokens_ref[...].astype(jnp.float32), grad_ref[...].astype(jnp.float32)], axis=0
    ).astype(jnp.bfloat16)


def pack(tokens_in, grad_out, pre_act, after):
    rows, width = tokens_in.shape
    shapes = [(2 * rows, width), pre_act.shape]
    return call(
        pack_body,
        [(shape, jnp.bfloat16) for shape in shapes],
        [tokens_in, grad_out, pre_act, after],
        "pack",
        [
            pltpu.VMEM(tokens_in.shape, jnp.bfloat16),
            pltpu.VMEM(tokens_in.shape, jnp.bfloat16),
            pltpu.SemaphoreType.DMA((3,)),
        ],
        flops=10**10,
        bytes_accessed=36 * 10**6,
        in_space=pltpu.HBM,
    )


def join_body(count, after, *refs):
    rows_in = refs[:count]
    *pieces, grad_ref, slabs = refs[count:]
    places, _, _, part = slabs.shape
    parts = [x[...].astype(jnp.float32) for x in rows_in]
    each = parts[0].shape[0] // 2
    tokens = jnp.concatenate([x[:each] for x in parts], axis=0)
    grad = jnp.concatenate([x[each:] for x in parts], axis=0)
    grad_ref[...] = grad.astype(jnp.bfloat16)
    for p in range(places):
        here = slice(p * part, (p + 1) * part)
        slabs[p, 0] = tokens[:, here]
        slabs[p, 1] = grad[:, here]
    t = lax.axis_index("tokens")
    for k, ref in enumerate(pieces):
        taker = t ^ k if places & (places - 1) == 0 else lax.rem(t - k + places, places)
        ref[...] = slabs[taker].astype(jnp.bfloat16)


def join(rows_in, n_tok, after):
    count, (both, width) = len(rows_in), rows_in[0].shape
    rows, part = count * both // 2, width // n_tok
    shapes = [(2, rows, part)] * n_tok + [(rows, width)]
    return call(
        functools.partial(join_body, count),
        [(shape, jnp.bfloat16) for shape in shapes],
        [after, *rows_in],
        "join",
        [pltpu.VMEM((n_tok, 2, rows, part), jnp.float32)],
        limit=16,
    )


def stack_body(count, *refs):
    pieces, out = refs[:count], refs[-1]
    for k, x in enumerate(pieces):
        out[k] = x[...]


def stack(pieces, after=()):
    shape = (len(pieces),) + pieces[0].shape
    body = functools.partial(stack_body, len(pieces))
    return call(body, [(shape, jnp.bfloat16)], [*pieces, *after], "stack")[0]


def pile_body(low, high, out):
    count = out.shape[0] // 2
    if count == 1:
        out[0] = low[...]
        out[1] = high[...]
    else:
        out[:count] = low[...]
        out[count:] = high[...]


def spread(x, masks):
    held, got, order, where = x, [], [0], {0: (0, 0)}
    n = lax.axis_size("tokens")
    for mask in masks:
        if got:
            shape = (len(order),) + x.shape
            held = call(pile_body, [(shape, jnp.bfloat16)], [held, got[-1]], "pile")[0]
        got.append(lax.ppermute(held, "tokens", [(i ^ mask, i) for i in range(n)]))
        for j, k in enumerate(order):
            where[k ^ mask] = (len(got), j)
        order = order + [k ^ mask for k in order]
    return held, got, where


def grad_pre_body(block, own_ref, other_ref, pre_ref, w_ref, out_ref, rows, total):
    hidden, group = total.shape
    half = own_ref.shape[0]
    rows[:half, :] = own_ref[...]
    rows[half:, :] = other_ref[...]
    for low in range(0, hidden, block):
        here = slice(low, low + block)
        total[here, :] = lax.dot_general(
            w_ref[here, :], rows[...], (((1,), (1,)), ((), ())), preferred_element_type=jnp.float32
        )
    each = group // lax.axis_size("mp")
    chips = half // each
    row = lax.broadcasted_iota(jnp.int32, (group, 1), 0)
    from_row = row
    for b in range(group // each):
        inside = (row >= b * each) & (row < (b + 1) * each)
        from_row = jnp.where(inside, row + (place_of(b, chips) - b) * each, from_row)
    pick = from_row == lax.broadcasted_iota(jnp.int32, (group, group), 1)
    pre = jnp.dot(
        pick.astype(jnp.float32).astype(jnp.bfloat16), pre_ref[...], preferred_element_type=jnp.float32
    )
    out_ref[...] = (total[...].T * gelu_slope(pre)).astype(jnp.bfloat16)


def grad_pre_of(own, other, pre_act, w_out):
    group, hidden = pre_act.shape
    width = w_out.shape[1]
    return call(
        functools.partial(grad_pre_body, block_of(hidden, 432, 16)),
        [((group, hidden), jnp.bfloat16)],
        [own, other, pre_act, w_out],
        "grad_pre",
        [pltpu.VMEM((group, width), jnp.bfloat16), pltpu.VMEM((hidden, group), jnp.float32)],
        flops=2 * group * width * hidden,
        bytes_accessed=2 * hidden * width,
    )[0]


def grad_in_body(block, grad_pre_ref, w_ref, *refs):
    out_ref = refs[-1]
    places, rows, width = out_ref.shape
    for low in range(0, width, block):
        here = slice(low, low + block)
        term = jnp.dot(grad_pre_ref[...], w_ref[:, here], preferred_element_type=jnp.float32)
        for b in range(places):
            out_ref[place_of(b, places // 2), :, here] = term[b * rows : (b + 1) * rows].astype(
                jnp.bfloat16
            )


def grad_in_part(grad_pre, w_in_t, places, after):
    group, hidden = grad_pre.shape
    width = w_in_t.shape[1]
    return call(
        functools.partial(grad_in_body, block_of(width, 1024, 128)),
        [((places, group // places, width), jnp.bfloat16)],
        [grad_pre, w_in_t, *after],
        "grad_in_part",
        flops=2 * group * width * hidden,
        bytes_accessed=2 * hidden * width,
    )[0]


def finish_body(terms_ref, after, out):
    total = terms_ref[0].astype(jnp.float32)
    for k in range(1, terms_ref.shape[0]):
        total = total + terms_ref[k].astype(jnp.float32)
    out[...] = total.astype(jnp.bfloat16)


def finish(terms, after):
    return call(finish_body, [(terms.shape[1:], jnp.bfloat16)], [terms, after], "finish")[0]


def turn(x_ref, to_ref, unit):
    hidden = x_ref.shape[1]
    for low in range(0, hidden, unit):
        size = min(unit, hidden - low)
        eye = lax.broadcasted_iota(jnp.int32, (size, size), 0) == lax.broadcasted_iota(
            jnp.int32, (size, size), 1
        )
        to_ref[low : low + size, :] = lax.dot_general(
            eye.astype(jnp.float32).astype(jnp.bfloat16),
            x_ref[:, low : low + size],
            (((1,), (1,)), ((), ())),
            preferred_element_type=jnp.float32,
        ).astype(jnp.bfloat16)


def grad_w_body(places, arrays, where, scale_back, block, *refs):
    pre_refs, grad_pre_refs = refs[:arrays], refs[arrays : arrays + places]
    own_ref, other_ref, in_ref, out_ref, end_ref = refs[arrays + places : arrays + places + 5]
    flat, sorted_rows, turned, held_in, held_out, sems = refs[arrays + places + 5 :]
    end_ref[...] = jnp.zeros_like(end_ref)
    group, hidden = grad_pre_refs[0].shape
    part = own_ref.shape[3]
    half, total = group // 2, places * group
    chips = lax.axis_size("mp") // 2
    rows = half // chips
    copies = []

    def arrange(place):
        size = block_of(total, 128, rows)
        blocks = [(core, k, chip) for core in range(2) for k in range(places) for chip in range(chips)]
        for low in range(0, total, size):
            row = low + lax.broadcasted_iota(jnp.int32, (size, 1), 0)
            from_row = row
            for core, k, chip in blocks[low // rows : (low + size) // rows]:
                first = core * places * half + k * half + chip * rows
                inside = (row >= first) & (row < first + rows)
                shift = k * group + place(core * chips + chip) * rows - first
                from_row = jnp.where(inside, row + shift, from_row)
            pick = from_row == lax.broadcasted_iota(jnp.int32, (size, total), 1)
            sorted_rows[low : low + size, :] = jnp.dot(
                pick.astype(jnp.float32).astype(jnp.bfloat16),
                flat[...],
                preferred_element_type=jnp.float32,
            ).astype(jnp.bfloat16)
        turn(sorted_rows, turned, 256)

    def product(right, held, to_ref):
        for low in range(0, part, block):
            here = slice(low, low + block)
            cols = jnp.concatenate(
                [ref[k, right, :, here] for ref in (own_ref, other_ref) for k in range(places)], axis=0
            )
            term = jnp.dot(turned[...], cols, preferred_element_type=jnp.float32)
            held[:, here] = (term * scale_back).astype(jnp.bfloat16)
            copies.append(
                pltpu.make_async_copy(held.at[:, here], to_ref.at[:, here], sems.at[len(copies)])
            )
            copies[-1].start()

    for k in range(places):
        array, j = where[k]
        ref = pre_refs[array]
        pre = (ref[...] if len(ref.shape) == 2 else ref[j]).astype(jnp.float32)
        flat[k * group : (k + 1) * group, :] = gelu_value(pre).astype(jnp.bfloat16)
    arrange(lambda b: place_of(b, chips))
    product(1, held_out, out_ref)
    for k in range(places):
        flat[k * group : (k + 1) * group, :] = grad_pre_refs[k][...]
    arrange(lambda b: b)
    product(0, held_in, in_ref)
    for copy in copies:
        copy.wait()


def grad_w_of(pre, where, grad_pre, own, other, scale_back):
    places = len(grad_pre)
    group, hidden = grad_pre[0].shape
    total, part = places * group, own.shape[3]
    block = block_of(part, 256, 128)
    return call(
        functools.partial(grad_w_body, places, len(pre), where, scale_back, block),
        [((hidden, part), jnp.bfloat16)] * 2 + [((8, 128), jnp.float32)],
        [*pre, *grad_pre, own, other],
        "grad_w",
        [
            pltpu.VMEM((total, hidden), jnp.bfloat16),
            pltpu.VMEM((total, hidden), jnp.bfloat16),
            pltpu.VMEM((hidden, total), jnp.bfloat16),
            pltpu.VMEM((hidden, part), jnp.bfloat16),
            pltpu.VMEM((hidden, part), jnp.bfloat16),
            pltpu.SemaphoreType.DMA((2 * (part // block),)),
        ],
        limit=20,
        flops=80 * total * part * hidden,
        bytes_accessed=40 * hidden * part,
        out_spaces=[pltpu.HBM, pltpu.HBM, pltpu.VMEM],
    )


def shards(tokens_in, grad_out, pre_act, w_in, w_out):
    n_mp, n_tok = lax.axis_size("mp"), lax.axis_size("tokens")
    chips = n_mp // 2
    scale_back = 1.0 / math.sqrt(pre_act.shape[0] * n_tok)

    masks = (3, 1) if n_tok == 4 else [1 << i for i in range(n_tok.bit_length() - 1)]
    held, pre, where = spread(pre_act, masks)
    both, pre_act = pack(tokens_in, grad_out, pre_act, lead())
    *pieces, own_rows = join(
        [both] + [fetch_chip(both, k) for k in range(1, chips)], n_tok, held
    )
    pieces = [x if k == 0 else fetch(x, "tokens", k) for k, x in enumerate(pieces)]

    grad_pre = grad_pre_of(own_rows, other_core(own_rows), pre_act, w_out)
    own_cols = stack(pieces, [grad_pre])
    other_cols = other_core(own_cols)
    grad_pre_all = [grad_pre] + [fetch(grad_pre, "tokens", k) for k in range(1, n_tok)]
    terms = lax.all_to_all(grad_in_part(grad_pre, w_in.T, n_mp, []), "mp", 0, 0)
    grad_w_in_t, grad_w_out, end = grad_w_of(
        [pre_act, *pre], where, grad_pre_all, own_cols, other_cols, scale_back
    )
    return (finish(terms, end), grad_w_in_t.T, grad_w_out)


def solution(mesh):
    placed = (
        P(("tokens", "mp"), None),
        P(("tokens", "mp"), None),
        P("tokens", "mp"),
        P(None, "mp"),
        P("mp", None),
    )
    return jax.shard_map(
        shards,
        mesh=mesh,
        in_specs=placed,
        out_specs=(P(("tokens", "mp"), None), P("tokens", "mp"), P("mp", "tokens")),
        check_vma=False,
    )
```

```python
import functools
import math

import jax
import jax.numpy as jnp
from jax import lax
from jax.experimental import pallas as pl
from jax.experimental.pallas import tpu as pltpu
from jax.sharding import PartitionSpec as P

root_two_pi = math.sqrt(2.0 / math.pi)
cubic = 0.044715


def gelu_value(pre):
    inner = root_two_pi * (pre + cubic * pre * pre * pre)
    return 0.5 * pre * (1.0 + jnp.tanh(inner))


def gelu_slope(pre):
    tanh_val = jnp.tanh(root_two_pi * (pre + cubic * pre * pre * pre))
    return 0.5 * (1.0 + tanh_val) + 0.5 * pre * (1.0 - tanh_val * tanh_val) * root_two_pi * (
        1.0 + 3.0 * cubic * pre * pre
    )


def partner(i, k, n):
    if n & (n - 1) == 0:
        return i ^ k
    return (i + k) % n if isinstance(i, int) else lax.rem(i + k, n)


def fetch(x, axis, k):
    n = lax.axis_size(axis)
    return lax.ppermute(x, axis, [(partner(i, k, n), i) for i in range(n)])


def other_core(x):
    return lax.ppermute(x, "mp", [(i ^ 1, i) for i in range(lax.axis_size("mp"))])


def chip_pairs(k):
    n = lax.axis_size("mp")
    return [(i, partner(i // 2, k, n // 2) * 2 + i % 2) for i in range(n)]


def fetch_chip(x, k):
    return lax.ppermute(x, "mp", [(there, here) for here, there in chip_pairs(k)])


def give_chip(x, k):
    return lax.ppermute(x, "mp", chip_pairs(k))


def block_of(size, most, unit):
    return max([b for b in range(unit, most + 1, unit) if size % b == 0], default=size)


def call(body, shapes, args, name, scratch=(), limit=8, flops=10**6, bytes_accessed=10**5,
         in_space=pltpu.VMEM, out_spaces=None):
    return pl.pallas_call(
        body,
        in_specs=[pl.BlockSpec(memory_space=in_space)] * len(args),
        out_specs=[
            pl.BlockSpec(memory_space=space) for space in out_spaces or [pltpu.VMEM] * len(shapes)
        ],
        out_shape=[jax.ShapeDtypeStruct(*shape) for shape in shapes],
        scratch_shapes=list(scratch),
        compiler_params=pltpu.CompilerParams(vmem_limit_bytes=limit << 20),
        cost_estimate=pl.CostEstimate(
            flops=flops, bytes_accessed=bytes_accessed, transcendentals=0
        ),
        name=name,
    )(*args)


def place_of(block, chips):
    m = lax.axis_index("mp")
    core, k = divmod(block, chips)
    return 2 * partner(lax.shift_right_logical(m, 1), k, chips) + ((m & 1) ^ core)


def lead_body(out):
    out[...] = jnp.zeros_like(out)


def lead():
    return call(
        lead_body, [((8, 128), jnp.float32)], [], "lead", flops=10**10, bytes_accessed=36 * 10**6
    )[0]


def pack_body(tokens_in, grad_in, pre_in, after, both, pre_ref, tokens_ref, grad_ref, sems):
    copies = [
        pltpu.make_async_copy(source, target, sems.at[i])
        for i, (source, target) in enumerate(
            ((tokens_in, tokens_ref), (grad_in, grad_ref), (pre_in, pre_ref))
        )
    ]
    for copy in copies:
        copy.start()
    for copy in copies:
        copy.wait()
    both[...] = jnp.concatenate(
        [tokens_ref[...].astype(jnp.float32), grad_ref[...].astype(jnp.float32)], axis=0
    ).astype(jnp.bfloat16)


def pack(tokens_in, grad_out, pre_act, after):
    rows, width = tokens_in.shape
    shapes = [(2 * rows, width), pre_act.shape]
    return call(
        pack_body,
        [(shape, jnp.bfloat16) for shape in shapes],
        [tokens_in, grad_out, pre_act, after],
        "pack",
        [
            pltpu.VMEM(tokens_in.shape, jnp.bfloat16),
            pltpu.VMEM(tokens_in.shape, jnp.bfloat16),
            pltpu.SemaphoreType.DMA((3,)),
        ],
        flops=10**10,
        bytes_accessed=36 * 10**6,
        in_space=pltpu.HBM,
    )


def join_body(count, after, *refs):
    rows_in = refs[:count]
    *pieces, grad_ref, slabs = refs[count:]
    places, _, _, part = slabs.shape
    parts = [x[...].astype(jnp.float32) for x in rows_in]
    each = parts[0].shape[0] // 2
    tokens = jnp.concatenate([x[:each] for x in parts], axis=0)
    grad = jnp.concatenate([x[each:] for x in parts], axis=0)
    grad_ref[...] = grad.astype(jnp.bfloat16)
    for p in range(places):
        here = slice(p * part, (p + 1) * part)
        slabs[p, 0] = tokens[:, here]
        slabs[p, 1] = grad[:, here]
    t = lax.axis_index("tokens")
    for k, ref in enumerate(pieces):
        taker = t ^ k if places & (places - 1) == 0 else lax.rem(t - k + places, places)
        ref[...] = slabs[taker].astype(jnp.bfloat16)


def join(rows_in, n_tok, after):
    count, (both, width) = len(rows_in), rows_in[0].shape
    rows, part = count * both // 2, width // n_tok
    shapes = [(2, rows, part)] * n_tok + [(rows, width)]
    return call(
        functools.partial(join_body, count),
        [(shape, jnp.bfloat16) for shape in shapes],
        [after, *rows_in],
        "join",
        [pltpu.VMEM((n_tok, 2, rows, part), jnp.float32)],
        limit=16,
    )


def stack_body(count, *refs):
    pieces, out = refs[:count], refs[-1]
    for k, x in enumerate(pieces):
        out[k] = x[...]


def stack(pieces, after=()):
    shape = (len(pieces),) + pieces[0].shape
    body = functools.partial(stack_body, len(pieces))
    return call(body, [(shape, jnp.bfloat16)], [*pieces, *after], "stack")[0]


def pile_body(low, high, out):
    count = out.shape[0] // 2
    if count == 1:
        out[0] = low[...]
        out[1] = high[...]
    else:
        out[:count] = low[...]
        out[count:] = high[...]


def spread(x, masks):
    held, got, order, where = x, [], [0], {0: (0, 0)}
    n = lax.axis_size("tokens")
    for mask in masks:
        if got:
            shape = (len(order),) + x.shape
            held = call(pile_body, [(shape, jnp.bfloat16)], [held, got[-1]], "pile")[0]
        got.append(lax.ppermute(held, "tokens", [(i ^ mask, i) for i in range(n)]))
        for j, k in enumerate(order):
            where[k ^ mask] = (len(got), j)
        order = order + [k ^ mask for k in order]
    return held, got, where


def grad_pre_body(block, own_ref, other_ref, pre_ref, w_ref, out_ref, rows, total):
    hidden, group = total.shape
    half = own_ref.shape[0]
    rows[:half, :] = own_ref[...]
    rows[half:, :] = other_ref[...]
    for low in range(0, hidden, block):
        here = slice(low, low + block)
        total[here, :] = lax.dot_general(
            w_ref[here, :], rows[...], (((1,), (1,)), ((), ())), preferred_element_type=jnp.float32
        )
    each = group // lax.axis_size("mp")
    chips = half // each
    row = lax.broadcasted_iota(jnp.int32, (group, 1), 0)
    from_row = row
    for b in range(group // each):
        inside = (row >= b * each) & (row < (b + 1) * each)
        from_row = jnp.where(inside, row + (place_of(b, chips) - b) * each, from_row)
    pick = from_row == lax.broadcasted_iota(jnp.int32, (group, group), 1)
    pre = jnp.dot(
        pick.astype(jnp.float32).astype(jnp.bfloat16), pre_ref[...], preferred_element_type=jnp.float32
    )
    out_ref[...] = (total[...].T * gelu_slope(pre)).astype(jnp.bfloat16)


def grad_pre_of(own, other, pre_act, w_out):
    group, hidden = pre_act.shape
    width = w_out.shape[1]
    return call(
        functools.partial(grad_pre_body, block_of(hidden, 432, 16)),
        [((group, hidden), jnp.bfloat16)],
        [own, other, pre_act, w_out],
        "grad_pre",
        [pltpu.VMEM((group, width), jnp.bfloat16), pltpu.VMEM((hidden, group), jnp.float32)],
        flops=2 * group * width * hidden,
        bytes_accessed=2 * hidden * width,
    )[0]


def grad_in_body(block, grad_pre_ref, w_ref, *refs):
    out_ref = refs[-1]
    places, rows, width = out_ref.shape
    for low in range(0, width, block):
        here = slice(low, low + block)
        term = jnp.dot(grad_pre_ref[...], w_ref[:, here], preferred_element_type=jnp.float32)
        for b in range(places):
            out_ref[place_of(b, places // 2), :, here] = term[b * rows : (b + 1) * rows].astype(
                jnp.bfloat16
            )


def grad_in_part(grad_pre, w_in_t, places, after):
    group, hidden = grad_pre.shape
    width = w_in_t.shape[1]
    return call(
        functools.partial(grad_in_body, block_of(width, 1024, 128)),
        [((places, group // places, width), jnp.bfloat16)],
        [grad_pre, w_in_t, *after],
        "grad_in_part",
        flops=2 * group * width * hidden,
        bytes_accessed=2 * hidden * width,
    )[0]


def finish_body(terms_ref, after, out):
    total = terms_ref[0].astype(jnp.float32)
    for k in range(1, terms_ref.shape[0]):
        total = total + terms_ref[k].astype(jnp.float32)
    out[...] = total.astype(jnp.bfloat16)


def finish(terms, after):
    return call(finish_body, [(terms.shape[1:], jnp.bfloat16)], [terms, after], "finish")[0]


def turn(x_ref, to_ref, unit):
    hidden = x_ref.shape[1]
    for low in range(0, hidden, unit):
        size = min(unit, hidden - low)
        eye = lax.broadcasted_iota(jnp.int32, (size, size), 0) == lax.broadcasted_iota(
            jnp.int32, (size, size), 1
        )
        to_ref[low : low + size, :] = lax.dot_general(
            eye.astype(jnp.float32).astype(jnp.bfloat16),
            x_ref[:, low : low + size],
            (((1,), (1,)), ((), ())),
            preferred_element_type=jnp.float32,
        ).astype(jnp.bfloat16)


def grad_w_body(count, places, slab, act, scale_back, block, *refs):
    row_refs = refs[:count]
    own_ref, other_ref = refs[count : count + 2]
    to_ref, end_ref, flat, sorted_rows, turned, held, sems = refs[-7:]
    end_ref[...] = jnp.zeros_like(end_ref)
    total, hidden = flat.shape
    group = total // places
    part = own_ref.shape[3]
    half = group // 2
    chips = lax.axis_size("mp") // 2
    rows = half // chips

    for k in range(places):
        here = slice(k * group, (k + 1) * group)
        if act is None:
            flat[here, :] = row_refs[k][...]
        else:
            array, j = act[k]
            ref = row_refs[array]
            pre = (ref[...] if len(ref.shape) == 2 else ref[j]).astype(jnp.float32)
            flat[here, :] = gelu_value(pre).astype(jnp.bfloat16)

    size = block_of(total, 128, rows)
    blocks = [(core, k, chip) for core in range(2) for k in range(places) for chip in range(chips)]
    for low in range(0, total, size):
        row = low + lax.broadcasted_iota(jnp.int32, (size, 1), 0)
        from_row = row
        for core, k, chip in blocks[low // rows : (low + size) // rows]:
            first = core * places * half + k * half + chip * rows
            inside = (row >= first) & (row < first + rows)
            b = core * chips + chip
            place = b if act is None else place_of(b, chips)
            from_row = jnp.where(inside, row + (k * group + place * rows - first), from_row)
        pick = from_row == lax.broadcasted_iota(jnp.int32, (size, total), 1)
        sorted_rows[low : low + size, :] = jnp.dot(
            pick.astype(jnp.float32).astype(jnp.bfloat16),
            flat[...],
            preferred_element_type=jnp.float32,
        ).astype(jnp.bfloat16)
    turn(sorted_rows, turned, 256)

    copies = []
    for low in range(0, part, block):
        here = slice(low, low + block)
        cols = jnp.concatenate(
            [ref[k, slab, :, here] for ref in (own_ref, other_ref) for k in range(places)], axis=0
        )
        term = jnp.dot(turned[...], cols, preferred_element_type=jnp.float32)
        held[:, here] = (term * scale_back).astype(jnp.bfloat16)
        copies.append(
            pltpu.make_async_copy(held.at[:, here], to_ref.at[:, here], sems.at[len(copies)])
        )
        copies[-1].start()
    for copy in copies:
        copy.wait()


def grad_w_of(row_arrays, act, own, other, slab, scale_back, name, flops, after=()):
    group, hidden = row_arrays[0].shape
    places, _, _, part = own.shape
    total = places * group
    block = block_of(part, 256, 128)
    body = functools.partial(grad_w_body, len(row_arrays), places, slab, act, scale_back, block)
    return call(
        body,
        [((hidden, part), jnp.bfloat16), ((8, 128), jnp.float32)],
        [*row_arrays, own, other, *after],
        name,
        [
            pltpu.VMEM((total, hidden), jnp.bfloat16),
            pltpu.VMEM((total, hidden), jnp.bfloat16),
            pltpu.VMEM((hidden, total), jnp.bfloat16),
            pltpu.VMEM((hidden, part), jnp.bfloat16),
            pltpu.SemaphoreType.DMA((part // block,)),
        ],
        limit=20,
        flops=flops,
        bytes_accessed=2 * hidden * part,
        out_spaces=[pltpu.HBM, pltpu.VMEM],
    )


def shards(tokens_in, grad_out, pre_act, w_in, w_out):
    n_mp, n_tok = lax.axis_size("mp"), lax.axis_size("tokens")
    chips = n_mp // 2
    scale_back = 1.0 / math.sqrt(pre_act.shape[0] * n_tok)

    masks = (3, 1) if n_tok == 4 else [1 << i for i in range(n_tok.bit_length() - 1)]
    held, pre, where = spread(pre_act, masks)
    both, pre_act = pack(tokens_in, grad_out, pre_act, lead())
    *pieces, own_rows = join(
        [both] + [fetch_chip(both, k) for k in range(1, chips)], n_tok, held
    )
    pieces = [x if k == 0 else fetch(x, "tokens", k) for k, x in enumerate(pieces)]

    grad_pre = grad_pre_of(own_rows, other_core(own_rows), pre_act, w_out)
    grad_pre_all = [grad_pre] + [fetch(grad_pre, "tokens", k) for k in range(1, n_tok)]
    own_cols = stack(pieces, [grad_pre])
    other_cols = other_core(own_cols)
    blocks = grad_in_part(grad_pre, w_in.T, n_mp, [pre[-1]])
    terms = lax.all_to_all(blocks, "mp", 0, 0)
    grad_w_out, mid = grad_w_of(
        [pre_act, *pre], where, own_cols, other_cols, 1, scale_back, "grad_w_out", 10**9
    )
    grad_w_in_t, end = grad_w_of(
        grad_pre_all, None, own_cols, other_cols, 0, scale_back, "grad_w_in", 5 * 10**10, [mid]
    )
    return (finish(terms, end), grad_w_in_t.T, grad_w_out)


def solution(mesh):
    placed = (
        P(("tokens", "mp"), None),
        P(("tokens", "mp"), None),
        P("tokens", "mp"),
        P(None, "mp"),
        P("mp", None),
    )
    return jax.shard_map(
        shards,
        mesh=mesh,
        in_specs=placed,
        out_specs=(P(("tokens", "mp"), None), P("tokens", "mp"), P("mp", "tokens")),
        check_vma=False,
    )
```

```python
import functools
import math

import jax
import jax.numpy as jnp
from jax import lax
from jax.experimental import pallas as pl
from jax.experimental.pallas import tpu as pltpu
from jax.sharding import PartitionSpec as P

root_two_pi = math.sqrt(2.0 / math.pi)
cubic = 0.044715


def gelu_value(pre):
    inner = root_two_pi * (pre + cubic * pre * pre * pre)
    return 0.5 * pre * (1.0 + jnp.tanh(inner))


def gelu_slope(pre):
    tanh_val = jnp.tanh(root_two_pi * (pre + cubic * pre * pre * pre))
    return 0.5 * (1.0 + tanh_val) + 0.5 * pre * (1.0 - tanh_val * tanh_val) * root_two_pi * (
        1.0 + 3.0 * cubic * pre * pre
    )


def partner(i, k, n):
    if n & (n - 1) == 0:
        return i ^ k
    return (i + k) % n if isinstance(i, int) else lax.rem(i + k, n)


def fetch(x, axis, k):
    n = lax.axis_size(axis)
    return lax.ppermute(x, axis, [(partner(i, k, n), i) for i in range(n)])


def other_core(x):
    return lax.ppermute(x, "mp", [(i ^ 1, i) for i in range(lax.axis_size("mp"))])


def chip_pairs(k):
    n = lax.axis_size("mp")
    return [(i, partner(i // 2, k, n // 2) * 2 + i % 2) for i in range(n)]


def fetch_chip(x, k):
    return lax.ppermute(x, "mp", [(there, here) for here, there in chip_pairs(k)])


def give_chip(x, k):
    return lax.ppermute(x, "mp", chip_pairs(k))


def block_of(size, most, unit):
    return max([b for b in range(unit, most + 1, unit) if size % b == 0], default=size)


def call(body, shapes, args, name, scratch=(), limit=8, flops=10**6, bytes_accessed=10**5,
         in_space=pltpu.VMEM, out_spaces=None):
    return pl.pallas_call(
        body,
        in_specs=[pl.BlockSpec(memory_space=in_space)] * len(args),
        out_specs=[
            pl.BlockSpec(memory_space=space) for space in out_spaces or [pltpu.VMEM] * len(shapes)
        ],
        out_shape=[jax.ShapeDtypeStruct(*shape) for shape in shapes],
        scratch_shapes=list(scratch),
        compiler_params=pltpu.CompilerParams(vmem_limit_bytes=limit << 20),
        cost_estimate=pl.CostEstimate(
            flops=flops, bytes_accessed=bytes_accessed, transcendentals=0
        ),
        name=name,
    )(*args)


def place_of(block, chips):
    m = lax.axis_index("mp")
    core, k = divmod(block, chips)
    return 2 * partner(lax.shift_right_logical(m, 1), k, chips) + ((m & 1) ^ core)


def lead_body(out):
    out[...] = jnp.zeros_like(out)


def lead():
    return call(
        lead_body, [((8, 128), jnp.float32)], [], "lead", flops=10**10, bytes_accessed=36 * 10**6
    )[0]


def pack_body(tokens_ref, grad_ref, pre_in, after, both, pre_ref):
    both[...] = jnp.concatenate(
        [tokens_ref[...].astype(jnp.float32), grad_ref[...].astype(jnp.float32)], axis=0
    ).astype(jnp.bfloat16)
    pre_ref[...] = pre_in[...]


def pack(tokens_in, grad_out, pre_act, after):
    rows, width = tokens_in.shape
    shapes = [(2 * rows, width), pre_act.shape]
    return call(
        pack_body,
        [(shape, jnp.bfloat16) for shape in shapes],
        [tokens_in, grad_out, pre_act, after],
        "pack",
        flops=10**10,
        bytes_accessed=36 * 10**6,
    )


def join_body(count, after, *refs):
    rows_in = refs[:count]
    *pieces, grad_ref, slabs = refs[count:]
    places, _, _, part = slabs.shape
    parts = [x[...].astype(jnp.float32) for x in rows_in]
    each = parts[0].shape[0] // 2
    tokens = jnp.concatenate([x[:each] for x in parts], axis=0)
    grad = jnp.concatenate([x[each:] for x in parts], axis=0)
    grad_ref[...] = grad.astype(jnp.bfloat16)
    for p in range(places):
        here = slice(p * part, (p + 1) * part)
        slabs[p, 0] = tokens[:, here]
        slabs[p, 1] = grad[:, here]
    t = lax.axis_index("tokens")
    for k, ref in enumerate(pieces):
        taker = t ^ k if places & (places - 1) == 0 else lax.rem(t - k + places, places)
        ref[...] = slabs[taker].astype(jnp.bfloat16)


def join(rows_in, n_tok, after):
    count, (both, width) = len(rows_in), rows_in[0].shape
    rows, part = count * both // 2, width // n_tok
    shapes = [(2, rows, part)] * n_tok + [(rows, width)]
    return call(
        functools.partial(join_body, count),
        [(shape, jnp.bfloat16) for shape in shapes],
        [after, *rows_in],
        "join",
        [pltpu.VMEM((n_tok, 2, rows, part), jnp.float32)],
        limit=16,
    )


def stack_body(count, *refs):
    pieces, out = refs[:count], refs[-1]
    for k, x in enumerate(pieces):
        out[k] = x[...]


def stack(pieces, after=()):
    shape = (len(pieces),) + pieces[0].shape
    body = functools.partial(stack_body, len(pieces))
    return call(body, [(shape, jnp.bfloat16)], [*pieces, *after], "stack")[0]


def pile_body(low, high, *refs):
    out = refs[-1]
    count = out.shape[0] // 2
    if count == 1:
        out[0] = low[...]
        out[1] = high[...]
    else:
        out[:count] = low[...]
        out[count:] = high[...]


def swap(x, mask):
    return lax.ppermute(x, "tokens", [(i ^ mask, i) for i in range(lax.axis_size("tokens"))])


def spread(x, first, masks, after):
    held, got, order, where = x, [first], [0, masks[0]], {0: (0, 0), masks[0]: (1, 0)}
    for mask in masks[1:]:
        shape = (len(order),) + x.shape
        held = call(pile_body, [(shape, jnp.bfloat16)], [held, got[-1], *after], "pile")[0]
        got.append(swap(held, mask))
        for j, k in enumerate(order):
            where[k ^ mask] = (len(got), j)
        order = order + [k ^ mask for k in order]
    return got, where


def grad_pre_body(block, own_ref, other_ref, pre_ref, w_ref, out_ref, rows, total):
    hidden, group = total.shape
    half = own_ref.shape[0]
    rows[:half, :] = own_ref[...]
    rows[half:, :] = other_ref[...]
    for low in range(0, hidden, block):
        here = slice(low, low + block)
        total[here, :] = lax.dot_general(
            w_ref[here, :], rows[...], (((1,), (1,)), ((), ())), preferred_element_type=jnp.float32
        )
    each = group // lax.axis_size("mp")
    chips = half // each
    row = lax.broadcasted_iota(jnp.int32, (group, 1), 0)
    from_row = row
    for b in range(group // each):
        inside = (row >= b * each) & (row < (b + 1) * each)
        from_row = jnp.where(inside, row + (place_of(b, chips) - b) * each, from_row)
    pick = from_row == lax.broadcasted_iota(jnp.int32, (group, group), 1)
    pre = jnp.dot(
        pick.astype(jnp.float32).astype(jnp.bfloat16), pre_ref[...], preferred_element_type=jnp.float32
    )
    out_ref[...] = (total[...].T * gelu_slope(pre)).astype(jnp.bfloat16)


def grad_pre_of(own, other, pre_act, w_out):
    group, hidden = pre_act.shape
    width = w_out.shape[1]
    return call(
        functools.partial(grad_pre_body, block_of(hidden, 432, 16)),
        [((group, hidden), jnp.bfloat16)],
        [own, other, pre_act, w_out],
        "grad_pre",
        [pltpu.VMEM((group, width), jnp.bfloat16), pltpu.VMEM((hidden, group), jnp.float32)],
        flops=2 * group * width * hidden,
        bytes_accessed=2 * hidden * width,
    )[0]


def grad_in_body(block, grad_pre_ref, w_ref, *refs):
    out_ref = refs[-1]
    places, rows, width = out_ref.shape
    for low in range(0, width, block):
        here = slice(low, low + block)
        term = jnp.dot(grad_pre_ref[...], w_ref[:, here], preferred_element_type=jnp.float32)
        for b in range(places):
            out_ref[place_of(b, places // 2), :, here] = term[b * rows : (b + 1) * rows].astype(
                jnp.bfloat16
            )


def grad_in_part(grad_pre, w_in_t, places, after):
    group, hidden = grad_pre.shape
    width = w_in_t.shape[1]
    return call(
        functools.partial(grad_in_body, block_of(width, 1024, 128)),
        [((places, group // places, width), jnp.bfloat16)],
        [grad_pre, w_in_t, *after],
        "grad_in_part",
        flops=2 * group * width * hidden,
        bytes_accessed=2 * hidden * width,
    )[0]


def finish_body(terms_ref, after, out):
    total = terms_ref[0].astype(jnp.float32)
    for k in range(1, terms_ref.shape[0]):
        total = total + terms_ref[k].astype(jnp.float32)
    out[...] = total.astype(jnp.bfloat16)


def finish(terms, after):
    return call(finish_body, [(terms.shape[1:], jnp.bfloat16)], [terms, after], "finish")[0]


def turn(x_ref, to_ref, unit):
    hidden = x_ref.shape[1]
    for low in range(0, hidden, unit):
        size = min(unit, hidden - low)
        eye = lax.broadcasted_iota(jnp.int32, (size, size), 0) == lax.broadcasted_iota(
            jnp.int32, (size, size), 1
        )
        to_ref[low : low + size, :] = lax.dot_general(
            eye.astype(jnp.float32).astype(jnp.bfloat16),
            x_ref[:, low : low + size],
            (((1,), (1,)), ((), ())),
            preferred_element_type=jnp.float32,
        ).astype(jnp.bfloat16)


def grad_w_body(count, places, slab, act, scale_back, block, *refs):
    row_refs = refs[:count]
    own_ref, other_ref = refs[count : count + 2]
    to_ref, end_ref, flat, sorted_rows, turned, held, sems = refs[-7:]
    end_ref[...] = jnp.zeros_like(end_ref)
    total, hidden = flat.shape
    group = total // places
    part = own_ref.shape[3]
    half = group // 2
    chips = lax.axis_size("mp") // 2
    rows = half // chips

    for k in range(places):
        here = slice(k * group, (k + 1) * group)
        if act is None:
            flat[here, :] = row_refs[k][...]
        else:
            array, j = act[k]
            ref = row_refs[array]
            pre = (ref[...] if len(ref.shape) == 2 else ref[j]).astype(jnp.float32)
            flat[here, :] = gelu_value(pre).astype(jnp.bfloat16)

    size = block_of(total, 128, rows)
    blocks = [(core, k, chip) for core in range(2) for k in range(places) for chip in range(chips)]
    for low in range(0, total, size):
        row = low + lax.broadcasted_iota(jnp.int32, (size, 1), 0)
        from_row = row
        for core, k, chip in blocks[low // rows : (low + size) // rows]:
            first = core * places * half + k * half + chip * rows
            inside = (row >= first) & (row < first + rows)
            b = core * chips + chip
            place = b if act is None else place_of(b, chips)
            from_row = jnp.where(inside, row + (k * group + place * rows - first), from_row)
        pick = from_row == lax.broadcasted_iota(jnp.int32, (size, total), 1)
        sorted_rows[low : low + size, :] = jnp.dot(
            pick.astype(jnp.float32).astype(jnp.bfloat16),
            flat[...],
            preferred_element_type=jnp.float32,
        ).astype(jnp.bfloat16)
    turn(sorted_rows, turned, 256)

    copies = []
    for low in range(0, part, block):
        here = slice(low, low + block)
        cols = jnp.concatenate(
            [ref[k, slab, :, here] for ref in (own_ref, other_ref) for k in range(places)], axis=0
        )
        term = jnp.dot(turned[...], cols, preferred_element_type=jnp.float32)
        held[:, here] = (term * scale_back).astype(jnp.bfloat16)
        copies.append(
            pltpu.make_async_copy(held.at[:, here], to_ref.at[:, here], sems.at[len(copies)])
        )
        copies[-1].start()
    for copy in copies:
        copy.wait()


def grad_w_of(row_arrays, act, own, other, slab, scale_back, name, flops, after=()):
    group, hidden = row_arrays[0].shape
    places, _, _, part = own.shape
    total = places * group
    block = block_of(part, 256, 128)
    body = functools.partial(grad_w_body, len(row_arrays), places, slab, act, scale_back, block)
    return call(
        body,
        [((hidden, part), jnp.bfloat16), ((8, 128), jnp.float32)],
        [*row_arrays, own, other, *after],
        name,
        [
            pltpu.VMEM((total, hidden), jnp.bfloat16),
            pltpu.VMEM((total, hidden), jnp.bfloat16),
            pltpu.VMEM((hidden, total), jnp.bfloat16),
            pltpu.VMEM((hidden, part), jnp.bfloat16),
            pltpu.SemaphoreType.DMA((part // block,)),
        ],
        limit=20,
        flops=flops,
        out_spaces=[pltpu.HBM, pltpu.VMEM],
    )


def shards(tokens_in, grad_out, pre_act, w_in, w_out):
    n_mp, n_tok = lax.axis_size("mp"), lax.axis_size("tokens")
    chips = n_mp // 2
    scale_back = 1.0 / math.sqrt(pre_act.shape[0] * n_tok)

    masks = (3, 1) if n_tok == 4 else [1 << i for i in range(n_tok.bit_length() - 1)]
    first = swap(pre_act, masks[0])
    both, pre_act = pack(tokens_in, grad_out, pre_act, lead())
    *pieces, own_rows = join(
        [both] + [fetch_chip(both, k) for k in range(1, chips)], n_tok, first
    )
    pieces = [x if k == 0 else fetch(x, "tokens", k) for k, x in enumerate(pieces)]

    grad_pre = grad_pre_of(own_rows, other_core(own_rows), pre_act, w_out)
    grad_pre_all = [grad_pre] + [fetch(grad_pre, "tokens", k) for k in range(1, n_tok)]
    own_cols = stack(pieces, [grad_pre])
    other_cols = other_core(own_cols)
    blocks = grad_in_part(grad_pre, w_in.T, n_mp, [])
    terms = lax.all_to_all(blocks, "mp", 0, 0)
    pre, where = spread(pre_act, first, masks, [grad_pre])
    grad_w_in_t, mid = grad_w_of(
        grad_pre_all, None, own_cols, other_cols, 0, scale_back, "grad_w_in", 10**6
    )
    grad_w_out, end = grad_w_of(
        [pre_act, *pre], where, own_cols, other_cols, 1, scale_back, "grad_w_out", 5 * 10**10, [mid]
    )
    return (finish(terms, end), grad_w_in_t.T, grad_w_out)


def solution(mesh):
    placed = (
        P(("tokens", "mp"), None),
        P(("tokens", "mp"), None),
        P("tokens", "mp"),
        P(None, "mp"),
        P("mp", None),
    )
    return jax.shard_map(
        shards,
        mesh=mesh,
        in_specs=placed,
        out_specs=(P(("tokens", "mp"), None), P("tokens", "mp"), P("mp", "tokens")),
        check_vma=False,
    )
```

```python
import functools
import math

import jax
import jax.numpy as jnp
from jax import lax
from jax.experimental import pallas as pl
from jax.experimental.pallas import tpu as pltpu
from jax.sharding import PartitionSpec as P

root_two_pi = math.sqrt(2.0 / math.pi)
cubic = 0.044715


def gelu_value(pre):
    inner = root_two_pi * (pre + cubic * pre * pre * pre)
    return 0.5 * pre * (1.0 + jnp.tanh(inner))


def gelu_slope(pre):
    tanh_val = jnp.tanh(root_two_pi * (pre + cubic * pre * pre * pre))
    return 0.5 * (1.0 + tanh_val) + 0.5 * pre * (1.0 - tanh_val * tanh_val) * root_two_pi * (
        1.0 + 3.0 * cubic * pre * pre
    )


def partner(i, k, n):
    if n & (n - 1) == 0:
        return i ^ k
    return (i + k) % n if isinstance(i, int) else lax.rem(i + k, n)


def fetch(x, axis, k):
    n = lax.axis_size(axis)
    return lax.ppermute(x, axis, [(partner(i, k, n), i) for i in range(n)])


def other_core(x):
    return lax.ppermute(x, "mp", [(i ^ 1, i) for i in range(lax.axis_size("mp"))])


def chip_pairs(k):
    n = lax.axis_size("mp")
    return [(i, partner(i // 2, k, n // 2) * 2 + i % 2) for i in range(n)]


def fetch_chip(x, k):
    return lax.ppermute(x, "mp", [(there, here) for here, there in chip_pairs(k)])


def give_chip(x, k):
    return lax.ppermute(x, "mp", chip_pairs(k))


def block_of(size, most, unit):
    return max([b for b in range(unit, most + 1, unit) if size % b == 0], default=size)


def call(body, shapes, args, name, scratch=(), limit=8, flops=10**6, bytes_accessed=10**5,
         in_space=pltpu.VMEM, out_spaces=None):
    return pl.pallas_call(
        body,
        in_specs=[pl.BlockSpec(memory_space=in_space)] * len(args),
        out_specs=[
            pl.BlockSpec(memory_space=space) for space in out_spaces or [pltpu.VMEM] * len(shapes)
        ],
        out_shape=[jax.ShapeDtypeStruct(*shape) for shape in shapes],
        scratch_shapes=list(scratch),
        compiler_params=pltpu.CompilerParams(vmem_limit_bytes=limit << 20),
        cost_estimate=pl.CostEstimate(
            flops=flops, bytes_accessed=bytes_accessed, transcendentals=0
        ),
        name=name,
    )(*args)


def place_of(block, chips):
    m = lax.axis_index("mp")
    core, k = divmod(block, chips)
    return 2 * partner(lax.shift_right_logical(m, 1), k, chips) + ((m & 1) ^ core)


def lead_body(out):
    out[...] = jnp.zeros_like(out)


def lead():
    return call(
        lead_body, [((8, 128), jnp.float32)], [], "lead", flops=10**10, bytes_accessed=36 * 10**6
    )[0]


def pack_body(tokens_ref, grad_ref, pre_in, after, both, pre_ref):
    both[...] = jnp.concatenate(
        [tokens_ref[...].astype(jnp.float32), grad_ref[...].astype(jnp.float32)], axis=0
    ).astype(jnp.bfloat16)
    pre_ref[...] = pre_in[...]


def pack(tokens_in, grad_out, pre_act, after):
    rows, width = tokens_in.shape
    shapes = [(2 * rows, width), pre_act.shape]
    return call(
        pack_body,
        [(shape, jnp.bfloat16) for shape in shapes],
        [tokens_in, grad_out, pre_act, after],
        "pack",
        flops=10**10,
        bytes_accessed=36 * 10**6,
    )


def join_body(count, places, *refs):
    rows_in = refs[:count]
    *pieces, grad_ref, slabs = refs[-places - 2 :]
    part = slabs.shape[3]
    parts = [x[...].astype(jnp.float32) for x in rows_in]
    each = parts[0].shape[0] // 2
    tokens = jnp.concatenate([x[:each] for x in parts], axis=0)
    grad = jnp.concatenate([x[each:] for x in parts], axis=0)
    grad_ref[...] = grad.astype(jnp.bfloat16)
    for p in range(places):
        here = slice(p * part, (p + 1) * part)
        slabs[p, 0] = tokens[:, here]
        slabs[p, 1] = grad[:, here]
    t = lax.axis_index("tokens")
    for k, ref in enumerate(pieces):
        taker = t ^ k if places & (places - 1) == 0 else lax.rem(t - k + places, places)
        ref[...] = slabs[taker].astype(jnp.bfloat16)


def join(rows_in, n_tok, after):
    count, (both, width) = len(rows_in), rows_in[0].shape
    rows, part = count * both // 2, width // n_tok
    shapes = [(2, rows, part)] * n_tok + [(rows, width)]
    return call(
        functools.partial(join_body, count, n_tok),
        [(shape, jnp.bfloat16) for shape in shapes],
        [*rows_in, *after],
        "join",
        [pltpu.VMEM((n_tok, 2, rows, part), jnp.float32)],
        limit=16,
    )


def stack_body(count, *refs):
    pieces, out = refs[:count], refs[-1]
    for k, x in enumerate(pieces):
        out[k] = x[...]


def stack(pieces, after=()):
    shape = (len(pieces),) + pieces[0].shape
    body = functools.partial(stack_body, len(pieces))
    return call(body, [(shape, jnp.bfloat16)], [*pieces, *after], "stack")[0]


def grad_pre_body(block, own_ref, other_ref, pre_ref, w_ref, rider_ref, out_ref, duo_ref, rows, total):
    hidden, group = total.shape
    half = own_ref.shape[0]
    rows[:half, :] = own_ref[...]
    rows[half:, :] = other_ref[...]
    for low in range(0, hidden, block):
        here = slice(low, low + block)
        total[here, :] = lax.dot_general(
            w_ref[here, :], rows[...], (((1,), (1,)), ((), ())), preferred_element_type=jnp.float32
        )
    each = group // lax.axis_size("mp")
    chips = half // each
    row = lax.broadcasted_iota(jnp.int32, (group, 1), 0)
    from_row = row
    for b in range(group // each):
        inside = (row >= b * each) & (row < (b + 1) * each)
        from_row = jnp.where(inside, row + (place_of(b, chips) - b) * each, from_row)
    pick = from_row == lax.broadcasted_iota(jnp.int32, (group, group), 1)
    pre = jnp.dot(
        pick.astype(jnp.float32).astype(jnp.bfloat16), pre_ref[...], preferred_element_type=jnp.float32
    )
    grad_pre = (total[...].T * gelu_slope(pre)).astype(jnp.bfloat16)
    out_ref[...] = grad_pre
    duo_ref[0] = grad_pre
    duo_ref[1] = rider_ref[...]


def grad_pre_of(own, other, pre_act, w_out, rider):
    group, hidden = pre_act.shape
    width = w_out.shape[1]
    return call(
        functools.partial(grad_pre_body, block_of(hidden, 432, 16)),
        [((group, hidden), jnp.bfloat16), ((2, group, hidden), jnp.bfloat16)],
        [own, other, pre_act, w_out, rider],
        "grad_pre",
        [pltpu.VMEM((group, width), jnp.bfloat16), pltpu.VMEM((hidden, group), jnp.float32)],
        flops=2 * group * width * hidden,
        bytes_accessed=2 * hidden * width,
    )


def grad_in_body(block, grad_pre_ref, w_ref, *refs):
    out_ref = refs[-1]
    places, rows, width = out_ref.shape
    for low in range(0, width, block):
        here = slice(low, low + block)
        term = jnp.dot(grad_pre_ref[...], w_ref[:, here], preferred_element_type=jnp.float32)
        for b in range(places):
            out_ref[place_of(b, places // 2), :, here] = term[b * rows : (b + 1) * rows].astype(
                jnp.bfloat16
            )


def grad_in_part(grad_pre, w_in_t, places, after):
    group, hidden = grad_pre.shape
    width = w_in_t.shape[1]
    return call(
        functools.partial(grad_in_body, block_of(width, 1024, 128)),
        [((places, group // places, width), jnp.bfloat16)],
        [grad_pre, w_in_t, *after],
        "grad_in_part",
        flops=2 * group * width * hidden,
        bytes_accessed=2 * hidden * width,
    )[0]


def finish_body(terms_ref, after, out):
    total = terms_ref[0].astype(jnp.float32)
    for k in range(1, terms_ref.shape[0]):
        total = total + terms_ref[k].astype(jnp.float32)
    out[...] = total.astype(jnp.bfloat16)


def finish(terms, after):
    return call(finish_body, [(terms.shape[1:], jnp.bfloat16)], [terms, after], "finish")[0]


def turn(x_ref, to_ref, unit):
    hidden = x_ref.shape[1]
    for low in range(0, hidden, unit):
        size = min(unit, hidden - low)
        eye = lax.broadcasted_iota(jnp.int32, (size, size), 0) == lax.broadcasted_iota(
            jnp.int32, (size, size), 1
        )
        to_ref[low : low + size, :] = lax.dot_general(
            eye.astype(jnp.float32).astype(jnp.bfloat16),
            x_ref[:, low : low + size],
            (((1,), (1,)), ((), ())),
            preferred_element_type=jnp.float32,
        ).astype(jnp.bfloat16)


def grad_w_body(arrays, pre_at, grad_pre_at, scale_back, block, *refs):
    own_ref, other_ref, in_ref, out_ref, end_ref = refs[arrays : arrays + 5]
    flat, sorted_rows, turned, held_in, held_out, sems = refs[arrays + 5 :]
    places = len(pre_at)

    def rows_of(at):
        ref = refs[at[0]]
        return ref[...] if len(ref.shape) == 2 else ref[at[1]]

    end_ref[...] = jnp.zeros_like(end_ref)
    group, part = flat.shape[0] // places, own_ref.shape[3]
    half, total = group // 2, places * group
    chips = lax.axis_size("mp") // 2
    rows = half // chips
    copies = []

    def arrange(place):
        size = block_of(total, 128, rows)
        blocks = [(core, k, chip) for core in range(2) for k in range(places) for chip in range(chips)]
        for low in range(0, total, size):
            row = low + lax.broadcasted_iota(jnp.int32, (size, 1), 0)
            from_row = row
            for core, k, chip in blocks[low // rows : (low + size) // rows]:
                first = core * places * half + k * half + chip * rows
                inside = (row >= first) & (row < first + rows)
                shift = k * group + place(core * chips + chip) * rows - first
                from_row = jnp.where(inside, row + shift, from_row)
            pick = from_row == lax.broadcasted_iota(jnp.int32, (size, total), 1)
            sorted_rows[low : low + size, :] = jnp.dot(
                pick.astype(jnp.float32).astype(jnp.bfloat16),
                flat[...],
                preferred_element_type=jnp.float32,
            ).astype(jnp.bfloat16)
        turn(sorted_rows, turned, 256)

    def product(right, held, to_ref):
        for low in range(0, part, block):
            here = slice(low, low + block)
            cols = jnp.concatenate(
                [ref[k, right, :, here] for ref in (own_ref, other_ref) for k in range(places)], axis=0
            )
            term = jnp.dot(turned[...], cols, preferred_element_type=jnp.float32)
            held[:, here] = (term * scale_back).astype(jnp.bfloat16)
            copies.append(
                pltpu.make_async_copy(held.at[:, here], to_ref.at[:, here], sems.at[len(copies)])
            )
            copies[-1].start()

    for k in range(places):
        pre = rows_of(pre_at[k]).astype(jnp.float32)
        flat[k * group : (k + 1) * group, :] = gelu_value(pre).astype(jnp.bfloat16)
    arrange(lambda b: place_of(b, chips))
    product(1, held_out, out_ref)
    for k in range(places):
        flat[k * group : (k + 1) * group, :] = rows_of(grad_pre_at[k])
    arrange(lambda b: b)
    product(0, held_in, in_ref)
    for copy in copies:
        copy.wait()


def grad_w_of(arrays, pre_at, grad_pre_at, own, other, scale_back):
    places = len(pre_at)
    group, hidden = arrays[0].shape
    total, part = places * group, own.shape[3]
    block = block_of(part, 256, 128)
    return call(
        functools.partial(grad_w_body, len(arrays), pre_at, grad_pre_at, scale_back, block),
        [((hidden, part), jnp.bfloat16)] * 2 + [((8, 128), jnp.float32)],
        [*arrays, own, other],
        "grad_w",
        [
            pltpu.VMEM((total, hidden), jnp.bfloat16),
            pltpu.VMEM((total, hidden), jnp.bfloat16),
            pltpu.VMEM((hidden, total), jnp.bfloat16),
            pltpu.VMEM((hidden, part), jnp.bfloat16),
            pltpu.VMEM((hidden, part), jnp.bfloat16),
            pltpu.SemaphoreType.DMA((2 * (part // block),)),
        ],
        limit=20,
        flops=80 * total * part * hidden,
        bytes_accessed=40 * hidden * part,
        out_spaces=[pltpu.HBM, pltpu.HBM, pltpu.VMEM],
    )


def shards(tokens_in, grad_out, pre_act, w_in, w_out):
    n_mp, n_tok = lax.axis_size("mp"), lax.axis_size("tokens")
    chips = n_mp // 2
    scale_back = 1.0 / math.sqrt(pre_act.shape[0] * n_tok)

    relay = n_tok == 4
    early = [k for k in range(1, n_tok) if not (relay and k == 2)]
    pre = {k: fetch(pre_act, "tokens", k) for k in reversed(early)}
    both, pre_act = pack(tokens_in, grad_out, pre_act, lead())
    *pieces, own_rows = join(
        [both] + [fetch_chip(both, k) for k in range(1, chips)],
        n_tok,
        [pre[k] for k in early] if relay else [],
    )
    pieces = [x if k == 0 else fetch(x, "tokens", k) for k, x in enumerate(pieces)]

    rider = pre[3] if relay else pre_act
    grad_pre, duo = grad_pre_of(own_rows, other_core(own_rows), pre_act, w_out, rider)
    grad_pre_all = [grad_pre] + [
        fetch(duo if relay and k == 1 else grad_pre, "tokens", k) for k in range(1, n_tok)
    ]
    own_cols = stack(pieces, [grad_pre])
    other_cols = other_core(own_cols)
    terms = lax.all_to_all(grad_in_part(grad_pre, w_in.T, n_mp, []), "mp", 0, 0)
    arrays = [pre_act] + [pre[k] for k in early] + grad_pre_all
    pre_at = {k: (i, 0) for i, k in enumerate([0] + early)}
    grad_pre_at = [(len(pre_at) + k, 0) for k in range(n_tok)]
    if relay:
        pre_at[2] = (grad_pre_at[1][0], 1)
    grad_w_in_t, grad_w_out, end = grad_w_of(
        arrays, pre_at, grad_pre_at, own_cols, other_cols, scale_back
    )
    return (finish(terms, end), grad_w_in_t.T, grad_w_out)


def solution(mesh):
    placed = (
        P(("tokens", "mp"), None),
        P(("tokens", "mp"), None),
        P("tokens", "mp"),
        P(None, "mp"),
        P("mp", None),
    )
    return jax.shard_map(
        shards,
        mesh=mesh,
        in_specs=placed,
        out_specs=(P(("tokens", "mp"), None), P("tokens", "mp"), P("mp", "tokens")),
        check_vma=False,
    )
```

```python
import functools
import math

import jax
import jax.numpy as jnp
from jax import lax
from jax.experimental import pallas as pl
from jax.experimental.pallas import tpu as pltpu
from jax.sharding import PartitionSpec as P

root_two_pi = math.sqrt(2.0 / math.pi)
cubic = 0.044715


def gelu_value(pre):
    inner = root_two_pi * (pre + cubic * pre * pre * pre)
    return 0.5 * pre * (1.0 + jnp.tanh(inner))


def gelu_slope(pre):
    tanh_val = jnp.tanh(root_two_pi * (pre + cubic * pre * pre * pre))
    return 0.5 * (1.0 + tanh_val) + 0.5 * pre * (1.0 - tanh_val * tanh_val) * root_two_pi * (
        1.0 + 3.0 * cubic * pre * pre
    )


def partner(i, k, n):
    if n & (n - 1) == 0:
        return i ^ k
    return (i + k) % n if isinstance(i, int) else lax.rem(i + k, n)


def fetch(x, axis, k):
    n = lax.axis_size(axis)
    return lax.ppermute(x, axis, [(partner(i, k, n), i) for i in range(n)])


def other_core(x):
    return lax.ppermute(x, "mp", [(i ^ 1, i) for i in range(lax.axis_size("mp"))])


def chip_pairs(k):
    n = lax.axis_size("mp")
    return [(i, partner(i // 2, k, n // 2) * 2 + i % 2) for i in range(n)]


def fetch_chip(x, k):
    return lax.ppermute(x, "mp", [(there, here) for here, there in chip_pairs(k)])


def give_chip(x, k):
    return lax.ppermute(x, "mp", chip_pairs(k))


def block_of(size, most, unit):
    return max([b for b in range(unit, most + 1, unit) if size % b == 0], default=size)


def call(body, shapes, args, name, scratch=(), limit=8, flops=10**6, bytes_accessed=10**5,
         in_space=pltpu.VMEM, out_spaces=None):
    return pl.pallas_call(
        body,
        in_specs=[pl.BlockSpec(memory_space=in_space)] * len(args),
        out_specs=[
            pl.BlockSpec(memory_space=space) for space in out_spaces or [pltpu.VMEM] * len(shapes)
        ],
        out_shape=[jax.ShapeDtypeStruct(*shape) for shape in shapes],
        scratch_shapes=list(scratch),
        compiler_params=pltpu.CompilerParams(vmem_limit_bytes=limit << 20),
        cost_estimate=pl.CostEstimate(
            flops=flops, bytes_accessed=bytes_accessed, transcendentals=0
        ),
        name=name,
    )(*args)


def place_of(block, chips):
    m = lax.axis_index("mp")
    core, k = divmod(block, chips)
    return 2 * partner(lax.shift_right_logical(m, 1), k, chips) + ((m & 1) ^ core)


def lead_body(out):
    out[...] = jnp.zeros_like(out)


def lead():
    return call(
        lead_body, [((8, 128), jnp.float32)], [], "lead", flops=10**10, bytes_accessed=36 * 10**6
    )[0]


def pack_body(tokens_ref, grad_ref, pre_in, after, both, pre_ref):
    both[...] = jnp.concatenate(
        [tokens_ref[...].astype(jnp.float32), grad_ref[...].astype(jnp.float32)], axis=0
    ).astype(jnp.bfloat16)
    pre_ref[...] = pre_in[...]


def pack(tokens_in, grad_out, pre_act, after):
    rows, width = tokens_in.shape
    shapes = [(2 * rows, width), pre_act.shape]
    return call(
        pack_body,
        [(shape, jnp.bfloat16) for shape in shapes],
        [tokens_in, grad_out, pre_act, after],
        "pack",
        flops=10**10,
        bytes_accessed=36 * 10**6,
    )


def join_body(count, places, *refs):
    rows_in = refs[:count]
    *pieces, grad_ref, slabs = refs[-places - 2 :]
    part = slabs.shape[3]
    parts = [x[...].astype(jnp.float32) for x in rows_in]
    each = parts[0].shape[0] // 2
    tokens = jnp.concatenate([x[:each] for x in parts], axis=0)
    grad = jnp.concatenate([x[each:] for x in parts], axis=0)
    grad_ref[...] = grad.astype(jnp.bfloat16)
    for p in range(places):
        here = slice(p * part, (p + 1) * part)
        slabs[p, 0] = tokens[:, here]
        slabs[p, 1] = grad[:, here]
    t = lax.axis_index("tokens")
    for k, ref in enumerate(pieces):
        taker = t ^ k if places & (places - 1) == 0 else lax.rem(t - k + places, places)
        ref[...] = slabs[taker].astype(jnp.bfloat16)


def join(rows_in, n_tok, after):
    count, (both, width) = len(rows_in), rows_in[0].shape
    rows, part = count * both // 2, width // n_tok
    shapes = [(2, rows, part)] * n_tok + [(rows, width)]
    return call(
        functools.partial(join_body, count, n_tok),
        [(shape, jnp.bfloat16) for shape in shapes],
        [*rows_in, *after],
        "join",
        [pltpu.VMEM((n_tok, 2, rows, part), jnp.float32)],
        limit=16,
    )


def stack_body(count, *refs):
    pieces, out = refs[:count], refs[-1]
    for k, x in enumerate(pieces):
        out[k] = x[...]


def stack(pieces, after=()):
    shape = (len(pieces),) + pieces[0].shape
    body = functools.partial(stack_body, len(pieces))
    return call(body, [(shape, jnp.bfloat16)], [*pieces, *after], "stack")[0]


def grad_pre_body(block, own_ref, other_ref, pre_ref, w_ref, rider_ref, out_ref, duo_ref, rows, slope):
    group, hidden = slope.shape
    half = own_ref.shape[0]
    rows[:half, :] = own_ref[...]
    rows[half:, :] = other_ref[...]
    each = group // lax.axis_size("mp")
    chips = half // each
    row = lax.broadcasted_iota(jnp.int32, (group, 1), 0)
    from_row = row
    for b in range(group // each):
        inside = (row >= b * each) & (row < (b + 1) * each)
        from_row = jnp.where(inside, row + (place_of(b, chips) - b) * each, from_row)
    pick = from_row == lax.broadcasted_iota(jnp.int32, (group, group), 1)
    pre = jnp.dot(
        pick.astype(jnp.float32).astype(jnp.bfloat16), pre_ref[...], preferred_element_type=jnp.float32
    )
    slope[...] = gelu_slope(pre)
    duo_ref[1] = rider_ref[...]
    for low in range(0, hidden, block):
        here = slice(low, min(low + block, hidden))
        term = lax.dot_general(
            w_ref[here, :], rows[...], (((1,), (1,)), ((), ())), preferred_element_type=jnp.float32
        )
        grad_pre = (term.T * slope[:, here]).astype(jnp.bfloat16)
        out_ref[:, here] = grad_pre
        duo_ref[0, :, here] = grad_pre


def grad_pre_of(own, other, pre_act, w_out, rider):
    group, hidden = pre_act.shape
    width = w_out.shape[1]
    return call(
        functools.partial(grad_pre_body, 384),
        [((group, hidden), jnp.bfloat16), ((2, group, hidden), jnp.bfloat16)],
        [own, other, pre_act, w_out, rider],
        "grad_pre",
        [pltpu.VMEM((group, width), jnp.bfloat16), pltpu.VMEM((group, hidden), jnp.float32)],
        flops=2 * group * width * hidden,
        bytes_accessed=2 * hidden * width,
    )


def grad_in_body(block, grad_pre_ref, w_ref, *refs):
    out_ref = refs[-1]
    places, rows, width = out_ref.shape
    for low in range(0, width, block):
        here = slice(low, low + block)
        term = jnp.dot(grad_pre_ref[...], w_ref[:, here], preferred_element_type=jnp.float32)
        for b in range(places):
            out_ref[place_of(b, places // 2), :, here] = term[b * rows : (b + 1) * rows].astype(
                jnp.bfloat16
            )


def grad_in_part(grad_pre, w_in_t, places, after):
    group, hidden = grad_pre.shape
    width = w_in_t.shape[1]
    return call(
        functools.partial(grad_in_body, block_of(width, 1024, 128)),
        [((places, group // places, width), jnp.bfloat16)],
        [grad_pre, w_in_t, *after],
        "grad_in_part",
        flops=2 * group * width * hidden,
        bytes_accessed=2 * hidden * width,
    )[0]


def finish_body(terms_ref, after, out):
    total = terms_ref[0].astype(jnp.float32)
    for k in range(1, terms_ref.shape[0]):
        total = total + terms_ref[k].astype(jnp.float32)
    out[...] = total.astype(jnp.bfloat16)


def finish(terms, after):
    return call(finish_body, [(terms.shape[1:], jnp.bfloat16)], [terms, after], "finish")[0]


def turn(x_ref, to_ref, unit):
    hidden = x_ref.shape[1]
    for low in range(0, hidden, unit):
        size = min(unit, hidden - low)
        eye = lax.broadcasted_iota(jnp.int32, (size, size), 0) == lax.broadcasted_iota(
            jnp.int32, (size, size), 1
        )
        to_ref[low : low + size, :] = lax.dot_general(
            eye.astype(jnp.float32).astype(jnp.bfloat16),
            x_ref[:, low : low + size],
            (((1,), (1,)), ((), ())),
            preferred_element_type=jnp.float32,
        ).astype(jnp.bfloat16)


def grad_w_body(arrays, pre_at, grad_pre_at, scale_back, block, *refs):
    own_ref, other_ref, in_ref, out_ref, end_ref = refs[arrays : arrays + 5]
    flat, sorted_rows, turned, held_in, held_out, sems = refs[arrays + 5 :]
    places = len(pre_at)

    def rows_of(at):
        ref = refs[at[0]]
        return ref[...] if len(ref.shape) == 2 else ref[at[1]]

    end_ref[...] = jnp.zeros_like(end_ref)
    group, part = flat.shape[0] // places, own_ref.shape[3]
    half, total = group // 2, places * group
    chips = lax.axis_size("mp") // 2
    rows = half // chips
    copies = []

    def arrange(place):
        size = block_of(total, 128, rows)
        blocks = [(core, k, chip) for core in range(2) for k in range(places) for chip in range(chips)]
        for low in range(0, total, size):
            row = low + lax.broadcasted_iota(jnp.int32, (size, 1), 0)
            from_row = row
            for core, k, chip in blocks[low // rows : (low + size) // rows]:
                first = core * places * half + k * half + chip * rows
                inside = (row >= first) & (row < first + rows)
                shift = k * group + place(core * chips + chip) * rows - first
                from_row = jnp.where(inside, row + shift, from_row)
            pick = from_row == lax.broadcasted_iota(jnp.int32, (size, total), 1)
            sorted_rows[low : low + size, :] = jnp.dot(
                pick.astype(jnp.float32).astype(jnp.bfloat16),
                flat[...],
                preferred_element_type=jnp.float32,
            ).astype(jnp.bfloat16)
        turn(sorted_rows, turned, 256)

    def product(right, held, to_ref):
        for low in range(0, part, block):
            here = slice(low, low + block)
            cols = jnp.concatenate(
                [ref[k, right, :, here] for ref in (own_ref, other_ref) for k in range(places)], axis=0
            )
            term = jnp.dot(turned[...], cols, preferred_element_type=jnp.float32)
            held[:, here] = (term * scale_back).astype(jnp.bfloat16)
            copies.append(
                pltpu.make_async_copy(held.at[:, here], to_ref.at[:, here], sems.at[len(copies)])
            )
            copies[-1].start()

    for k in range(places):
        pre = rows_of(pre_at[k]).astype(jnp.float32)
        flat[k * group : (k + 1) * group, :] = gelu_value(pre).astype(jnp.bfloat16)
    arrange(lambda b: place_of(b, chips))
    product(1, held_out, out_ref)
    for k in range(places):
        flat[k * group : (k + 1) * group, :] = rows_of(grad_pre_at[k])
    arrange(lambda b: b)
    product(0, held_in, in_ref)
    for copy in copies:
        copy.wait()


def grad_w_of(arrays, pre_at, grad_pre_at, own, other, scale_back):
    places = len(pre_at)
    group, hidden = arrays[0].shape
    total, part = places * group, own.shape[3]
    block = block_of(part, 256, 128)
    return call(
        functools.partial(grad_w_body, len(arrays), pre_at, grad_pre_at, scale_back, block),
        [((hidden, part), jnp.bfloat16)] * 2 + [((8, 128), jnp.float32)],
        [*arrays, own, other],
        "grad_w",
        [
            pltpu.VMEM((total, hidden), jnp.bfloat16),
            pltpu.VMEM((total, hidden), jnp.bfloat16),
            pltpu.VMEM((hidden, total), jnp.bfloat16),
            pltpu.VMEM((hidden, part), jnp.bfloat16),
            pltpu.VMEM((hidden, part), jnp.bfloat16),
            pltpu.SemaphoreType.DMA((2 * (part // block),)),
        ],
        limit=20,
        flops=80 * total * part * hidden,
        bytes_accessed=40 * hidden * part,
        out_spaces=[pltpu.HBM, pltpu.HBM, pltpu.VMEM],
    )


def shards(tokens_in, grad_out, pre_act, w_in, w_out):
    n_mp, n_tok = lax.axis_size("mp"), lax.axis_size("tokens")
    chips = n_mp // 2
    scale_back = 1.0 / math.sqrt(pre_act.shape[0] * n_tok)

    relay = n_tok == 4
    early = [k for k in range(1, n_tok) if not (relay and k == 2)]
    pre = {k: fetch(pre_act, "tokens", k) for k in reversed(early)}
    both, pre_act = pack(tokens_in, grad_out, pre_act, lead())
    *pieces, own_rows = join(
        [both] + [fetch_chip(both, k) for k in range(1, chips)],
        n_tok,
        [pre[k] for k in early] if relay else [],
    )
    pieces = [x if k == 0 else fetch(x, "tokens", k) for k, x in enumerate(pieces)]

    rider = pre[3] if relay else pre_act
    grad_pre, duo = grad_pre_of(own_rows, other_core(own_rows), pre_act, w_out, rider)
    grad_pre_all = [grad_pre] + [
        fetch(duo if relay and k == 1 else grad_pre, "tokens", k) for k in range(1, n_tok)
    ]
    own_cols = stack(pieces, [grad_pre])
    other_cols = other_core(own_cols)
    terms = lax.all_to_all(grad_in_part(grad_pre, w_in.T, n_mp, []), "mp", 0, 0)
    arrays = [pre_act] + [pre[k] for k in early] + grad_pre_all
    pre_at = {k: (i, 0) for i, k in enumerate([0] + early)}
    grad_pre_at = [(len(pre_at) + k, 0) for k in range(n_tok)]
    if relay:
        pre_at[2] = (grad_pre_at[1][0], 1)
    grad_w_in_t, grad_w_out, end = grad_w_of(
        arrays, pre_at, grad_pre_at, own_cols, other_cols, scale_back
    )
    return (finish(terms, end), grad_w_in_t.T, grad_w_out)


def solution(mesh):
    placed = (
        P(("tokens", "mp"), None),
        P(("tokens", "mp"), None),
        P("tokens", "mp"),
        P(None, "mp"),
        P("mp", None),
    )
    return jax.shard_map(
        shards,
        mesh=mesh,
        in_specs=placed,
        out_specs=(P(("tokens", "mp"), None), P("tokens", "mp"), P("mp", "tokens")),
        check_vma=False,
    )
```
